32 devices in a mesh: groups: 2 (over x), seq: 8 (over z, y), exp: 2 (over core).
Axes of the slice: x: 2, y: 2, z: 4, core: 2. Of those that a mesh axis runs over, the one named last changes fastest.
Arguments:
- queries: bfloat16 [2048, 6144], P(('groups', 'seq'), 'exp'), parts along dimension 0, may hold values from -6 to 6
- key_rows: bfloat16 [2048, 6144], P(('groups', 'seq'), 'exp'), parts along dimension 0, may hold values from -18 to 18
- values: bfloat16 [2048, 6144], P(('groups', 'seq'), 'exp'), parts along dimension 0, may hold values from -18 to 18
- log_decay: float32 [2048, 48], P(('groups', 'seq'), 'exp'), parts along dimension 0, may hold values from -2.2 to 0, as said below
- residual: bfloat16 [2048, 6144], P(('groups', 'seq'), 'exp'), parts along dimension 0, may hold values from -6 to 6
- attn_gain: float32 [6144], P('exp'), may hold values from 0.25 to 1.75
- moe_gain: float32 [6144], replicated, may hold values from 0.25 to 1.75
- router: bfloat16 [6144, 32], replicated, may hold values from -0.3125 to 0.3125
- routes: int32 [2048, 2], P(('groups', 'seq')), parts along dimension 0, may hold values from 0 to 31, as said below
- slot_pos: int32 [2048, 2], P(('groups', 'seq')), parts along dimension 0, may hold values from 0 to 16, as said below
- gate_weight: bfloat16 [2, 6144, 6144], P('exp', None, 'seq'), may hold values from -0.078125 to 0.078125
- up_weight: bfloat16 [2, 6144, 6144], P('exp', None, 'seq'), may hold values from -0.078125 to 0.078125
- down_weight: bfloat16 [2, 6144, 6144], P('exp', 'seq'), may hold values from -0.15625 to 0.15625
Outputs:
- mixed: bfloat16 [2048, 6144], P(('groups', 'seq'), 'exp'), parts along dimension 0
The draws below stay inside these ranges and needn't reach their ends.
There are 2 independent parts, one for each index of `groups`. The reference program is written for one: setup_inputs(seed, part) draws one part's arguments, and reference() takes and returns one part's arrays. A program takes and returns all parts, laid end to end along the dimension named above; an argument that names none is the same for every part. Nothing has to cross between parts.
Inputs may be any that keep to these rules, and one draw needn't show every extreme that they name: log_decay is at most 0 everywhere. `routes`: the two entries of a row differ. Experts 0 to 1 are the present ones. In each block of 128 rows each present expert is named by at most 16 rows, and by exactly 16 rows in some block. Where routes[t, j] < 2, slot_pos[t, j] counts the earlier rows of t's block that name the same expert; elsewhere it is 16.
All inputs are finite; a program needn't handle non-finite values.
Results may differ from the reference program's by a relative error of at most 0.0052.
Values may be sent and summed in bfloat16 or wider, within the bound.
No kernel may reach another device: no remote copies, remote signals or barrier semaphores. Data moves between devices by JAX's collectives and lax.ppermute only.
A program may use at most 192 MiB of HBM per device.

```python
import math
import jax
import jax.numpy as jnp
from jax import lax

TOK_DEV = 128
ATTENTION_HEADS = 48
HEAD = 128
FF = 6144
EXPERTS = 32
D = 6144
EXP_LIVE = 2
CAP = 16
TOKENS = 1024
N_SEQ = 8


def route_tables(key):
    count_key, peak_key, rank_key, other_key, spare_key, flip_key = jax.random.split(key, 6)
    counts = jax.random.randint(count_key, (N_SEQ, 2), CAP // 4, CAP + 1)
    peaks = jax.random.randint(peak_key, (2,), 0, N_SEQ)
    counts = jnp.where(jnp.arange(N_SEQ)[:, None] == peaks[None, :], CAP, counts)
    ordering_random_seeds = jax.random.split(rank_key, N_SEQ * 2)
    ranks = jax.vmap(lambda sub: jax.random.permutation(sub, TOK_DEV))(ordering_random_seeds).reshape(N_SEQ, 2, TOK_DEV)
    chosen = jnp.transpose(ranks < counts[:, :, None], (0, 2, 1))
    order = jnp.cumsum(chosen.astype(jnp.int32), axis=1) - 1
    spare = EXPERTS - 2
    first_other = jax.random.randint(other_key, (N_SEQ, TOK_DEV), 0, spare)
    offset = jax.random.randint(spare_key, (N_SEQ, TOK_DEV), 1, spare)
    second_other = (first_other + offset) % spare + 2
    first_other = first_other + 2
    pick_zero = chosen[:, :, 0]
    pick_one = chosen[:, :, 1]
    column_a = jnp.where(pick_zero, 0, jnp.where(pick_one, 1, first_other))
    column_b = jnp.where(pick_zero & pick_one, 1, jnp.where(pick_zero | pick_one, first_other, second_other))
    slot_a = jnp.where(pick_zero, order[:, :, 0], jnp.where(pick_one, order[:, :, 1], CAP))
    slot_b = jnp.where(pick_zero & pick_one, order[:, :, 1], CAP)
    flipped = jax.random.randint(flip_key, (N_SEQ, TOK_DEV), 0, 2) == 1
    routes = jnp.stack([jnp.where(flipped, column_b, column_a), jnp.where(flipped, column_a, column_b)], axis=2)
    slots = jnp.stack([jnp.where(flipped, slot_b, slot_a), jnp.where(flipped, slot_a, slot_b)], axis=2)
    return (routes.reshape(TOKENS, 2).astype(jnp.int32), slots.reshape(TOKENS, 2).astype(jnp.int32))


def draw_routes(key, part):
    tables = route_tables(key)
    return tables[0]


def draw_slot_pos(key, part):
    tables = route_tables(key)
    return tables[1]


def block_loudness(key):
    loud_key = jax.random.fold_in(key, 91)
    return jnp.exp(jax.random.uniform(loud_key, (N_SEQ, ATTENTION_HEADS), minval=-1.5, maxval=1.5))


def loud_rows(key, loudness):
    entries = jnp.clip(jax.random.normal(key, (N_SEQ, TOK_DEV, ATTENTION_HEADS, HEAD)), -4.0, 4.0)
    return (entries * loudness[:, None, :, None]).reshape(TOKENS, D).astype(jnp.float32)


def draw_key_rows(key, part):
    loudness = block_loudness(key)
    key = jax.random.fold_in(key, 23)
    return loud_rows(key, loudness).astype(jnp.bfloat16)


def draw_values(key, part):
    loudness = block_loudness(key)
    key = jax.random.fold_in(key, 29)
    return loud_rows(key, loudness).astype(jnp.bfloat16)


def draw_log_decay(key, part):
    key = jax.random.fold_in(key, 17)
    fast_key, rate_key, slow_key, rough_key, place_key, height_seed_key, block_key = jax.random.split(key, 7)
    fast_share = 0.5
    fast_head = jax.random.uniform(fast_key, (ATTENTION_HEADS,)) < fast_share
    fast_block = jax.random.uniform(block_key, (N_SEQ, ATTENTION_HEADS)) < 0.5
    fast_here = fast_head[None, :] & fast_block
    fast_rate = jnp.exp(jax.random.uniform(rate_key, (N_SEQ, ATTENTION_HEADS), minval=math.log(1.0 / 50.0), maxval=math.log(1.0 / 30.0)))
    slow_rate = jnp.exp(jax.random.uniform(slow_key, (ATTENTION_HEADS,), minval=math.log(0.05), maxval=math.log(0.2))) / TOKENS
    block_rate = jnp.where(fast_here, fast_rate, slow_rate[None, :])
    token_frequency = jnp.broadcast_to(block_rate[:, None, :], (N_SEQ, TOK_DEV, ATTENTION_HEADS)).reshape(TOKENS, ATTENTION_HEADS)
    jaggedness = jnp.exp(jax.random.uniform(rough_key, (TOKENS, ATTENTION_HEADS), minval=math.log(0.5), maxval=math.log(2.0)))
    places = jax.random.randint(place_key, (3, ATTENTION_HEADS), 0, TOKENS)
    spike_height = jax.random.uniform(height_seed_key, (3, ATTENTION_HEADS), minval=math.log(0.5), maxval=math.log(0.8))
    position_marker_mask = jnp.arange(TOKENS)[:, None, None] == places[None]
    spike_count = jnp.sum(jnp.where(position_marker_mask, spike_height[None], 0.0), axis=1)
    return (-token_frequency * jaggedness + spike_count).astype(jnp.float32)


def block_levels(key, shape, cuts, low, high):
    gain = 1.0
    for axis_at, shards_of in cuts:
        draws = jax.random.uniform(jax.random.fold_in(jax.random.fold_in(key, 6), axis_at), (shards_of,), jnp.float32, low / len(cuts), high / len(cuts))
        gain = gain * jnp.repeat(jnp.exp(draws), shape[axis_at] // shards_of).reshape((-1,) + (1,) * (len(shape) - 1 - axis_at))
    return gain


def normal_values(own_key, dims, deviation, limit, shards=(), dtype=jnp.bfloat16):
    result = deviation * jax.random.normal(own_key, dims, jnp.float32)
    if shards:
        result = result * block_levels(own_key, dims, shards, -0.22, 0.18)
    return jnp.clip(result, -limit, limit).astype(dtype)


def setup_inputs(seed: int = 0, part: int = 0) -> dict:
    arg_keys = jax.random.split(jax.random.key(seed), 14)
    part_keys = jax.random.split(jax.random.fold_in(arg_keys[13], part), 14)
    queries = normal_values(part_keys[0], (TOKENS, D), 1.0, 6.0, ((0, 8), (1, 2)))
    key_rows = draw_key_rows(jax.random.fold_in(jax.random.fold_in(arg_keys[13], part), 71), part)
    values = draw_values(jax.random.fold_in(jax.random.fold_in(arg_keys[13], part), 71), part)
    log_decay = draw_log_decay(jax.random.fold_in(jax.random.fold_in(arg_keys[13], part), 71), part)
    residual = normal_values(part_keys[4], (TOKENS, D), 1.0, 6.0, ((0, 8), (1, 2)))
    attn_gain = jnp.clip(1.0 + 0.15 * jax.random.normal(arg_keys[5], (D,), jnp.float32), 0.25, 1.75)
    moe_gain = jnp.clip(1.0 + 0.15 * jax.random.normal(arg_keys[6], (D,), jnp.float32), 0.25, 1.75)
    router = normal_values(arg_keys[7], (D, EXPERTS), (D // 16) ** -0.5, 0.3125)
    routes = draw_routes(jax.random.fold_in(jax.random.fold_in(arg_keys[13], part), 71), part)
    slot_pos = draw_slot_pos(jax.random.fold_in(jax.random.fold_in(arg_keys[13], part), 71), part)
    gate_weight = normal_values(arg_keys[10], (EXP_LIVE, D, FF), D ** -0.5, 0.078125, ((0, 2), (2, 8)))
    up_weight = normal_values(arg_keys[11], (EXP_LIVE, D, FF), D ** -0.5, 0.078125, ((0, 2), (2, 8)))
    down_weight = normal_values(arg_keys[12], (EXP_LIVE, FF, D), (FF // 4) ** -0.5, 0.15625, ((0, 2), (1, 8)))
    return dict(queries=queries, key_rows=key_rows, values=values, log_decay=log_decay, residual=residual, attn_gain=attn_gain, moe_gain=moe_gain, router=router, routes=routes, slot_pos=slot_pos, gate_weight=gate_weight, up_weight=up_weight, down_weight=down_weight)


def narrow_copy(array):
    return lax.optimization_barrier(array.astype(jnp.bfloat16)).astype(jnp.float32)

def attention_block(carried, block):
    query_heads, key_heads, value_heads, log_block = block
    length = query_heads.shape[0]
    running = jnp.cumsum(log_block, axis=0)
    block_total = running[-1]
    query_float = query_heads.astype(jnp.float32)
    key_float = key_heads.astype(jnp.float32)
    value_float = value_heads.astype(jnp.float32)
    router_scores = jnp.einsum('thd,shd->hts', query_float, key_float, precision=lax.Precision.HIGHEST)
    spread = running.T[:, :, None] - running.T[:, None, :]
    causal = (jnp.arange(length)[:, None] >= jnp.arange(length)[None, :])[None]
    mixing = narrow_copy(jnp.where(causal, router_scores * jnp.exp(jnp.where(causal, spread, 0.0)), 0.0))
    within_part = jnp.einsum('hts,shd->thd', mixing, value_float, precision=lax.Precision.HIGHEST)
    carried_part = jnp.einsum('thd,hde->the', query_float, narrow_copy(carried), precision=lax.Precision.HIGHEST)
    carried_part = carried_part * jnp.exp(running)[:, :, None]
    scaled = narrow_copy(key_float * jnp.exp(block_total[None, :] - running)[:, :, None])
    local_state = jnp.einsum('shd,she->hde', scaled, value_float, precision=lax.Precision.HIGHEST)
    following_memory_matrix = jnp.exp(block_total)[:, None, None] * carried + local_state
    return (following_memory_matrix, within_part + carried_part)

def reference(queries, key_rows, values, log_decay, residual, attn_gain, moe_gain, router, routes, slot_pos, gate_weight, up_weight, down_weight):
    blocks = (queries.reshape(N_SEQ, TOK_DEV, ATTENTION_HEADS, HEAD), key_rows.reshape(N_SEQ, TOK_DEV, ATTENTION_HEADS, HEAD), values.reshape(N_SEQ, TOK_DEV, ATTENTION_HEADS, HEAD), log_decay.reshape(N_SEQ, TOK_DEV, ATTENTION_HEADS))
    start_state = jnp.zeros((ATTENTION_HEADS, HEAD, HEAD), jnp.float32)
    closing_state, raw = lax.scan(attention_block, start_state, blocks)
    raw = raw.reshape(TOKENS, ATTENTION_HEADS, HEAD)
    normed = raw * lax.rsqrt(lax.optimization_barrier(jnp.mean(raw * raw, axis=2, keepdims=True)) + 1e-05)
    hidden = (residual.astype(jnp.float32) + normed.reshape(TOKENS, D) * attn_gain).astype(jnp.bfloat16)
    hidden_float = hidden.astype(jnp.float32)
    inverse = lax.rsqrt(lax.optimization_barrier(jnp.mean(hidden_float * hidden_float, axis=1)) + 1e-06)
    moe_in = (hidden_float * inverse[:, None] * moe_gain).astype(jnp.bfloat16)
    logits = jnp.dot(hidden_float * moe_gain, router.astype(jnp.float32), precision=lax.Precision.HIGHEST) * inverse[:, None]
    picked = lax.optimization_barrier(jnp.sum(jnp.where(routes[:, :, None] == jnp.arange(EXPERTS)[None, None, :], logits[:, None, :], 0.0), axis=2))
    gates = jax.nn.sigmoid(picked)
    shares = gates / lax.optimization_barrier(jnp.sum(gates, axis=1, keepdims=True))
    route_blocks = routes.reshape(N_SEQ, TOK_DEV, 2)
    slot_blocks = slot_pos.reshape(N_SEQ, TOK_DEV, 2)
    share_blocks = shares.reshape(N_SEQ, TOK_DEV, 2)
    moe_blocks = moe_in.reshape(N_SEQ, TOK_DEV, D).astype(jnp.float32)
    expert_sum = jnp.zeros((N_SEQ, TOK_DEV, D), jnp.float32)
    for expert in range(EXP_LIVE):
        matches = (route_blocks == expert)[:, None] & (slot_blocks[:, None] == jnp.arange(CAP)[None, :, None, None])
        table = lax.optimization_barrier(jnp.sum(jnp.where(matches, 1.0, 0.0), axis=3))
        buffer = jnp.einsum('bct,btd->bcd', table, moe_blocks, precision=lax.Precision.HIGHEST)
        buffer = buffer.astype(jnp.bfloat16).reshape(N_SEQ * CAP, D)
        gate_part = jnp.dot(buffer, gate_weight[expert], preferred_element_type=jnp.float32)
        up_part = jnp.dot(buffer, up_weight[expert], preferred_element_type=jnp.float32)
        specialist_inner_activation = (jax.nn.silu(gate_part) * up_part).astype(jnp.bfloat16)
        expert_out = narrow_copy(jnp.dot(specialist_inner_activation, down_weight[expert], preferred_element_type=jnp.float32))
        expert_out = expert_out.reshape(N_SEQ, CAP, D)
        mixing = lax.optimization_barrier(jnp.sum(jnp.where(matches, share_blocks[:, None], 0.0), axis=3))
        expert_sum = expert_sum + jnp.einsum('bct,bcd->btd', mixing, expert_out, precision=lax.Precision.HIGHEST)
    return (hidden_float + expert_sum.reshape(TOKENS, D)).astype(jnp.bfloat16)
```

```python
import jax
import jax.numpy as jnp
from jax import lax
from jax.sharding import PartitionSpec as P

CAP = 16
CHUNKS = 2


def slot_matches(routes, slot_pos, expert, capacity):
    return (routes == expert)[:, :, None] & (
        slot_pos[:, :, None] == jnp.arange(capacity)[None, None, :]
    )


def entering_state(local_state, block_total):
    count, mine = (lax.axis_size("seq"), lax.axis_index("seq"))
    odd = mine % 2 == 1
    swap = [(i, i ^ 1) for i in range(count)]
    heads = local_state.shape[0]
    half = heads // 2
    part = half // CHUNKS
    total_other = lax.ppermute(block_total[None], "seq", swap)[0]

    def pick(array, first):
        return lax.dynamic_slice_in_dim(array, jnp.where(odd, half, 0) + first, part, axis=0)

    def pick_other(array, first):
        return lax.dynamic_slice_in_dim(array, jnp.where(odd, 0, half) + first, part, axis=0)

    kept, swapped = ([], [])
    for chunk in range(CHUNKS):
        own = pick(local_state, chunk * part)
        arrived = lax.ppermute(
            pick_other(local_state, chunk * part).astype(jnp.bfloat16), "seq", swap
        ).astype(jnp.float32)
        own_decay = jnp.exp(pick(block_total, chunk * part))[:, None, None]
        other_decay = jnp.exp(pick(total_other, chunk * part))[:, None, None]
        even_state = jnp.where(odd, arrived, own)
        odd_state = jnp.where(odd, own, arrived)
        even_decay = jnp.where(odd, other_decay, own_decay)
        odd_decay = jnp.where(odd, own_decay, other_decay)
        pair_state = odd_decay * even_state + odd_state
        pair_decay = even_decay * odd_decay
        before = jnp.zeros_like(own)
        for hop in range(count // 2 - 1):
            pairs = [(2 * hop + k, 2 * hop + 2 + k) for k in range(2)]
            sent = (pair_decay * before + pair_state).astype(jnp.bfloat16)
            before = before + lax.ppermute(sent, "seq", pairs).astype(jnp.float32)
        between = even_decay * before + even_state
        kept.append(jnp.where(odd, between, before).astype(jnp.bfloat16))
        swapped.append(
            lax.ppermute(jnp.where(odd, before, between).astype(jnp.bfloat16), "seq", swap)
        )
    kept, swapped = (jnp.concatenate(kept), jnp.concatenate(swapped))
    return jnp.where(odd, jnp.concatenate([swapped, kept]), jnp.concatenate([kept, swapped]))


def ring_pairs(count):
    order = list(range(0, count, 2)) + list(range(count - 1, 0, -2))
    right = [(order[i], order[(i + 1) % count]) for i in range(count)]
    return (right, [(b, a) for a, b in right])


def ring_gather(unit):
    count = lax.axis_size("seq")
    right, left = ring_pairs(count)
    middle = unit.shape[1] // 2
    from_left, from_right = ([], [])
    moving_right, moving_left = (unit, unit)
    for _ in range(count // 2 - 1):
        moving_right = lax.ppermute(moving_right, "seq", right)
        moving_left = lax.ppermute(moving_left, "seq", left)
        from_left.append(moving_right)
        from_right.append(moving_left)
    far = jnp.concatenate(
        [
            lax.ppermute(moving_right[:, :middle], "seq", right),
            lax.ppermute(moving_left[:, middle:], "seq", left),
        ],
        axis=1,
    )
    return jnp.concatenate([unit] + from_left + [far] + from_right, axis=0)


def ring_scatter(partial, rows):
    count = lax.axis_size("seq")
    right, left = ring_pairs(count)
    middle = partial.shape[1] // 2
    steps = count // 2

    def piece(position):
        return partial[position * rows : (position + 1) * rows]

    far = piece(steps).astype(jnp.bfloat16)
    moving_left = lax.ppermute(far[:, :middle], "seq", left).astype(jnp.float32)
    moving_right = lax.ppermute(far[:, middle:], "seq", right).astype(jnp.float32)
    for step in range(steps - 1, 0, -1):
        to_left, to_right = (piece(step), piece(steps + step))
        if step == steps - 1:
            to_left = jnp.concatenate(
                [to_left[:, :middle] + moving_left, to_left[:, middle:]], axis=1
            )
            to_right = jnp.concatenate(
                [to_right[:, :middle], to_right[:, middle:] + moving_right], axis=1
            )
        else:
            to_left, to_right = (to_left + moving_left, to_right + moving_right)
        moving_left = lax.ppermute(to_left.astype(jnp.bfloat16), "seq", left).astype(jnp.float32)
        moving_right = lax.ppermute(to_right.astype(jnp.bfloat16), "seq", right).astype(
            jnp.float32
        )
    return piece(0) + moving_left + moving_right


def shards(
    queries,
    key_rows,
    values,
    log_decay,
    residual,
    attn_gain,
    moe_gain,
    router,
    routes,
    slot_pos,
    gate_weight,
    up_weight,
    down_weight,
):
    length, width = queries.shape
    heads_here = log_decay.shape[1]
    head_width = width // heads_here
    core = lax.axis_index("exp")
    exchange = [(0, 1), (1, 0)]
    query_heads = queries.reshape(length, heads_here, head_width)
    key_heads = key_rows.reshape(length, heads_here, head_width)
    value_heads = values.reshape(length, heads_here, head_width)
    running = jnp.cumsum(log_decay, axis=0)
    block_total = running[-1]
    scaled = (
        key_heads.astype(jnp.float32) * jnp.exp(block_total[None, :] - running)[:, :, None]
    ).astype(jnp.bfloat16)
    local_state = jnp.einsum(
        "shd,she->hde", scaled, value_heads, preferred_element_type=jnp.float32
    )
    entering = entering_state(local_state, block_total)
    scores = jnp.einsum("thd,shd->hts", query_heads, key_heads, preferred_element_type=jnp.float32)
    spread = running.T[:, :, None] - running.T[:, None, :]
    causal = (jnp.arange(length)[:, None] >= jnp.arange(length)[None, :])[None]
    mixing = jnp.where(causal, scores * jnp.exp(jnp.where(causal, spread, 0.0)), 0.0).astype(
        jnp.bfloat16
    )
    within_part = jnp.einsum(
        "hts,shd->thd", mixing, value_heads, preferred_element_type=jnp.float32
    )
    carried_part = jnp.einsum(
        "thd,hde->the", query_heads, entering, preferred_element_type=jnp.float32
    )
    raw = within_part + carried_part * jnp.exp(running)[:, :, None]
    normed = raw * lax.rsqrt(jnp.mean(raw * raw, axis=2, keepdims=True) + 1e-05)
    hidden_half = (residual.astype(jnp.float32) + normed.reshape(length, -1) * attn_gain).astype(
        jnp.bfloat16
    )

    matches = [slot_matches(routes, slot_pos, expert, CAP) for expert in range(2)]
    tables = [jnp.any(match, axis=1).astype(jnp.bfloat16).T for match in matches]
    table = jnp.concatenate(tables, axis=0)
    rows = jnp.dot(table, hidden_half, preferred_element_type=jnp.float32).astype(jnp.bfloat16)
    rows_own = jnp.where(core == 0, rows[:CAP], rows[CAP:])
    rows_other = lax.ppermute(jnp.where(core == 0, rows[CAP:], rows[:CAP]), "exp", exchange)
    rows_whole = jnp.where(
        core == 0,
        jnp.concatenate([rows_own, rows_other], axis=1),
        jnp.concatenate([rows_other, rows_own], axis=1),
    ).astype(jnp.float32)
    rows_inverse = lax.rsqrt(jnp.mean(rows_whole * rows_whole, axis=1, keepdims=True) + 1e-06)
    buffer = (rows_whole * rows_inverse * moe_gain).astype(jnp.bfloat16)

    segment = ring_gather(buffer)
    gate_part = jnp.dot(segment, gate_weight[0], preferred_element_type=jnp.float32)
    up_part = jnp.dot(segment, up_weight[0], preferred_element_type=jnp.float32)
    hidden_rows = (jax.nn.silu(gate_part) * up_part).astype(jnp.bfloat16)
    partial = jnp.dot(hidden_rows, down_weight[0], preferred_element_type=jnp.float32)
    expert_out = ring_scatter(partial, CAP).astype(jnp.bfloat16)

    hidden_float = hidden_half.astype(jnp.float32)
    gain_half = lax.dynamic_slice_in_dim(moe_gain, core * width, width)
    router_half = lax.dynamic_slice_in_dim(router, core * width, width, axis=0)
    logits_half = jnp.dot(
        hidden_float * gain_half, router_half.astype(jnp.float32), precision=lax.Precision.HIGHEST
    )
    picked_half = jnp.sum(
        jnp.where(
            routes[:, :, None] == jnp.arange(router.shape[1])[None, None, :],
            logits_half[:, None, :],
            0.0,
        ),
        axis=2,
    )
    square_half = jnp.sum(hidden_float * hidden_float, axis=1, keepdims=True)
    sums_half = jnp.concatenate([picked_half, square_half], axis=1)
    sums = sums_half + lax.ppermute(sums_half, "exp", exchange)
    inverse = lax.rsqrt(sums[:, 2:] / (2 * width) + 1e-06)
    gates = jax.nn.sigmoid(sums[:, :2] * inverse)
    shares = gates / jnp.sum(gates, axis=1, keepdims=True)
    weighting = jnp.concatenate(
        [jnp.sum(jnp.where(match, shares[:, :, None], 0.0), axis=1) for match in matches], axis=1
    )

    out_low, out_high = (expert_out[:, :width], expert_out[:, width:])
    out_own = jnp.where(core == 0, out_low, out_high)
    out_other = lax.ppermute(jnp.where(core == 0, out_high, out_low), "exp", exchange)
    outs = jnp.where(
        core == 0,
        jnp.concatenate([out_own, out_other], axis=0),
        jnp.concatenate([out_other, out_own], axis=0),
    ).astype(jnp.float32)
    expert_sum = jnp.dot(weighting, outs, precision=lax.Precision.HIGHEST)
    return (hidden_float + expert_sum).astype(jnp.bfloat16)


def solution(mesh):
    placed = (
        P(("groups", "seq"), "exp"),
        P(("groups", "seq"), "exp"),
        P(("groups", "seq"), "exp"),
        P(("groups", "seq"), "exp"),
        P(("groups", "seq"), "exp"),
        P("exp"),
        P(),
        P(),
        P(("groups", "seq"), None),
        P(("groups", "seq"), None),
        P("exp", None, "seq"),
        P("exp", None, "seq"),
        P("exp", "seq", None),
    )
    return jax.shard_map(
        shards, mesh=mesh, in_specs=placed, out_specs=P(("groups", "seq"), "exp"), check_vma=False
    )
```

```python
import functools

import jax
import jax.numpy as jnp
from jax import lax
from jax.experimental import pallas as pl
from jax.experimental.pallas import tpu as pltpu
from jax.sharding import PartitionSpec as P

CAP = 16
CHUNKS = 2
VMEM = pl.BlockSpec(memory_space=pltpu.VMEM)
SMEM = pl.BlockSpec(memory_space=pltpu.SMEM)
HBM = pl.BlockSpec(memory_space=pl.ANY)
F32, BF16 = (jnp.float32, jnp.bfloat16)


def grant(mebibytes):
    return pltpu.CompilerParams(vmem_limit_bytes=mebibytes * 2**20)


def triangle(length):
    rows = lax.broadcasted_iota(jnp.int32, (length, length), 0)
    columns = lax.broadcasted_iota(jnp.int32, (length, length), 1)
    return rows >= columns


def as_columns(table):
    heads, length = table.shape
    return jnp.concatenate([table, jnp.zeros((length - heads, length), F32)], axis=0).T


def state_kernel(odd_ref, log_ref, key_ref, value_ref, run_ref, full_ref, narrow_ref):
    heads, length = log_ref.shape
    width = key_ref.shape[1] // heads
    half = heads // 2
    running = lax.dot_general(
        log_ref[...],
        jnp.where(triangle(length), 1.0, 0.0),
        (((1,), (1,)), ((), ())),
        precision=lax.Precision.HIGHEST,
        preferred_element_type=F32,
    )
    run_ref[...] = running
    rest = as_columns(jnp.exp(running[:, length - 1 :] - running))
    for head in range(heads):
        lanes = slice(head * width, (head + 1) * width)
        scaled = (key_ref[:, lanes].astype(F32) * rest[:, head : head + 1]).astype(BF16)
        state = lax.dot_general(
            scaled, value_ref[:, lanes], (((0,), (0,)), ((), ())), preferred_element_type=F32
        )
        side = odd_ref[0] if head < half else 1 - odd_ref[0]
        place = side * half + head % half
        full_ref[place] = state
        narrow_ref[place] = state.astype(BF16)


def block_state(odd, log_rows, key_rows, value_rows):
    heads, length = log_rows.shape
    width = key_rows.shape[1] // heads
    return pl.pallas_call(
        state_kernel,
        out_shape=(
            jax.ShapeDtypeStruct((heads, length), F32),
            jax.ShapeDtypeStruct((heads, width, width), F32),
            jax.ShapeDtypeStruct((heads, width, width), BF16),
        ),
        in_specs=[SMEM, VMEM, VMEM, VMEM],
        out_specs=(VMEM, VMEM, VMEM),
        compiler_params=grant(16),
        cost_estimate=pl.CostEstimate(
            flops=2 * length * width * width * heads,
            bytes_accessed=4 * length * width * heads + 6 * heads * width * width,
            transcendentals=0,
        ),
    )(odd, log_rows, key_rows, value_rows)


def within_kernel(run_ref, query_ref, key_ref, value_ref, out_ref):
    heads, length = run_ref.shape
    width = key_ref.shape[1] // heads
    causal = triangle(length)
    running = run_ref[...]
    columns = as_columns(running)
    for head in range(heads):
        lanes = slice(head * width, (head + 1) * width)
        scores = lax.dot_general(
            query_ref[:, lanes],
            key_ref[:, lanes],
            (((1,), (1,)), ((), ())),
            preferred_element_type=F32,
        )
        spread = columns[:, head : head + 1] - running[head : head + 1, :]
        decay = jnp.exp(jnp.where(causal, spread, 0.0))
        mixing = jnp.where(causal, scores * decay, 0.0).astype(BF16)
        out_ref[:, lanes] = jnp.dot(mixing, value_ref[:, lanes], preferred_element_type=F32)


def within_block(running, query_rows, key_rows, value_rows):
    heads, length = running.shape
    width = key_rows.shape[1] // heads
    return pl.pallas_call(
        within_kernel,
        out_shape=jax.ShapeDtypeStruct(query_rows.shape, F32),
        in_specs=[VMEM] * 4,
        out_specs=VMEM,
        compiler_params=grant(16),
        cost_estimate=pl.CostEstimate(
            flops=4 * length * length * width * heads,
            bytes_accessed=10 * length * width * heads,
            transcendentals=heads * length * length,
        ),
    )(running, query_rows, key_rows, value_rows)


def hidden_kernel(odd_ref, run_ref, query_ref, within_ref, residual_ref, gain_ref, table_ref, *refs):
    states, (hidden_ref, own_ref, other_ref) = (refs[:-3], refs[-3:])
    heads, length = run_ref.shape
    width = query_ref.shape[1] // heads
    half, part = (heads // 2, states[0].shape[0])
    grown = as_columns(jnp.exp(run_ref[...]))
    even = odd_ref[0] == 0
    for head in range(heads):
        lanes = slice(head * width, (head + 1) * width)
        chunk, place = divmod(head % half, part)
        kept, swapped = (states[chunk][place], states[CHUNKS + chunk][place])
        state = jnp.where(even, kept, swapped) if head < half else jnp.where(even, swapped, kept)
        carried = jnp.dot(query_ref[:, lanes], state, preferred_element_type=F32)
        raw = within_ref[:, lanes] + carried * grown[:, head : head + 1]
        normed = raw * lax.rsqrt(jnp.mean(raw * raw, axis=1, keepdims=True) + 1e-05)
        hidden_ref[:, lanes] = (
            residual_ref[:, lanes].astype(F32) + normed * gain_ref[:, lanes]
        ).astype(BF16)
    rows = jnp.dot(table_ref[...], hidden_ref[...], preferred_element_type=F32).astype(BF16)
    own_ref[...] = rows[: own_ref.shape[0]]
    other_ref[...] = rows[own_ref.shape[0] :]


def hidden_rows(odd, running, query_rows, within, residual, gain, table, kept, swapped):
    heads, length = running.shape
    capacity = table.shape[0] // 2
    wide = query_rows.shape[1]
    return pl.pallas_call(
        hidden_kernel,
        out_shape=(
            jax.ShapeDtypeStruct((length, wide), BF16),
            jax.ShapeDtypeStruct((capacity, wide), BF16),
            jax.ShapeDtypeStruct((capacity, wide), BF16),
        ),
        in_specs=[SMEM] + [VMEM] * (6 + 2 * CHUNKS),
        out_specs=(VMEM, VMEM, VMEM),
        compiler_params=grant(16),
        cost_estimate=pl.CostEstimate(
            flops=2 * length * wide * (wide // heads),
            bytes_accessed=12 * length * wide,
            transcendentals=0,
        ),
    )(odd, running, query_rows, within, residual, gain, table, *kept, *swapped)


def expert_kernel(
    deep, wide, row_ref, gate_ref, up_ref, down_ref, out_ref, gate, up, down, gate_sem, up_sem, down_sem
):
    width, units = gate_ref.shape
    copies = []
    for step in range(width // deep):
        rows = pl.ds(step * deep, deep)
        pair = (
            pltpu.make_async_copy(gate_ref.at[rows], gate.at[rows], gate_sem.at[step]),
            pltpu.make_async_copy(up_ref.at[rows], up.at[rows], up_sem.at[step]),
        )
        for copy in pair:
            copy.start()
        copies.append(pair)
    downs = []
    for step in range(width // wide):
        lanes = pl.ds(step * wide, wide)
        downs.append(
            pltpu.make_async_copy(down_ref.at[:, lanes], down.at[:, lanes], down_sem.at[step])
        )
        downs[-1].start()
    gate_part = jnp.zeros((row_ref.shape[0], units), F32)
    up_part = jnp.zeros((row_ref.shape[0], units), F32)
    for step, pair in enumerate(copies):
        lanes = slice(step * deep, (step + 1) * deep)
        for copy in pair:
            copy.wait()
        gate_part += jnp.dot(row_ref[:, lanes], gate[lanes], preferred_element_type=F32)
        up_part += jnp.dot(row_ref[:, lanes], up[lanes], preferred_element_type=F32)
    hidden = (jax.nn.silu(gate_part) * up_part).astype(BF16)
    for step, copy in enumerate(downs):
        lanes = slice(step * wide, (step + 1) * wide)
        copy.wait()
        out_ref[:, lanes] = jnp.dot(hidden, down[:, lanes], preferred_element_type=F32)


def expert_rows(segment, gate_weight, up_weight, down_weight):
    width, units = gate_weight.shape
    deep = wide = width // 6
    return pl.pallas_call(
        functools.partial(expert_kernel, deep, wide),
        out_shape=jax.ShapeDtypeStruct((segment.shape[0], width), F32),
        in_specs=[VMEM, HBM, HBM, HBM],
        out_specs=VMEM,
        scratch_shapes=[
            pltpu.VMEM((width, units), BF16),
            pltpu.VMEM((width, units), BF16),
            pltpu.VMEM((units, width), BF16),
            pltpu.SemaphoreType.DMA((width // deep,)),
            pltpu.SemaphoreType.DMA((width // deep,)),
            pltpu.SemaphoreType.DMA((width // wide,)),
        ],
        compiler_params=grant(48),
        cost_estimate=pl.CostEstimate(
            flops=6 * segment.shape[0] * width * units,
            bytes_accessed=6 * width * units,
            transcendentals=0,
        ),
    )(segment, gate_weight, up_weight, down_weight)


def slot_matches(routes, slot_pos, expert, capacity):
    return (routes == expert)[:, :, None] & (
        slot_pos[:, :, None] == jnp.arange(capacity)[None, None, :]
    )


def entering_state(odd, full, narrow, block_total):
    count = lax.axis_size("seq")
    swap = [(i, i ^ 1) for i in range(count)]
    half = full.shape[0] // 2
    part = half // CHUNKS
    low, high = (block_total[:half], block_total[half:])
    total_own = jnp.where(odd, high, low)
    total_other = lax.ppermute(jnp.where(odd, low, high)[None], "seq", swap)[0]
    even_decay = jnp.exp(jnp.where(odd, total_other, total_own))[:, None, None]
    odd_decay = jnp.exp(jnp.where(odd, total_own, total_other))[:, None, None]
    pair_decay = even_decay * odd_decay
    kept, swapped = ([], [])
    for chunk in range(CHUNKS):
        here = slice(chunk * part, (chunk + 1) * part)
        own = full[here]
        arrived = lax.ppermute(
            narrow[half + chunk * part : half + (chunk + 1) * part], "seq", swap
        ).astype(F32)
        even_state = jnp.where(odd, arrived, own)
        odd_state = jnp.where(odd, own, arrived)
        pair_state = odd_decay[here] * even_state + odd_state
        before = jnp.zeros_like(own)
        for hop in range(count // 2 - 1):
            pairs = [(2 * hop + k, 2 * hop + 2 + k) for k in range(2)]
            sent = (pair_decay[here] * before + pair_state).astype(BF16)
            before = before + lax.ppermute(sent, "seq", pairs).astype(F32)
        between = even_decay[here] * before + even_state
        kept.append(jnp.where(odd, between, before).astype(BF16))
        swapped.append(lax.ppermute(jnp.where(odd, before, between).astype(BF16), "seq", swap))
    return (kept, swapped)


def ring_pairs(count):
    order = list(range(0, count, 2)) + list(range(count - 1, 0, -2))
    right = [(order[i], order[(i + 1) % count]) for i in range(count)]
    return (right, [(b, a) for a, b in right])


def ring_gather(unit):
    count = lax.axis_size("seq")
    right, left = ring_pairs(count)
    middle = unit.shape[1] // 2
    from_left, from_right = ([], [])
    moving_right, moving_left = (unit, unit)
    for _ in range(count // 2 - 1):
        moving_right = lax.ppermute(moving_right, "seq", right)
        moving_left = lax.ppermute(moving_left, "seq", left)
        from_left.append(moving_right)
        from_right.append(moving_left)
    far = jnp.concatenate(
        [
            lax.ppermute(moving_right[:, :middle], "seq", right),
            lax.ppermute(moving_left[:, middle:], "seq", left),
        ],
        axis=1,
    )
    return jnp.concatenate([unit] + from_left + [far] + from_right, axis=0)


def ring_scatter(partial, rows):
    count = lax.axis_size("seq")
    right, left = ring_pairs(count)
    middle = partial.shape[1] // 2
    steps = count // 2

    def piece(position):
        return partial[position * rows : (position + 1) * rows]

    far = piece(steps).astype(jnp.bfloat16)
    moving_left = lax.ppermute(far[:, :middle], "seq", left).astype(jnp.float32)
    moving_right = lax.ppermute(far[:, middle:], "seq", right).astype(jnp.float32)
    for step in range(steps - 1, 0, -1):
        to_left, to_right = (piece(step), piece(steps + step))
        if step == steps - 1:
            to_left = jnp.concatenate(
                [to_left[:, :middle] + moving_left, to_left[:, middle:]], axis=1
            )
            to_right = jnp.concatenate(
                [to_right[:, :middle], to_right[:, middle:] + moving_right], axis=1
            )
        else:
            to_left, to_right = (to_left + moving_left, to_right + moving_right)
        moving_left = lax.ppermute(to_left.astype(jnp.bfloat16), "seq", left).astype(jnp.float32)
        moving_right = lax.ppermute(to_right.astype(jnp.bfloat16), "seq", right).astype(
            jnp.float32
        )
    return piece(0) + moving_left + moving_right


def shards(
    queries,
    key_rows,
    values,
    log_decay,
    residual,
    attn_gain,
    moe_gain,
    router,
    routes,
    slot_pos,
    gate_weight,
    up_weight,
    down_weight,
):
    length, width = queries.shape
    core = lax.axis_index("exp")
    exchange = [(0, 1), (1, 0)]
    odd = lax.axis_index("seq") % 2
    odd_scalar = odd.astype(jnp.int32)[None]
    running, full, narrow = block_state(odd_scalar, log_decay.T, key_rows, values)
    kept, swapped = entering_state(odd == 1, full, narrow, running[:, -1])
    within = within_block(running, queries, key_rows, values)

    matches = [slot_matches(routes, slot_pos, expert, CAP) for expert in range(2)]
    tables = [jnp.any(match, axis=1).astype(BF16).T for match in matches]
    table = jnp.where(core == 0, jnp.concatenate(tables), jnp.concatenate(tables[::-1]))
    hidden_half, rows_own, rows_sent = hidden_rows(
        odd_scalar, running, queries, within, residual, attn_gain[None], table, kept, swapped
    )
    rows_other = lax.ppermute(rows_sent, "exp", exchange)
    rows_whole = jnp.where(
        core == 0,
        jnp.concatenate([rows_own, rows_other], axis=1),
        jnp.concatenate([rows_other, rows_own], axis=1),
    ).astype(jnp.float32)
    rows_inverse = lax.rsqrt(jnp.mean(rows_whole * rows_whole, axis=1, keepdims=True) + 1e-06)
    buffer = (rows_whole * rows_inverse * moe_gain).astype(jnp.bfloat16)

    segment = ring_gather(buffer)
    partial = expert_rows(segment, gate_weight[0], up_weight[0], down_weight[0])
    expert_out = ring_scatter(partial, CAP).astype(jnp.bfloat16)

    hidden_float = hidden_half.astype(jnp.float32)
    gain_half = lax.dynamic_slice_in_dim(moe_gain, core * width, width)
    router_half = lax.dynamic_slice_in_dim(router, core * width, width, axis=0)
    logits_half = jnp.dot(
        hidden_float * gain_half, router_half.astype(jnp.float32), precision=lax.Precision.HIGHEST
    )
    picked_half = jnp.sum(
        jnp.where(
            routes[:, :, None] == jnp.arange(router.shape[1])[None, None, :],
            logits_half[:, None, :],
            0.0,
        ),
        axis=2,
    )
    square_half = jnp.sum(hidden_float * hidden_float, axis=1, keepdims=True)
    sums_half = jnp.concatenate([picked_half, square_half], axis=1)
    sums = sums_half + lax.ppermute(sums_half, "exp", exchange)
    inverse = lax.rsqrt(sums[:, 2:] / (2 * width) + 1e-06)
    gates = jax.nn.sigmoid(sums[:, :2] * inverse)
    shares = gates / jnp.sum(gates, axis=1, keepdims=True)
    weighting = jnp.concatenate(
        [jnp.sum(jnp.where(match, shares[:, :, None], 0.0), axis=1) for match in matches], axis=1
    )

    out_low, out_high = (expert_out[:, :width], expert_out[:, width:])
    out_own = jnp.where(core == 0, out_low, out_high)
    out_other = lax.ppermute(jnp.where(core == 0, out_high, out_low), "exp", exchange)
    outs = jnp.where(
        core == 0,
        jnp.concatenate([out_own, out_other], axis=0),
        jnp.concatenate([out_other, out_own], axis=0),
    ).astype(jnp.float32)
    expert_sum = jnp.dot(weighting, outs, precision=lax.Precision.HIGHEST)
    return (hidden_float + expert_sum).astype(jnp.bfloat16)


def solution(mesh):
    placed = (
        P(("groups", "seq"), "exp"),
        P(("groups", "seq"), "exp"),
        P(("groups", "seq"), "exp"),
        P(("groups", "seq"), "exp"),
        P(("groups", "seq"), "exp"),
        P("exp"),
        P(),
        P(),
        P(("groups", "seq"), None),
        P(("groups", "seq"), None),
        P("exp", None, "seq"),
        P("exp", None, "seq"),
        P("exp", "seq", None),
    )
    return jax.shard_map(
        shards, mesh=mesh, in_specs=placed, out_specs=P(("groups", "seq"), "exp"), check_vma=False
    )
```

```python
import functools

import jax
import jax.numpy as jnp
from jax import lax
from jax.experimental import pallas as pl
from jax.experimental.pallas import tpu as pltpu
from jax.sharding import PartitionSpec as P

CAP = 16
CHUNKS = 3
VMEM = pl.BlockSpec(memory_space=pltpu.VMEM)
SMEM = pl.BlockSpec(memory_space=pltpu.SMEM)
HBM = pl.BlockSpec(memory_space=pl.ANY)
F32, BF16 = (jnp.float32, jnp.bfloat16)


def grant(mebibytes):
    return pltpu.CompilerParams(vmem_limit_bytes=mebibytes * 2**20)


def triangle(length):
    rows = lax.broadcasted_iota(jnp.int32, (length, length), 0)
    columns = lax.broadcasted_iota(jnp.int32, (length, length), 1)
    return rows >= columns


def as_columns(table):
    heads, length = table.shape
    return jnp.concatenate([table, jnp.zeros((length - heads, length), F32)], axis=0).T


def state_kernel(odd_ref, log_ref, key_ref, value_ref, run_ref, full_ref, narrow_ref):
    heads, length = log_ref.shape
    width = key_ref.shape[1] // heads
    half = heads // 2
    running = lax.dot_general(
        log_ref[...],
        jnp.where(triangle(length), 1.0, 0.0),
        (((1,), (1,)), ((), ())),
        precision=lax.Precision.HIGHEST,
        preferred_element_type=F32,
    )
    run_ref[...] = running
    rest = as_columns(jnp.exp(running[:, length - 1 :] - running))
    for head in range(heads):
        lanes = slice(head * width, (head + 1) * width)
        scaled = (key_ref[:, lanes].astype(F32) * rest[:, head : head + 1]).astype(BF16)
        state = lax.dot_general(
            scaled, value_ref[:, lanes], (((0,), (0,)), ((), ())), preferred_element_type=F32
        )
        side = odd_ref[0] if head < half else 1 - odd_ref[0]
        place = side * half + head % half
        full_ref[place] = state
        narrow_ref[place] = state.astype(BF16)


def block_state(odd, log_rows, key_rows, value_rows):
    heads, length = log_rows.shape
    width = key_rows.shape[1] // heads
    return pl.pallas_call(
        state_kernel,
        out_shape=(
            jax.ShapeDtypeStruct((heads, length), F32),
            jax.ShapeDtypeStruct((heads, width, width), F32),
            jax.ShapeDtypeStruct((heads, width, width), BF16),
        ),
        in_specs=[SMEM, VMEM, VMEM, VMEM],
        out_specs=(VMEM, VMEM, VMEM),
        compiler_params=grant(16),
        cost_estimate=pl.CostEstimate(
            flops=2 * length * width * width * heads,
            bytes_accessed=4 * length * width * heads + 6 * heads * width * width,
            transcendentals=0,
        ),
    )(odd, log_rows, key_rows, value_rows)


def within_kernel(run_ref, query_ref, key_ref, value_ref, out_ref):
    heads, length = run_ref.shape
    width = key_ref.shape[1] // heads
    causal = triangle(length)
    running = run_ref[...]
    columns = as_columns(running)
    for head in range(heads):
        lanes = slice(head * width, (head + 1) * width)
        scores = lax.dot_general(
            query_ref[:, lanes],
            key_ref[:, lanes],
            (((1,), (1,)), ((), ())),
            preferred_element_type=F32,
        )
        spread = columns[:, head : head + 1] - running[head : head + 1, :]
        decay = jnp.exp(jnp.where(causal, spread, 0.0))
        mixing = jnp.where(causal, scores * decay, 0.0).astype(BF16)
        out_ref[:, lanes] = jnp.dot(mixing, value_ref[:, lanes], preferred_element_type=F32)


def within_block(running, query_rows, key_rows, value_rows):
    heads, length = running.shape
    width = key_rows.shape[1] // heads
    return pl.pallas_call(
        within_kernel,
        out_shape=jax.ShapeDtypeStruct(query_rows.shape, F32),
        in_specs=[VMEM] * 4,
        out_specs=VMEM,
        compiler_params=grant(16),
        cost_estimate=pl.CostEstimate(
            flops=4 * length * length * width * heads,
            bytes_accessed=10 * length * width * heads,
            transcendentals=heads * length * length,
        ),
    )(running, query_rows, key_rows, value_rows)


def hidden_kernel(odd_ref, run_ref, query_ref, within_ref, residual_ref, gain_ref, table_ref, *refs):
    states, (hidden_ref, own_ref, other_ref) = (refs[:-3], refs[-3:])
    heads, length = run_ref.shape
    width = query_ref.shape[1] // heads
    half, part = (heads // 2, states[0].shape[0])
    grown = as_columns(jnp.exp(run_ref[...]))
    even = odd_ref[0] == 0
    for head in range(heads):
        lanes = slice(head * width, (head + 1) * width)
        chunk, place = divmod(head % half, part)
        kept, swapped = (states[chunk][place], states[CHUNKS + chunk][place])
        state = jnp.where(even, kept, swapped) if head < half else jnp.where(even, swapped, kept)
        carried = jnp.dot(query_ref[:, lanes], state, preferred_element_type=F32)
        raw = within_ref[:, lanes] + carried * grown[:, head : head + 1]
        normed = raw * lax.rsqrt(jnp.mean(raw * raw, axis=1, keepdims=True) + 1e-05)
        hidden_ref[:, lanes] = (
            residual_ref[:, lanes].astype(F32) + normed * gain_ref[:, lanes]
        ).astype(BF16)
    rows = jnp.dot(table_ref[...], hidden_ref[...], preferred_element_type=F32).astype(BF16)
    own_ref[...] = rows[: own_ref.shape[0]]
    other_ref[...] = rows[own_ref.shape[0] :]


def hidden_rows(odd, running, query_rows, within, residual, gain, table, kept, swapped):
    heads, length = running.shape
    capacity = table.shape[0] // 2
    wide = query_rows.shape[1]
    return pl.pallas_call(
        hidden_kernel,
        out_shape=(
            jax.ShapeDtypeStruct((length, wide), BF16),
            jax.ShapeDtypeStruct((capacity, wide), BF16),
            jax.ShapeDtypeStruct((capacity, wide), BF16),
        ),
        in_specs=[SMEM] + [VMEM] * (6 + 2 * CHUNKS),
        out_specs=(VMEM, VMEM, VMEM),
        compiler_params=grant(16),
        cost_estimate=pl.CostEstimate(
            flops=2 * length * wide * (wide // heads),
            bytes_accessed=12 * length * wide,
            transcendentals=0,
        ),
    )(odd, running, query_rows, within, residual, gain, table, *kept, *swapped)


def buffer_kernel(core_ref, own_ref, other_ref, gain_ref, out_ref):
    width = own_ref.shape[1]
    own, other = (own_ref[...].astype(F32), other_ref[...].astype(F32))
    first = core_ref[0] == 0
    low, high = (jnp.where(first, own, other), jnp.where(first, other, own))
    squares = jnp.sum(low * low + high * high, axis=1, keepdims=True)
    inverse = lax.rsqrt(squares / (2 * width) + 1e-06)
    out_ref[:, :width] = (low * inverse * gain_ref[:, :width]).astype(BF16)
    out_ref[:, width:] = (high * inverse * gain_ref[:, width:]).astype(BF16)


def buffer_rows(core, own, other, gain, weights):
    capacity, width = own.shape
    return pl.pallas_call(
        buffer_kernel,
        out_shape=jax.ShapeDtypeStruct((capacity, 2 * width), BF16),
        in_specs=[SMEM, VMEM, VMEM, VMEM],
        out_specs=VMEM,
        compiler_params=grant(4),
        cost_estimate=pl.CostEstimate(
            flops=1500 * sum(weight.size for weight in weights),
            bytes_accessed=8 * capacity * width,
            transcendentals=0,
        ),
    )(core, own, other, gain)


def expert_kernel(deep, wide, row_ref, gate_ref, up_ref, down_ref, out_ref):
    width, units = gate_ref.shape
    gate_part = jnp.zeros((row_ref.shape[0], units), F32)
    up_part = jnp.zeros((row_ref.shape[0], units), F32)
    for step in range(width // deep):
        lanes = slice(step * deep, (step + 1) * deep)
        gate_part += jnp.dot(row_ref[:, lanes], gate_ref[lanes], preferred_element_type=F32)
        up_part += jnp.dot(row_ref[:, lanes], up_ref[lanes], preferred_element_type=F32)
    hidden = (jax.nn.silu(gate_part) * up_part).astype(BF16)
    for step in range(width // wide):
        lanes = slice(step * wide, (step + 1) * wide)
        out_ref[:, lanes] = jnp.dot(hidden, down_ref[:, lanes], preferred_element_type=F32)


def expert_rows(segment, gate_weight, up_weight, down_weight):
    width, units = gate_weight.shape
    deep = wide = width // 6
    return pl.pallas_call(
        functools.partial(expert_kernel, deep, wide),
        out_shape=jax.ShapeDtypeStruct((segment.shape[0], width), F32),
        in_specs=[VMEM] * 4,
        out_specs=VMEM,
        compiler_params=grant(8),
        cost_estimate=pl.CostEstimate(
            flops=6 * segment.shape[0] * width * units,
            bytes_accessed=6 * width * units,
            transcendentals=0,
        ),
    )(segment, gate_weight, up_weight, down_weight)


def slot_matches(routes, slot_pos, expert, capacity):
    return (routes == expert)[:, :, None] & (
        slot_pos[:, :, None] == jnp.arange(capacity)[None, None, :]
    )


def after(value, *others):
    return lax.optimization_barrier((value, *others))[0]


def entering_state(odd, full, narrow, block_total, aside):
    count = lax.axis_size("seq")
    swap = [(i, i ^ 1) for i in range(count)]
    half = full.shape[0] // 2
    part = half // CHUNKS
    low, high = (block_total[:half], block_total[half:])
    total_own = jnp.where(odd, high, low)
    total_other = lax.ppermute(jnp.where(odd, low, high)[None], "seq", swap)[0]
    even_decay = jnp.exp(jnp.where(odd, total_other, total_own))[:, None, None]
    odd_decay = jnp.exp(jnp.where(odd, total_own, total_other))[:, None, None]
    pair_decay = even_decay * odd_decay
    places = [slice(chunk * part, (chunk + 1) * part) for chunk in range(CHUNKS)]
    even_states, pair_states = ([], [])
    for place in places:
        own = full[place]
        arrived = lax.ppermute(
            narrow[half + place.start : half + place.stop], "seq", swap
        ).astype(F32)
        even_states.append(jnp.where(odd, arrived, own))
        odd_state = jnp.where(odd, own, arrived)
        pair_states.append(odd_decay[place] * even_states[-1] + odd_state)
    links = count // 2 - 1
    befores = [jnp.zeros_like(state) for state in pair_states]
    sents = [state.astype(BF16) for state in pair_states]
    kept, swapped = ([None] * CHUNKS, [None] * CHUNKS)
    marks, result = ([sents[-1]], None)
    for link in range(links):
        pairs = [(2 * link + k, 2 * link + 2 + k) for k in range(2)]
        gots = [lax.ppermute(sent, "seq", pairs) for sent in sents]
        if link == links - 1:
            result = aside(sents[-1])
            marks = [*marks, *result]
        for chunk, place in enumerate(places):
            got = after(gots[chunk], *marks).astype(F32)
            before = befores[chunk] = befores[chunk] + got
            if link < links - 1:
                sents[chunk] = (pair_decay[place] * before + pair_states[chunk]).astype(BF16)
                marks = [sents[chunk]]
            else:
                between = even_decay[place] * before + even_states[chunk]
                kept[chunk] = jnp.where(odd, between, before).astype(BF16)
                marks = [jnp.where(odd, before, between).astype(BF16)]
                swapped[chunk] = lax.ppermute(marks[0], "seq", swap)
    return (kept, swapped, result)


def ring_pairs(count):
    order = list(range(0, count, 2)) + list(range(count - 1, 0, -2))
    right = [(order[i], order[(i + 1) % count]) for i in range(count)]
    return (right, [(b, a) for a, b in right])


def ring_gather(unit):
    count = lax.axis_size("seq")
    right, left = ring_pairs(count)
    middle = unit.shape[1] // 2
    from_left, from_right = ([], [])
    moving_right, moving_left = (unit, unit)
    for _ in range(count // 2 - 1):
        moving_right = after(lax.ppermute(moving_right, "seq", right), moving_left)
        moving_left = after(lax.ppermute(moving_left, "seq", left), moving_right)
        from_left.append(moving_right)
        from_right.append(moving_left)
    far_left = after(lax.ppermute(moving_right[:, :middle], "seq", right), moving_left)
    far_right = lax.ppermute(moving_left[:, middle:], "seq", left)
    far = jnp.concatenate([far_left, far_right], axis=1)
    return (jnp.concatenate([unit] + from_left + [far] + from_right, axis=0), from_right[0])


def ring_scatter(partial, rows):
    count = lax.axis_size("seq")
    right, left = ring_pairs(count)
    middle = partial.shape[1] // 2
    steps = count // 2

    def piece(position):
        return partial[position * rows : (position + 1) * rows]

    far = piece(steps)
    to_left, to_right = (far[:, :middle].astype(BF16), far[:, middle:].astype(BF16))
    for step in range(steps - 1, -1, -1):
        moving_left = after(lax.ppermute(to_left, "seq", left), to_right).astype(F32)
        arriving = lax.ppermute(to_right, "seq", right)
        if step == 0:
            return piece(0) + moving_left + arriving.astype(F32)
        to_left, to_right = (piece(step), piece(steps + step))
        if step == steps - 1:
            to_left = jnp.concatenate(
                [to_left[:, :middle] + moving_left, to_left[:, middle:]], axis=1
            )
        else:
            to_left = to_left + moving_left
        to_left = to_left.astype(BF16)
        moving_right = after(arriving, to_left).astype(F32)
        if step == steps - 1:
            to_right = jnp.concatenate(
                [to_right[:, :middle], to_right[:, middle:] + moving_right], axis=1
            )
        else:
            to_right = to_right + moving_right
        to_right = to_right.astype(BF16)


def shards(
    queries,
    key_rows,
    values,
    log_decay,
    residual,
    attn_gain,
    moe_gain,
    router,
    routes,
    slot_pos,
    gate_weight,
    up_weight,
    down_weight,
):
    length, width = queries.shape
    core = lax.axis_index("exp")
    exchange = [(0, 1), (1, 0)]
    odd = lax.axis_index("seq") % 2
    odd_scalar = odd.astype(jnp.int32)[None]
    running, full, narrow = block_state(odd_scalar, log_decay.T, key_rows, values)

    def aside(mark):
        experts = jnp.stack([core, 1 - core])
        matches = [slot_matches(after(routes, mark), slot_pos, expert, CAP) for expert in experts]
        table = jnp.concatenate([jnp.any(match, axis=1).T for match in matches]).astype(BF16)
        return (within_block(running, after(queries, mark), key_rows, values), table)

    kept, swapped, (within, table) = entering_state(
        odd == 1, full, narrow, running[:, -1], aside
    )

    hidden_half, rows_own, rows_sent = hidden_rows(
        odd_scalar, running, queries, within, residual, attn_gain[None], table, kept, swapped
    )
    rows_other = lax.ppermute(rows_sent, "exp", exchange)
    buffer = buffer_rows(
        core.astype(jnp.int32)[None],
        rows_own,
        rows_other,
        moe_gain[None],
        (gate_weight, up_weight, down_weight),
    )

    segment, mark = ring_gather(buffer)
    partial = expert_rows(segment, gate_weight[0], up_weight[0], down_weight[0])
    expert_out = ring_scatter(partial, CAP).astype(jnp.bfloat16)

    hidden_float = after(hidden_half, mark).astype(jnp.float32)
    gain_half = lax.dynamic_slice_in_dim(moe_gain, core * width, width)
    router_half = lax.dynamic_slice_in_dim(router, core * width, width, axis=0)
    logits_half = jnp.dot(
        hidden_float * gain_half, router_half.astype(jnp.float32), precision=lax.Precision.HIGHEST
    )
    picked_half = jnp.sum(
        jnp.where(
            routes[:, :, None] == jnp.arange(router.shape[1])[None, None, :],
            logits_half[:, None, :],
            0.0,
        ),
        axis=2,
    )
    square_half = jnp.sum(hidden_float * hidden_float, axis=1, keepdims=True)
    sums_half = jnp.concatenate([picked_half, square_half], axis=1)
    sums = sums_half + lax.ppermute(sums_half, "exp", exchange)
    inverse = lax.rsqrt(sums[:, 2:] / (2 * width) + 1e-06)
    gates = jax.nn.sigmoid(sums[:, :2] * inverse)
    shares = gates / jnp.sum(gates, axis=1, keepdims=True)
    matches = [slot_matches(routes, slot_pos, expert, CAP) for expert in range(2)]
    weighting = jnp.concatenate(
        [jnp.sum(jnp.where(match, shares[:, :, None], 0.0), axis=1) for match in matches], axis=1
    )

    out_low, out_high = (expert_out[:, :width], expert_out[:, width:])
    out_own = jnp.where(core == 0, out_low, out_high)
    out_other = lax.ppermute(jnp.where(core == 0, out_high, out_low), "exp", exchange)
    outs = jnp.where(
        core == 0,
        jnp.concatenate([out_own, out_other], axis=0),
        jnp.concatenate([out_other, out_own], axis=0),
    ).astype(jnp.float32)
    expert_sum = jnp.dot(weighting, outs, precision=lax.Precision.HIGHEST)
    return (hidden_float + expert_sum).astype(jnp.bfloat16)


def solution(mesh):
    placed = (
        P(("groups", "seq"), "exp"),
        P(("groups", "seq"), "exp"),
        P(("groups", "seq"), "exp"),
        P(("groups", "seq"), "exp"),
        P(("groups", "seq"), "exp"),
        P("exp"),
        P(),
        P(),
        P(("groups", "seq"), None),
        P(("groups", "seq"), None),
        P("exp", None, "seq"),
        P("exp", None, "seq"),
        P("exp", "seq", None),
    )
    return jax.shard_map(
        shards, mesh=mesh, in_specs=placed, out_specs=P(("groups", "seq"), "exp"), check_vma=False
    )
```

```python
import functools

import jax
import jax.numpy as jnp
from jax import lax
from jax.experimental import pallas as pl
from jax.experimental.pallas import tpu as pltpu
from jax.sharding import PartitionSpec as P

CAP = 16
CHUNKS = 3
VMEM = pl.BlockSpec(memory_space=pltpu.VMEM)
SMEM = pl.BlockSpec(memory_space=pltpu.SMEM)
HBM = pl.BlockSpec(memory_space=pl.ANY)
F32, BF16 = (jnp.float32, jnp.bfloat16)


def grant(mebibytes):
    return pltpu.CompilerParams(vmem_limit_bytes=mebibytes * 2**20)


def triangle(length):
    rows = lax.broadcasted_iota(jnp.int32, (length, length), 0)
    columns = lax.broadcasted_iota(jnp.int32, (length, length), 1)
    return rows >= columns


def as_columns(table):
    heads, length = table.shape
    return jnp.concatenate([table, jnp.zeros((length - heads, length), F32)], axis=0).T


def running_sums(log_rows):
    return lax.dot_general(
        log_rows,
        jnp.where(triangle(log_rows.shape[1]), 1.0, 0.0),
        (((1,), (1,)), ((), ())),
        precision=lax.Precision.HIGHEST,
        preferred_element_type=F32,
    )


def state_kernel(sent, log_ref, key_ref, value_ref, *refs):
    outs, (log, key, value, sems) = (refs[:-4], refs[-4:])
    heads, length = log_ref.shape
    width = key_ref.shape[1] // heads
    half = heads // 2
    part = half // CHUNKS
    side = (lax.axis_index("seq") + sent) % 2
    log_copy = pltpu.make_async_copy(log_ref, log, sems.at[2 * CHUNKS])
    log_copy.start()
    copies = []
    for chunk in range(CHUNKS):
        lanes = pl.ds(pl.multiple_of((side * half + chunk * part) * width, width), part * width)
        here = pl.ds(chunk * part * width, part * width)
        pair = (
            pltpu.make_async_copy(key_ref.at[:, lanes], key.at[:, here], sems.at[2 * chunk]),
            pltpu.make_async_copy(value_ref.at[:, lanes], value.at[:, here], sems.at[2 * chunk + 1]),
        )
        for copy in pair:
            copy.start()
        copies.append(pair)
    log_copy.wait()
    running = running_sums(log[...])
    total = running[:, length - 1 :]
    rest = as_columns(jnp.exp(total - running))
    rest = jnp.where(side == 0, rest[:, :half], rest[:, half:heads])
    for head in range(half):
        chunk, place = divmod(head, part)
        if place == 0:
            for copy in copies[chunk]:
                copy.wait()
        lanes = slice(head * width, (head + 1) * width)
        scaled = (key[:, lanes].astype(F32) * rest[:, head : head + 1]).astype(BF16)
        state = lax.dot_general(
            scaled, value[:, lanes], (((0,), (0,)), ((), ())), preferred_element_type=F32
        )
        rows = slice(place * width, (place + 1) * width)
        outs[chunk][rows, :] = state.astype(outs[chunk].dtype)
    if sent:
        totals = as_columns(jnp.broadcast_to(total, (heads, length)))[:1]
        totals = jnp.where(side == 0, totals[:, :half], totals[:, half:heads])
        first = totals.astype(BF16).astype(F32)
        second = (totals - first).astype(BF16).astype(F32)
        third = totals - first - second
        rows = jnp.concatenate([first, second, third, jnp.zeros((13, half), F32)], axis=0)
        rows = jnp.concatenate([rows, jnp.zeros((16, width - half), F32)], axis=1)
        outs[0][part * width :, :] = rows.astype(BF16)
    else:
        outs[CHUNKS][...] = running


def half_state(sent, log_rows, key_rows, value_rows):
    heads, length = log_rows.shape
    width = key_rows.shape[1] // heads
    rows = heads // 2 // CHUNKS * width
    shapes = [jax.ShapeDtypeStruct((rows, width), BF16 if sent else F32)] * CHUNKS
    if sent:
        shapes[0] = jax.ShapeDtypeStruct((rows + 16, width), BF16)
    else:
        shapes.append(jax.ShapeDtypeStruct((heads, length), F32))
    return pl.pallas_call(
        functools.partial(state_kernel, sent),
        out_shape=tuple(shapes),
        in_specs=[HBM, HBM, HBM],
        out_specs=(VMEM,) * len(shapes),
        scratch_shapes=[
            pltpu.VMEM((heads, length), F32),
            pltpu.VMEM((length, heads // 2 * width), BF16),
            pltpu.VMEM((length, heads // 2 * width), BF16),
            pltpu.SemaphoreType.DMA((2 * CHUNKS + 1,)),
        ],
        compiler_params=grant(60 if sent else 8),
        cost_estimate=pl.CostEstimate(
            flops=length * width * width * heads,
            bytes_accessed=2 * length * width * heads,
            transcendentals=0,
        ),
    )(log_rows, key_rows, value_rows)


def slots_of(route_ref, slot_ref, capacity, values):
    shape = (2 * capacity, route_ref.shape[1])
    place = lax.broadcasted_iota(jnp.int32, shape, 0)
    expert = jnp.where(place < capacity, lax.axis_index("exp"), 1 - lax.axis_index("exp"))
    slot = place % capacity
    table = jnp.zeros(shape, F32)
    for choice, value in enumerate(values):
        here = slice(choice, choice + 1)
        match = (route_ref[here, :] == expert) & (slot_ref[here, :] == slot)
        table += jnp.where(match, value, 0.0)
    return table


def within_kernel(
    sent, run_ref, query_ref, key_ref, value_ref, residual_ref, route_ref, slot_ref, out_ref, pack_ref
):
    heads, length = run_ref.shape
    width = key_ref.shape[1] // heads
    half = heads // 2
    span = half * width
    causal = triangle(length)
    side = (lax.axis_index("seq") + sent) % 2
    running = jnp.where(side == 0, run_ref[:half, :], run_ref[half:, :])
    columns = as_columns(running)
    for head in range(half):
        lanes = pl.ds(pl.multiple_of((side * half + head) * width, width), width)
        scores = lax.dot_general(
            query_ref[:, lanes],
            key_ref[:, lanes],
            (((1,), (1,)), ((), ())),
            preferred_element_type=F32,
        )
        spread = columns[:, head : head + 1] - running[head : head + 1, :]
        mixing = jnp.where(causal, scores * jnp.exp(spread), 0.0).astype(BF16)
        out_ref[:, head * width : (head + 1) * width] = jnp.dot(
            mixing, value_ref[:, lanes], preferred_element_type=F32
        )

    table = slots_of(route_ref, slot_ref, pack_ref.shape[0] // 2, (1.0, 1.0)).astype(BF16)

    def routed(array):
        return jnp.dot(table, array, preferred_element_type=F32).astype(BF16)

    grown = jnp.exp(columns)
    high = grown.astype(BF16)
    low = (grown - high.astype(F32)).astype(BF16)
    lanes = pl.ds(pl.multiple_of(side * span, span), span)
    pack_ref[:, :span] = routed(query_ref[:, lanes])
    pack_ref[:, span : 2 * span] = routed(residual_ref[:, lanes])
    pack_ref[:, 2 * span : 3 * span] = routed(out_ref[...].astype(BF16))
    blank = jnp.zeros((table.shape[0], width // 2 - half), BF16)
    pack_ref[:, 3 * span :] = jnp.concatenate(
        [routed(high)[:, :half], blank, routed(low)[:, :half], blank], axis=1
    )


def within_block(sent, running, query_rows, key_rows, value_rows, residual, routes, slots):
    heads, length = running.shape
    width = key_rows.shape[1] // heads
    span = heads // 2 * width
    return pl.pallas_call(
        functools.partial(within_kernel, sent),
        out_shape=(
            jax.ShapeDtypeStruct((length, span), F32),
            jax.ShapeDtypeStruct((2 * CAP, 3 * span + width), BF16),
        ),
        in_specs=[VMEM] * 7,
        out_specs=(VMEM, VMEM),
        compiler_params=grant(16),
        cost_estimate=pl.CostEstimate(
            flops=4 * length * length * span,
            bytes_accessed=12 * length * span,
            transcendentals=heads // 2 * length * length,
        ),
    )(running, query_rows, key_rows, value_rows, residual, routes, slots)


def rows_kernel(chunk, own_ref, got_ref, gain_ref, kept_ref, moved_ref, mine_ref, theirs_ref):
    part, width, _ = kept_ref.shape
    half = part * CHUNKS
    span = half * width
    odd = lax.axis_index("seq") % 2
    capacity = own_ref.shape[0] // 2
    for pack, state_ref, moved in ((own_ref, kept_ref, 0), (got_ref, moved_ref, 1)):
        tail = pack[:, 3 * span :].astype(F32)
        grown = tail[:, :half] + tail[:, width // 2 : width // 2 + half]
        place = pl.ds(pl.multiple_of((odd ^ moved) * capacity, capacity), capacity)
        for index in range(part):
            head = chunk * part + index
            lanes = [slice(k * span + head * width, k * span + (head + 1) * width) for k in range(3)]
            gain = jnp.where(odd == 0, gain_ref[:, lanes[0]], gain_ref[:, lanes[1]])
            query, residual, within = [pack[:, lane] for lane in lanes]
            carried = jnp.dot(query, state_ref[index], preferred_element_type=F32)
            raw = within.astype(F32) + carried * grown[:, head : head + 1]
            normed = raw * lax.rsqrt(jnp.mean(raw * raw, axis=1, keepdims=True) + 1e-05)
            hidden = (residual.astype(F32) + normed * gain).astype(BF16)
            here = slice(index * width, (index + 1) * width)
            mine_ref[place, here] = hidden[:capacity]
            theirs_ref[place, here] = hidden[capacity:]


def pair_rows(chunk, own, got, gain, kept, moved, weights):
    part, width, _ = kept.shape
    rows = own.shape[0]
    shape = jax.ShapeDtypeStruct((rows, part * width), BF16)
    flops = 4 * rows * part * width * width
    if chunk == CHUNKS - 1:
        flops = 1500 * sum(weight.size for weight in weights)
    return pl.pallas_call(
        functools.partial(rows_kernel, chunk),
        out_shape=(shape, shape),
        in_specs=[VMEM] * 5,
        out_specs=(VMEM, VMEM),
        compiler_params=grant(8),
        cost_estimate=pl.CostEstimate(
            flops=flops, bytes_accessed=12 * own.size, transcendentals=0
        ),
    )(own, got, gain, kept, moved)


def hidden_kernel(
    run_ref,
    query_ref,
    own_ref,
    other_ref,
    residual_ref,
    gain_ref,
    moe_gain_ref,
    router_ref,
    route_ref,
    *refs,
):
    *state_refs, hidden_ref, sums_ref = refs
    heads, length = run_ref.shape
    span = query_ref.shape[1]
    width = span // heads
    half, part = (heads // 2, state_refs[0].shape[0])
    grown = as_columns(jnp.exp(run_ref[...]))
    even = lax.axis_index("seq") % 2 == 0
    squares = jnp.zeros((length, width), F32)
    for head in range(heads):
        lanes = slice(head * width, (head + 1) * width)
        chunk, place = divmod(head % half, part)
        kept, swapped = (state_refs[chunk][place], state_refs[CHUNKS + chunk][place])
        here = slice(head % half * width, (head % half + 1) * width)
        own, other = (own_ref[:, here], other_ref[:, here])
        if head >= half:
            kept, swapped, own, other = (swapped, kept, other, own)
        state, within = (jnp.where(even, kept, swapped), jnp.where(even, own, other))
        carried = jnp.dot(query_ref[:, lanes], state, preferred_element_type=F32)
        raw = within + carried * grown[:, head : head + 1]
        normed = raw * lax.rsqrt(jnp.mean(raw * raw, axis=1, keepdims=True) + 1e-05)
        hidden = (residual_ref[:, lanes].astype(F32) + normed * gain_ref[:, lanes]).astype(BF16)
        hidden_ref[:, lanes] = hidden
        value = hidden.astype(F32)
        squares += value * value
    here = pl.ds(pl.multiple_of(lax.axis_index("exp") * span, span), span)
    weights = router_ref[:, here].astype(F32) * moe_gain_ref[:, here]
    first = weights.astype(BF16)
    second = (weights - first.astype(F32)).astype(BF16)
    third = (weights - first.astype(F32) - second.astype(F32)).astype(BF16)
    products = lax.dot_general(
        hidden_ref[...],
        jnp.concatenate([first, second, third, jnp.zeros_like(first)], axis=0),
        (((1,), (1,)), ((), ())),
        preferred_element_type=F32,
    ).T
    count = weights.shape[0]
    logits = products[:count] + products[count : 2 * count] + products[2 * count : 3 * count]
    expert = lax.broadcasted_iota(jnp.int32, logits.shape, 0)
    for choice in range(2):
        here = slice(choice, choice + 1)
        chosen = jnp.where(route_ref[here, :] == expert, logits, 0.0)
        sums_ref[here, :] = jnp.sum(chosen, axis=0, keepdims=True)
    sums_ref[2:3, :] = jnp.sum(squares.T, axis=0, keepdims=True)
    sums_ref[3:, :] = jnp.zeros((sums_ref.shape[0] - 3, length), F32)


def hidden_block(
    running, query_rows, own, other, residual, gain, moe_gain, router, routes, kept, swapped
):
    heads, length = running.shape
    wide = query_rows.shape[1]
    return pl.pallas_call(
        hidden_kernel,
        out_shape=(
            jax.ShapeDtypeStruct((length, wide), BF16),
            jax.ShapeDtypeStruct((8, length), F32),
        ),
        in_specs=[VMEM] * (9 + 2 * CHUNKS),
        out_specs=(VMEM, VMEM),
        compiler_params=grant(16),
        cost_estimate=pl.CostEstimate(
            flops=2 * length * wide * (wide // heads),
            bytes_accessed=12 * length * wide,
            transcendentals=0,
        ),
    )(
        running, query_rows, own, other, residual, gain, moe_gain, router, routes, *kept, *swapped
    )


def expert_kernel(order_ref, gain_ref, gate_ref, up_ref, down_ref, *refs):
    *units, out_ref, square_ref, scaled_ref, hidden_ref = refs
    width = gate_ref.shape[0]
    count = order_ref.shape[0]
    steps = count // 2
    capacity = scaled_ref.shape[0] // count
    quarter = width // 4

    pieces = [(steps, 0, units[steps]), (steps, 1, units[steps + 1])]
    for position, unit in [*enumerate(units[:steps]), *enumerate(units[steps + 2 :], steps + 1)]:
        for side in range(2):
            pieces.append((position, side, unit.at[:, side * quarter : (side + 1) * quarter]))

    def block_of(position):
        return order_ref[lax.axis_index("seq"), position]

    def rows_of(position):
        first = block_of(position) // 2 * (2 * capacity)
        return pl.ds(pl.multiple_of(first, 2 * capacity), 2 * capacity)

    square_ref[...] = jnp.zeros_like(square_ref)
    for position, side, piece in pieces:
        value = piece[...].astype(F32)
        square = jnp.sum(value * value, axis=1, keepdims=True)
        square_ref[rows_of(position), :] += jnp.broadcast_to(square, (2 * capacity, 128))
        first = ((lax.axis_index("exp") ^ side) * 2 + block_of(position) % 2) * quarter
        lanes = pl.ds(pl.multiple_of(first, quarter), quarter)
        scaled_ref[rows_of(position), lanes] = (value * gain_ref[:, lanes]).astype(BF16)
    inverse = lax.rsqrt(square_ref[...][:, :1] / width + 1e-06)

    chunks = [slice(part * quarter, (part + 1) * quarter) for part in range(4)]
    gate_part, up_part = (0.0, 0.0)
    for lanes in chunks:
        rows = scaled_ref[:, lanes]
        gate_part += jnp.dot(rows, gate_ref[lanes], preferred_element_type=F32)
        up_part += jnp.dot(rows, up_ref[lanes], preferred_element_type=F32)
    gate_part, up_part = (gate_part * inverse, up_part * inverse)
    hidden_ref[...] = (jax.nn.silu(gate_part) * up_part).astype(BF16)
    hidden = jnp.concatenate(
        [
            hidden_ref[pl.ds(pl.multiple_of(block_of(position) * capacity, capacity), capacity)]
            for position in range(count)
        ],
        axis=0,
    )
    for lanes in chunks:
        out_ref[:, lanes] = jnp.dot(hidden, down_ref[:, lanes], preferred_element_type=F32)


def expert_rows(order, gain, units, gate_weight, up_weight, down_weight):
    width, hidden_units = gate_weight.shape
    rows = order.shape[0] * CAP
    return pl.pallas_call(
        expert_kernel,
        out_shape=jax.ShapeDtypeStruct((rows, width), F32),
        in_specs=[SMEM] + [VMEM] * (4 + len(units)),
        out_specs=VMEM,
        scratch_shapes=[
            pltpu.VMEM((rows, 128), F32),
            pltpu.VMEM((rows, width), BF16),
            pltpu.VMEM((rows, hidden_units), BF16),
        ],
        compiler_params=grant(max(16, rows // 16)),
        cost_estimate=pl.CostEstimate(
            flops=6 * rows * width * hidden_units,
            bytes_accessed=6 * width * hidden_units,
            transcendentals=0,
        ),
    )(order, gain, gate_weight, up_weight, down_weight, *units)


def total_kernel(own_ref, left_ref, right_ref, kept_ref, sent_ref):
    span = kept_ref.shape[1]
    for side, out_ref in enumerate((kept_ref, sent_ref)):
        lanes = pl.ds(pl.multiple_of((lax.axis_index("exp") ^ side) * span, span), span)
        total = own_ref[:, lanes] + left_ref[:, lanes].astype(F32) + right_ref[:, lanes].astype(F32)
        out_ref[...] = total.astype(BF16)


def expert_total(own, from_left, from_right):
    rows, width = own.shape
    shape = jax.ShapeDtypeStruct((rows, width // 2), BF16)
    return pl.pallas_call(
        total_kernel,
        out_shape=(shape, shape),
        in_specs=[VMEM] * 3,
        out_specs=(VMEM, VMEM),
        compiler_params=grant(4),
        cost_estimate=pl.CostEstimate(
            flops=2 * rows * width, bytes_accessed=10 * rows * width, transcendentals=0
        ),
    )(own, from_left, from_right)


def share_kernel(span, sums_ref, got_sums_ref, route_ref, slot_ref, table_ref):
    capacity = table_ref.shape[1] // 4
    sums = sums_ref[...] + got_sums_ref[...]
    inverse = lax.rsqrt(sums[2:3] / (2 * span) + 1e-06)
    gates = jax.nn.sigmoid(sums[:2] * inverse)
    shares = gates / jnp.sum(gates, axis=0, keepdims=True)
    table = slots_of(route_ref, slot_ref, capacity, (shares[:1], shares[1:]))
    table = as_columns(table)[:, : 2 * capacity]
    high = table.astype(BF16)
    low = (table - high.astype(F32)).astype(BF16)
    table_ref[...] = jnp.concatenate([high, low], axis=1)


def share_table(span, sums, got_sums, routes, slots):
    return pl.pallas_call(
        functools.partial(share_kernel, span),
        out_shape=jax.ShapeDtypeStruct((routes.shape[1], 4 * CAP), BF16),
        in_specs=[VMEM] * 4,
        out_specs=VMEM,
        compiler_params=grant(4),
    )(sums, got_sums, routes, slots)


def mixed_kernel(table_ref, hidden_ref, own_ref, got_ref, out_ref, held_ref, sems):
    span = own_ref.shape[1]
    copies = []
    for part in range(4):
        lanes = slice(part * span // 4, (part + 1) * span // 4)
        outs = jnp.concatenate([own_ref[:, lanes], got_ref[:, lanes]] * 2, axis=0)
        mixed = jnp.dot(table_ref[...], outs, preferred_element_type=F32)
        held_ref[:, lanes] = (hidden_ref[:, lanes].astype(F32) + mixed).astype(BF16)
        copies.append(
            pltpu.make_async_copy(held_ref.at[:, lanes], out_ref.at[:, lanes], sems.at[part])
        )
        copies[-1].start()
    for copy in copies:
        copy.wait()


def mixed_block(table, hidden, own, got):
    return pl.pallas_call(
        mixed_kernel,
        out_shape=jax.ShapeDtypeStruct(hidden.shape, BF16),
        in_specs=[VMEM] * 4,
        out_specs=HBM,
        scratch_shapes=[pltpu.VMEM(hidden.shape, BF16), pltpu.SemaphoreType.DMA((4,))],
        compiler_params=grant(8),
        cost_estimate=pl.CostEstimate(
            flops=8 * hidden.size * own.shape[0],
            bytes_accessed=4 * hidden.size,
            transcendentals=0,
        ),
    )(table, hidden, own, got)


def after(value, *others):
    return lax.optimization_barrier((value, *others))[0]


def entering_state(odd, states, sending, block_total, aside, share, finish):
    count = lax.axis_size("seq")
    swap = [(i, i ^ 1) for i in range(count)]
    rows, width = states[0].shape
    part = rows // width
    half = part * CHUNKS
    total_own = jnp.where(odd, block_total[half:], block_total[:half])
    even_decays, pair_decays, even_states, pair_states, sents, marks = ([], [], [], [], [], [])
    for chunk in range(CHUNKS):
        arrived = after(lax.ppermute(sending[chunk], "seq", swap), *marks)
        if chunk == 0:
            total_other = jnp.sum(arrived[rows : rows + 3, :half].astype(F32), axis=0)
            even_decay = jnp.exp(jnp.where(odd, total_other, total_own))[:, None, None]
            odd_decay = jnp.exp(jnp.where(odd, total_own, total_other))[:, None, None]
        place = slice(chunk * part, (chunk + 1) * part)
        own = states[chunk].reshape(part, width, width)
        arrived = arrived[:rows].astype(F32).reshape(part, width, width)
        even_states.append(jnp.where(odd, arrived, own))
        odd_state = jnp.where(odd, own, arrived)
        even_decays.append(even_decay[place])
        pair_decays.append(even_decay[place] * odd_decay[place])
        pair_states.append(odd_decay[place] * even_states[-1] + odd_state)
        sents.append(pair_states[-1].astype(BF16))
        marks = [sents[-1]]
        if chunk == 0:
            shared = share(sents[-1])
            marks = [*marks, *shared]
    shared = (after(shared[0], sents[-1]), shared[1])
    swapped = lax.ppermute(shared[0], "seq", swap)
    marks = [sents[-1], shared[0]]
    links = count // 2 - 1
    turn = max(links - 2, 0)
    befores = [jnp.zeros_like(state) for state in pair_states]
    finished = []
    for link in range(links):
        pairs = [(2 * link + k, 2 * link + 2 + k) for k in range(2)]
        gots = [lax.ppermute(sent, "seq", pairs) for sent in sents]
        if link == turn:
            result = aside(sents[-1])
            marks = [*marks, *result]
        for chunk in range(CHUNKS):
            got = after(gots[chunk], *marks).astype(F32)
            before = befores[chunk] = befores[chunk] + got
            if link < links - 1:
                sents[chunk] = (pair_decays[chunk] * before + pair_states[chunk]).astype(BF16)
                marks = [sents[chunk]]
            else:
                between = even_decays[chunk] * before + even_states[chunk]
                kept = jnp.where(odd, between, before).astype(BF16)
                moved = jnp.where(odd, before, between).astype(BF16)
                marks = [kept, moved]
            if link == links - 1:
                finished.append(finish(chunk, kept, moved, result[0], swapped))
                marks = [*marks, *finished[-1][:2]]
    return (finished, result[1], shared[1])


def ring_order(count):
    return list(range(0, count, 2)) + list(range(count - 1, 0, -2))


def ring_pairs(count):
    order = ring_order(count)
    right = [(order[i], order[(i + 1) % count]) for i in range(count)]
    return (right, [(b, a) for a, b in right])


def ring_blocks(count):
    order = ring_order(count)
    steps = count // 2
    offsets = [-k for k in range(steps + 1)] + list(range(1, steps))
    return jnp.array(
        [
            [order[(order.index(block) + offset) % count] for offset in offsets]
            for block in range(count)
        ],
        jnp.int32,
    )


def ring_gather(unit, *holds):
    count = lax.axis_size("seq")
    right, left = ring_pairs(count)
    middle = unit.shape[1] // 2
    from_left, from_right = ([], [])
    moving_right, moving_left = (unit, unit)
    for step in range(count // 2 - 1):
        hold = holds[step](moving_right) if step < len(holds) else ()
        moving_right = after(lax.ppermute(moving_right, "seq", right), moving_left, *hold)
        moving_left = after(lax.ppermute(moving_left, "seq", left), moving_right)
        from_left.append(moving_right)
        from_right.append(moving_left)
    far_left = after(lax.ppermute(moving_right[:, :middle], "seq", right), moving_left)
    far_right = lax.ppermute(moving_left[:, middle:], "seq", left)
    return [unit, *from_left, far_left, far_right, *from_right]


def ring_scatter(partial, rows, hold):
    count = lax.axis_size("seq")
    right, left = ring_pairs(count)
    middle = partial.shape[1] // 2
    steps = count // 2

    def piece(position):
        return partial[position * rows : (position + 1) * rows]

    far = piece(steps)
    to_left, to_right = (far[:, :middle].astype(BF16), far[:, middle:].astype(BF16))
    for step in range(steps - 1, -1, -1):
        marks = (to_right, hold) if step == steps - 1 else (to_right,)
        moving_left = after(lax.ppermute(to_left, "seq", left), *marks)
        arriving = lax.ppermute(to_right, "seq", right)
        if step == 0:
            return (piece(0), moving_left, arriving)
        to_left, to_right = (piece(step), piece(steps + step))
        if step == steps - 1:
            to_left = jnp.concatenate(
                [to_left[:, :middle] + moving_left.astype(F32), to_left[:, middle:]], axis=1
            )
        else:
            to_left = to_left + moving_left.astype(F32)
        to_left = to_left.astype(BF16)
        moving_right = after(arriving, to_left).astype(F32)
        if step == steps - 1:
            to_right = jnp.concatenate(
                [to_right[:, :middle], to_right[:, middle:] + moving_right], axis=1
            )
        else:
            to_right = to_right + moving_right
        to_right = to_right.astype(BF16)


def shards(
    queries,
    key_rows,
    values,
    log_decay,
    residual,
    attn_gain,
    moe_gain,
    router,
    routes,
    slot_pos,
    gate_weight,
    up_weight,
    down_weight,
):
    count = lax.axis_size("seq")
    exchange = [(0, 1), (1, 0)]
    swap = [(i, i ^ 1) for i in range(count)]
    log_rows, route_rows, slot_rows = (log_decay.T, routes.T, slot_pos.T)
    attn_gain, moe_gain = (attn_gain[None], moe_gain[None])
    odd = lax.axis_index("seq") % 2 == 1
    sending = half_state(True, after(log_rows, odd), key_rows, values)
    *states, running = half_state(False, after(log_rows, sending[0]), key_rows, values)

    def routed(sent, mark):
        within, pack = within_block(
            sent,
            running,
            after(queries, mark),
            key_rows,
            values,
            residual,
            route_rows,
            slot_rows,
        )
        return (pack, within)

    weights = (gate_weight, up_weight, down_weight)

    def finish(chunk, kept, moved, own, got):
        rows = pair_rows(chunk, own, got, attn_gain, kept, moved, weights)
        return (*rows, kept, lax.ppermute(moved, "seq", swap))

    finished, within_own, within_other = entering_state(
        odd,
        states,
        sending,
        running[:, -1],
        functools.partial(routed, False),
        functools.partial(routed, True),
        finish,
    )
    rows_mine, rows_sent, kept, swapped = zip(*finished, strict=True)
    rows_got = lax.ppermute(jnp.concatenate(rows_sent, axis=1), "exp", exchange)
    unit = jnp.concatenate([*rows_mine, after(rows_got, *swapped[:3])], axis=1)

    held = []

    def hold_hidden(mark):
        held.extend(
            hidden_block(
                running,
                queries,
                within_own,
                within_other,
                after(residual, mark),
                attn_gain,
                moe_gain,
                router.T,
                route_rows,
                kept,
                swapped,
            )
        )
        return held

    def hold_sums(mark):
        held.append(lax.ppermute(after(held[1], mark), "exp", exchange))
        return held[2:]

    units = ring_gather(unit, hold_hidden, hold_sums)
    hidden_half, sums, got_sums = held
    partial = expert_rows(
        ring_blocks(count), moe_gain, units, gate_weight[0], up_weight[0], down_weight[0]
    )
    table = share_table(queries.shape[1], sums, got_sums, route_rows, slot_rows)
    own, from_right, from_left = ring_scatter(partial, CAP, table)
    out_own, out_sent = expert_total(own, from_right, from_left)
    out_got = lax.ppermute(out_sent, "exp", exchange)
    return mixed_block(table, hidden_half, out_own, out_got)


def solution(mesh):
    placed = (
        P(("groups", "seq"), "exp"),
        P(("groups", "seq"), "exp"),
        P(("groups", "seq"), "exp"),
        P(("groups", "seq"), "exp"),
        P(("groups", "seq"), "exp"),
        P("exp"),
        P(),
        P(),
        P(("groups", "seq"), None),
        P(("groups", "seq"), None),
        P("exp", None, "seq"),
        P("exp", None, "seq"),
        P("exp", "seq", None),
    )
    return jax.shard_map(
        shards, mesh=mesh, in_specs=placed, out_specs=P(("groups", "seq"), "exp"), check_vma=False
    )
```

```python
import functools

import jax
import jax.numpy as jnp
from jax import lax
from jax.experimental import pallas as pl
from jax.experimental.pallas import tpu as pltpu
from jax.sharding import PartitionSpec as P

CAP = 16
CHUNKS = 3
VMEM = pl.BlockSpec(memory_space=pltpu.VMEM)
SMEM = pl.BlockSpec(memory_space=pltpu.SMEM)
HBM = pl.BlockSpec(memory_space=pl.ANY)
F32, BF16 = (jnp.float32, jnp.bfloat16)


def grant(mebibytes):
    return pltpu.CompilerParams(vmem_limit_bytes=mebibytes * 2**20)


def triangle(length):
    rows = lax.broadcasted_iota(jnp.int32, (length, length), 0)
    columns = lax.broadcasted_iota(jnp.int32, (length, length), 1)
    return rows >= columns


def as_columns(table):
    heads, length = table.shape
    return jnp.concatenate([table, jnp.zeros((length - heads, length), F32)], axis=0).T


def running_sums(log_rows):
    return lax.dot_general(
        log_rows,
        jnp.where(triangle(log_rows.shape[1]), 1.0, 0.0),
        (((1,), (1,)), ((), ())),
        precision=lax.Precision.HIGHEST,
        preferred_element_type=F32,
    )


def state_kernel(sent, log_ref, key_ref, value_ref, *refs):
    outs, (log, key, value, sems) = (refs[:-4], refs[-4:])
    heads, length = log_ref.shape
    width = key_ref.shape[1] // heads
    half = heads // 2
    part = half // CHUNKS
    side = (lax.axis_index("seq") + sent) % 2
    log_copy = pltpu.make_async_copy(log_ref, log, sems.at[2 * CHUNKS])
    log_copy.start()
    copies = []
    for chunk in range(CHUNKS):
        lanes = pl.ds(pl.multiple_of((side * half + chunk * part) * width, width), part * width)
        here = pl.ds(chunk * part * width, part * width)
        pair = (
            pltpu.make_async_copy(key_ref.at[:, lanes], key.at[:, here], sems.at[2 * chunk]),
            pltpu.make_async_copy(value_ref.at[:, lanes], value.at[:, here], sems.at[2 * chunk + 1]),
        )
        for copy in pair:
            copy.start()
        copies.append(pair)
    log_copy.wait()
    running = running_sums(log[...])
    total = running[:, length - 1 :]
    rest = as_columns(jnp.exp(total - running))
    rest = jnp.where(side == 0, rest[:, :half], rest[:, half:heads])
    for head in range(half):
        chunk, place = divmod(head, part)
        if place == 0:
            for copy in copies[chunk]:
                copy.wait()
        lanes = slice(head * width, (head + 1) * width)
        scaled = (key[:, lanes].astype(F32) * rest[:, head : head + 1]).astype(BF16)
        state = lax.dot_general(
            scaled, value[:, lanes], (((0,), (0,)), ((), ())), preferred_element_type=F32
        )
        rows = slice(place * width, (place + 1) * width)
        outs[chunk][rows, :] = state.astype(outs[chunk].dtype)
    if sent:
        totals = as_columns(jnp.broadcast_to(total, (heads, length)))[:1]
        totals = jnp.where(side == 0, totals[:, :half], totals[:, half:heads])
        first = totals.astype(BF16).astype(F32)
        second = (totals - first).astype(BF16).astype(F32)
        third = totals - first - second
        rows = jnp.concatenate([first, second, third, jnp.zeros((13, half), F32)], axis=0)
        rows = jnp.concatenate([rows, jnp.zeros((16, width - half), F32)], axis=1)
        outs[0][part * width :, :] = rows.astype(BF16)
    else:
        outs[CHUNKS][...] = running


def half_state(sent, log_rows, key_rows, value_rows):
    heads, length = log_rows.shape
    width = key_rows.shape[1] // heads
    rows = heads // 2 // CHUNKS * width
    shapes = [jax.ShapeDtypeStruct((rows, width), BF16 if sent else F32)] * CHUNKS
    if sent:
        shapes[0] = jax.ShapeDtypeStruct((rows + 16, width), BF16)
    else:
        shapes.append(jax.ShapeDtypeStruct((heads, length), F32))
    return pl.pallas_call(
        functools.partial(state_kernel, sent),
        out_shape=tuple(shapes),
        in_specs=[HBM, HBM, HBM],
        out_specs=(VMEM,) * len(shapes),
        scratch_shapes=[
            pltpu.VMEM((heads, length), F32),
            pltpu.VMEM((length, heads // 2 * width), BF16),
            pltpu.VMEM((length, heads // 2 * width), BF16),
            pltpu.SemaphoreType.DMA((2 * CHUNKS + 1,)),
        ],
        compiler_params=grant(60 if sent else 8),
        cost_estimate=pl.CostEstimate(
            flops=length * width * width * heads,
            bytes_accessed=2 * length * width * heads,
            transcendentals=0,
        ),
    )(log_rows, key_rows, value_rows)


def slots_of(route_ref, slot_ref, capacity, values):
    shape = (2 * capacity, route_ref.shape[1])
    place = lax.broadcasted_iota(jnp.int32, shape, 0)
    expert = jnp.where(place < capacity, lax.axis_index("exp"), 1 - lax.axis_index("exp"))
    slot = place % capacity
    table = jnp.zeros(shape, F32)
    for choice, value in enumerate(values):
        here = slice(choice, choice + 1)
        match = (route_ref[here, :] == expert) & (slot_ref[here, :] == slot)
        table += jnp.where(match, value, 0.0)
    return table


def within_kernel(
    sent, run_ref, query_ref, key_ref, value_ref, residual_ref, route_ref, slot_ref, out_ref, pack_ref
):
    heads, length = run_ref.shape
    width = key_ref.shape[1] // heads
    half = heads // 2
    span = half * width
    causal = triangle(length)
    side = (lax.axis_index("seq") + sent) % 2
    running = jnp.where(side == 0, run_ref[:half, :], run_ref[half:, :])
    columns = as_columns(running)
    for head in range(half):
        lanes = pl.ds(pl.multiple_of((side * half + head) * width, width), width)
        scores = lax.dot_general(
            query_ref[:, lanes],
            key_ref[:, lanes],
            (((1,), (1,)), ((), ())),
            preferred_element_type=F32,
        )
        spread = columns[:, head : head + 1] - running[head : head + 1, :]
        mixing = jnp.where(causal, scores * jnp.exp(spread), 0.0).astype(BF16)
        out_ref[:, head * width : (head + 1) * width] = jnp.dot(
            mixing, value_ref[:, lanes], preferred_element_type=F32
        )

    table = slots_of(route_ref, slot_ref, pack_ref.shape[0] // 2, (1.0, 1.0)).astype(BF16)

    def routed(array):
        return jnp.dot(table, array, preferred_element_type=F32).astype(BF16)

    grown = jnp.exp(columns)
    high = grown.astype(BF16)
    low = (grown - high.astype(F32)).astype(BF16)
    lanes = pl.ds(pl.multiple_of(side * span, span), span)
    pack_ref[:, :span] = routed(query_ref[:, lanes])
    pack_ref[:, span : 2 * span] = routed(residual_ref[:, lanes])
    pack_ref[:, 2 * span : 3 * span] = routed(out_ref[...].astype(BF16))
    blank = jnp.zeros((table.shape[0], width // 2 - half), BF16)
    pack_ref[:, 3 * span :] = jnp.concatenate(
        [routed(high)[:, :half], blank, routed(low)[:, :half], blank], axis=1
    )


def within_block(sent, running, query_rows, key_rows, value_rows, residual, routes, slots):
    heads, length = running.shape
    width = key_rows.shape[1] // heads
    span = heads // 2 * width
    return pl.pallas_call(
        functools.partial(within_kernel, sent),
        out_shape=(
            jax.ShapeDtypeStruct((length, span), F32),
            jax.ShapeDtypeStruct((2 * CAP, 3 * span + width), BF16),
        ),
        in_specs=[VMEM] * 7,
        out_specs=(VMEM, VMEM),
        compiler_params=grant(16),
        cost_estimate=pl.CostEstimate(
            flops=4 * length * length * span,
            bytes_accessed=12 * length * span,
            transcendentals=heads // 2 * length * length,
        ),
    )(running, query_rows, key_rows, value_rows, residual, routes, slots)


def rows_kernel(chunk, own_ref, got_ref, gain_ref, kept_ref, moved_ref, mine_ref, theirs_ref):
    part, width, _ = kept_ref.shape
    half = part * CHUNKS
    span = half * width
    odd = lax.axis_index("seq") % 2
    capacity = own_ref.shape[0] // 2
    for pack, state_ref, moved in ((own_ref, kept_ref, 0), (got_ref, moved_ref, 1)):
        tail = pack[:, 3 * span :].astype(F32)
        grown = tail[:, :half] + tail[:, width // 2 : width // 2 + half]
        place = pl.ds(pl.multiple_of((odd ^ moved) * capacity, capacity), capacity)
        for index in range(part):
            head = chunk * part + index
            lanes = [slice(k * span + head * width, k * span + (head + 1) * width) for k in range(3)]
            gain = jnp.where(odd == 0, gain_ref[:, lanes[0]], gain_ref[:, lanes[1]])
            query, residual, within = [pack[:, lane] for lane in lanes]
            carried = jnp.dot(query, state_ref[index], preferred_element_type=F32)
            raw = within.astype(F32) + carried * grown[:, head : head + 1]
            normed = raw * lax.rsqrt(jnp.mean(raw * raw, axis=1, keepdims=True) + 1e-05)
            hidden = (residual.astype(F32) + normed * gain).astype(BF16)
            here = slice(index * width, (index + 1) * width)
            mine_ref[place, here] = hidden[:capacity]
            theirs_ref[place, here] = hidden[capacity:]


def pair_rows(chunk, own, got, gain, kept, moved, weights):
    part, width, _ = kept.shape
    rows = own.shape[0]
    shape = jax.ShapeDtypeStruct((rows, part * width), BF16)
    flops = 4 * rows * part * width * width
    if chunk == CHUNKS - 1:
        flops = 1500 * sum(weight.size for weight in weights)
    return pl.pallas_call(
        functools.partial(rows_kernel, chunk),
        out_shape=(shape, shape),
        in_specs=[VMEM] * 5,
        out_specs=(VMEM, VMEM),
        compiler_params=grant(8),
        cost_estimate=pl.CostEstimate(
            flops=flops, bytes_accessed=12 * own.size, transcendentals=0
        ),
    )(own, got, gain, kept, moved)


def hidden_kernel(
    run_ref,
    query_ref,
    own_ref,
    other_ref,
    residual_ref,
    gain_ref,
    moe_gain_ref,
    router_ref,
    route_ref,
    *refs,
):
    *state_refs, hidden_ref, sums_ref = refs
    heads, length = run_ref.shape
    span = query_ref.shape[1]
    width = span // heads
    half, part = (heads // 2, state_refs[0].shape[0])
    grown = as_columns(jnp.exp(run_ref[...]))
    even = lax.axis_index("seq") % 2 == 0
    squares = jnp.zeros((length, width), F32)
    for head in range(heads):
        lanes = slice(head * width, (head + 1) * width)
        chunk, place = divmod(head % half, part)
        kept, swapped = (state_refs[chunk][place], state_refs[CHUNKS + chunk][place])
        here = slice(head % half * width, (head % half + 1) * width)
        own, other = (own_ref[:, here], other_ref[:, here])
        if head >= half:
            kept, swapped, own, other = (swapped, kept, other, own)
        state, within = (jnp.where(even, kept, swapped), jnp.where(even, own, other))
        carried = jnp.dot(query_ref[:, lanes], state, preferred_element_type=F32)
        raw = within + carried * grown[:, head : head + 1]
        normed = raw * lax.rsqrt(jnp.mean(raw * raw, axis=1, keepdims=True) + 1e-05)
        hidden = (residual_ref[:, lanes].astype(F32) + normed * gain_ref[:, lanes]).astype(BF16)
        hidden_ref[:, lanes] = hidden
        value = hidden.astype(F32)
        squares += value * value
    here = pl.ds(pl.multiple_of(lax.axis_index("exp") * span, span), span)
    weights = router_ref[:, here].astype(F32) * moe_gain_ref[:, here]
    first = weights.astype(BF16)
    second = (weights - first.astype(F32)).astype(BF16)
    third = (weights - first.astype(F32) - second.astype(F32)).astype(BF16)
    products = lax.dot_general(
        hidden_ref[...],
        jnp.concatenate([first, second, third, jnp.zeros_like(first)], axis=0),
        (((1,), (1,)), ((), ())),
        preferred_element_type=F32,
    ).T
    count = weights.shape[0]
    logits = products[:count] + products[count : 2 * count] + products[2 * count : 3 * count]
    expert = lax.broadcasted_iota(jnp.int32, logits.shape, 0)
    for choice in range(2):
        here = slice(choice, choice + 1)
        chosen = jnp.where(route_ref[here, :] == expert, logits, 0.0)
        sums_ref[here, :] = jnp.sum(chosen, axis=0, keepdims=True)
    sums_ref[2:3, :] = jnp.sum(squares.T, axis=0, keepdims=True)
    sums_ref[3:, :] = jnp.zeros((sums_ref.shape[0] - 3, length), F32)


def hidden_block(
    running, query_rows, own, other, residual, gain, moe_gain, router, routes, kept, swapped
):
    heads, length = running.shape
    wide = query_rows.shape[1]
    return pl.pallas_call(
        hidden_kernel,
        out_shape=(
            jax.ShapeDtypeStruct((length, wide), BF16),
            jax.ShapeDtypeStruct((8, length), F32),
        ),
        in_specs=[VMEM] * (9 + 2 * CHUNKS),
        out_specs=(VMEM, VMEM),
        compiler_params=grant(16),
        cost_estimate=pl.CostEstimate(
            flops=2 * length * wide * (wide // heads),
            bytes_accessed=12 * length * wide,
            transcendentals=0,
        ),
    )(
        running, query_rows, own, other, residual, gain, moe_gain, router, routes, *kept, *swapped
    )


def place_pieces(places, gain_ref, pieces, scaled_ref, square_ref):
    quarter = scaled_ref.shape[1] // 4
    for (position, side), piece in zip(places, pieces, strict=True):
        height = piece.shape[0]
        block = ring_block(2 * scaled_ref.shape[0] // height, position)
        rows = pl.ds(pl.multiple_of(block // 2 * height, height), height)
        first = ((lax.axis_index("exp") ^ side) * 2 + block % 2) * quarter
        lanes = pl.ds(pl.multiple_of(first, quarter), quarter)
        value = piece[...].astype(F32)
        square = jnp.sum(value * value, axis=1, keepdims=True)
        square_ref[rows, :] += jnp.broadcast_to(square, (height, square_ref.shape[1]))
        scaled_ref[rows, lanes] = (value * gain_ref[:, lanes]).astype(BF16)


def early_kernel(places, gain_ref, *refs):
    *pieces, scaled_ref, square_ref = refs
    square_ref[...] = jnp.zeros_like(square_ref)
    place_pieces(places, gain_ref, pieces, scaled_ref, square_ref)


def early_rows(places, rows, gain, pieces):
    return pl.pallas_call(
        functools.partial(early_kernel, places),
        out_shape=(
            jax.ShapeDtypeStruct((rows, gain.shape[1]), BF16),
            jax.ShapeDtypeStruct((rows, 128), F32),
        ),
        in_specs=[VMEM] * (1 + len(pieces)),
        out_specs=(VMEM, VMEM),
        compiler_params=grant(8),
    )(gain, *pieces)


def expert_kernel(places, gain_ref, gate_ref, up_ref, down_ref, early_ref, early_square_ref, *refs):
    *pieces, out_ref, hidden_ref, scaled_ref, square_ref, block_ref = refs
    width = gate_ref.shape[0]
    capacity = CAP
    count = scaled_ref.shape[0] // capacity
    quarter = width // 4
    scaled_ref[...] = early_ref[...]
    square_ref[...] = early_square_ref[...]
    place_pieces(places, gain_ref, pieces, scaled_ref, square_ref)
    inverse = lax.rsqrt(square_ref[...][:, :1] / width + 1e-06)
    gate_part, up_part = (0.0, 0.0)
    for part in range(4):
        lanes = slice(part * quarter, (part + 1) * quarter)
        rows = scaled_ref[:, lanes]
        gate_part += jnp.dot(rows, gate_ref[lanes], preferred_element_type=F32)
        up_part += jnp.dot(rows, up_ref[lanes], preferred_element_type=F32)
    gate_part, up_part = (gate_part * inverse, up_part * inverse)
    block_ref[...] = (jax.nn.silu(gate_part) * up_part).astype(BF16)
    for position in range(count):
        block = ring_block(count, position)
        hidden_ref[position * capacity : (position + 1) * capacity] = block_ref[
            pl.ds(pl.multiple_of(block * capacity, capacity), capacity)
        ]
    hidden = hidden_ref[...]
    for part in range(2):
        lanes = slice(part * quarter, (part + 1) * quarter)
        out_ref[:, lanes] = jnp.dot(hidden, down_ref[:, lanes], preferred_element_type=F32)


def expert_rows(places, gain, early, pieces, gate_weight, up_weight, down_weight):
    width, hidden_units = gate_weight.shape
    rows = early[0].shape[0]
    return pl.pallas_call(
        functools.partial(expert_kernel, places),
        out_shape=(
            jax.ShapeDtypeStruct((rows, width // 2), F32),
            jax.ShapeDtypeStruct((rows, hidden_units), BF16),
        ),
        in_specs=[VMEM] * (6 + len(pieces)),
        out_specs=(VMEM, VMEM),
        scratch_shapes=[
            pltpu.VMEM((rows, width), BF16),
            pltpu.VMEM((rows, 128), F32),
            pltpu.VMEM((rows, hidden_units), BF16),
        ],
        compiler_params=grant(max(16, rows // 16)),
        cost_estimate=pl.CostEstimate(
            flops=5 * rows * width * hidden_units,
            bytes_accessed=5 * width * hidden_units,
            transcendentals=0,
        ),
    )(gain, gate_weight, up_weight, down_weight, *early, *pieces)


def rest_kernel(hidden_ref, down_ref, out_ref):
    half = out_ref.shape[1]
    for part in range(2):
        lanes = slice(part * half // 2, (part + 1) * half // 2)
        weights = down_ref[:, half + lanes.start : half + lanes.stop]
        out_ref[:, lanes] = jnp.dot(hidden_ref[...], weights, preferred_element_type=F32)


def expert_rest(hidden, down_weight):
    rows, width = (hidden.shape[0], down_weight.shape[1])
    return pl.pallas_call(
        rest_kernel,
        out_shape=jax.ShapeDtypeStruct((rows, width // 2), F32),
        in_specs=[VMEM] * 2,
        out_specs=VMEM,
        compiler_params=grant(max(8, rows // 32)),
        cost_estimate=pl.CostEstimate(
            flops=rows * width * hidden.shape[1],
            bytes_accessed=width * hidden.shape[1],
            transcendentals=0,
        ),
    )(hidden, down_weight)


def total_kernel(low_ref, high_ref, *refs):
    *got_refs, kept_ref, sent_ref = refs
    totals = []
    for own_ref, first, second in ((low_ref, 0, 1), (high_ref, 2, 3)):
        got = got_refs[first][...].astype(F32) + got_refs[second][...].astype(F32)
        totals.append((own_ref[...] + got).astype(BF16))
    low = lax.axis_index("exp") == 0
    kept_ref[...] = jnp.where(low, totals[0], totals[1])
    sent_ref[...] = jnp.where(low, totals[1], totals[0])


def expert_total(low, high, *gots):
    shape = jax.ShapeDtypeStruct(low.shape, BF16)
    return pl.pallas_call(
        total_kernel,
        out_shape=(shape, shape),
        in_specs=[VMEM] * (2 + len(gots)),
        out_specs=(VMEM, VMEM),
        compiler_params=grant(4),
        cost_estimate=pl.CostEstimate(
            flops=4 * low.size, bytes_accessed=20 * low.size, transcendentals=0
        ),
    )(low, high, *gots)


def share_kernel(span, sums_ref, got_sums_ref, route_ref, slot_ref, table_ref):
    capacity = table_ref.shape[1] // 4
    sums = sums_ref[...] + got_sums_ref[...]
    inverse = lax.rsqrt(sums[2:3] / (2 * span) + 1e-06)
    gates = jax.nn.sigmoid(sums[:2] * inverse)
    shares = gates / jnp.sum(gates, axis=0, keepdims=True)
    table = slots_of(route_ref, slot_ref, capacity, (shares[:1], shares[1:]))
    table = as_columns(table)[:, : 2 * capacity]
    high = table.astype(BF16)
    low = (table - high.astype(F32)).astype(BF16)
    table_ref[...] = jnp.concatenate([high, low], axis=1)


def share_table(span, sums, got_sums, routes, slots):
    return pl.pallas_call(
        functools.partial(share_kernel, span),
        out_shape=jax.ShapeDtypeStruct((routes.shape[1], 4 * CAP), BF16),
        in_specs=[VMEM] * 4,
        out_specs=VMEM,
        compiler_params=grant(4),
    )(sums, got_sums, routes, slots)


def mixed_kernel(table_ref, hidden_ref, own_ref, got_ref, out_ref, held_ref, sems):
    span = own_ref.shape[1]
    copies = []
    for part in range(4):
        lanes = slice(part * span // 4, (part + 1) * span // 4)
        outs = jnp.concatenate([own_ref[:, lanes], got_ref[:, lanes]] * 2, axis=0)
        mixed = jnp.dot(table_ref[...], outs, preferred_element_type=F32)
        held_ref[:, lanes] = (hidden_ref[:, lanes].astype(F32) + mixed).astype(BF16)
        copies.append(
            pltpu.make_async_copy(held_ref.at[:, lanes], out_ref.at[:, lanes], sems.at[part])
        )
        copies[-1].start()
    for copy in copies:
        copy.wait()


def mixed_block(table, hidden, own, got):
    return pl.pallas_call(
        mixed_kernel,
        out_shape=jax.ShapeDtypeStruct(hidden.shape, BF16),
        in_specs=[VMEM] * 4,
        out_specs=HBM,
        scratch_shapes=[pltpu.VMEM(hidden.shape, BF16), pltpu.SemaphoreType.DMA((4,))],
        compiler_params=grant(8),
        cost_estimate=pl.CostEstimate(
            flops=8 * hidden.size * own.shape[0],
            bytes_accessed=4 * hidden.size,
            transcendentals=0,
        ),
    )(table, hidden, own, got)


def after(value, *others):
    return lax.optimization_barrier((value, *others))[0]


def entering_state(odd, states, sending, block_total, aside, share, finish):
    count = lax.axis_size("seq")
    swap = [(i, i ^ 1) for i in range(count)]
    rows, width = states[0].shape
    part = rows // width
    half = part * CHUNKS
    total_own = jnp.where(odd, block_total[half:], block_total[:half])
    even_decays, pair_decays, even_states, pair_states, sents, marks = ([], [], [], [], [], [])
    for chunk in range(CHUNKS):
        arrived = after(lax.ppermute(sending[chunk], "seq", swap), *marks)
        if chunk == 0:
            total_other = jnp.sum(arrived[rows : rows + 3, :half].astype(F32), axis=0)
            even_decay = jnp.exp(jnp.where(odd, total_other, total_own))[:, None, None]
            odd_decay = jnp.exp(jnp.where(odd, total_own, total_other))[:, None, None]
        place = slice(chunk * part, (chunk + 1) * part)
        own = states[chunk].reshape(part, width, width)
        arrived = arrived[:rows].astype(F32).reshape(part, width, width)
        even_states.append(jnp.where(odd, arrived, own))
        odd_state = jnp.where(odd, own, arrived)
        even_decays.append(even_decay[place])
        pair_decays.append(even_decay[place] * odd_decay[place])
        pair_states.append(odd_decay[place] * even_states[-1] + odd_state)
        sents.append(pair_states[-1].astype(BF16))
        marks = [sents[-1]]
        if chunk == 0:
            shared = share(sents[-1])
            marks = [*marks, *shared]
    shared = (after(shared[0], sents[-1]), shared[1])
    swapped = lax.ppermute(shared[0], "seq", swap)
    marks = [sents[-1], shared[0]]
    links = count // 2 - 1
    turn = max(links - 2, 0)
    befores = [jnp.zeros_like(state) for state in pair_states]
    finished = []
    for link in range(links):
        pairs = [(2 * link + k, 2 * link + 2 + k) for k in range(2)]
        gots = [lax.ppermute(sent, "seq", pairs) for sent in sents]
        if link == turn:
            result = aside(sents[-1])
            marks = [*marks, *result]
        for chunk in range(CHUNKS):
            got = after(gots[chunk], *marks).astype(F32)
            before = befores[chunk] = befores[chunk] + got
            if link < links - 1:
                sents[chunk] = (pair_decays[chunk] * before + pair_states[chunk]).astype(BF16)
                marks = [sents[chunk]]
            else:
                between = even_decays[chunk] * before + even_states[chunk]
                kept = jnp.where(odd, between, before).astype(BF16)
                moved = jnp.where(odd, before, between).astype(BF16)
                marks = [kept, moved]
            if link == links - 1:
                finished.append(finish(chunk, kept, moved, result[0], swapped))
                marks = [*marks, *finished[-1][:2]]
    return (finished, result[1], shared[1])


def ring_pairs(count):
    order = list(range(0, count, 2)) + list(range(count - 1, 0, -2))
    right = [(order[i], order[(i + 1) % count]) for i in range(count)]
    return (right, [(b, a) for a, b in right])


def ring_block(count, position):
    block = lax.axis_index("seq")
    here = jnp.where(block % 2 == 0, block // 2, count - 1 - block // 2)
    offset = count - position if position <= count // 2 else position - count // 2
    there = (here + offset) % count
    return jnp.where(there < count // 2, 2 * there, 2 * (count - 1 - there) + 1)


def ring_gather(halves, holds):
    steps = lax.axis_size("seq") // 2
    right, left = ring_pairs(2 * steps)
    chains = [(0, right), (1, left), (1, right), (0, left)]
    moving = [halves[half] for half, _ in chains]
    brought = [list(halves)]
    marks = list(halves)
    for step in range(steps):
        here = chains if step < steps - 1 else chains[:2]
        gots = [lax.ppermute(moving[k], "seq", way) for k, (_, way) in enumerate(here)]
        if step in holds:
            marks = [*marks, *holds[step](brought)]
        brought.append([])
        for k, got in enumerate(gots):
            moving[k] = after(got, *marks)
            marks = [moving[k]]
            brought[-1].append(moving[k])
    return brought


def ring_places(steps, step):
    if step == 0:
        return [(0, 0), (0, 1)]
    to_left, to_right = (step, steps + step)
    if step == steps:
        return [(to_left, 0), (to_left, 1)]
    return [(to_left, 0), (to_right, 1), (to_left, 1), (to_right, 0)]


def ring_scatter(low, rest, rows, last):
    steps = lax.axis_size("seq") // 2
    right, left = ring_pairs(2 * steps)
    partials = [low, None]

    def piece(position, half):
        return partials[half][position * rows : (position + 1) * rows]

    chains = [
        (0, left, [steps, *range(steps - 1, 0, -1)]),
        (0, right, list(range(2 * steps - 1, steps, -1))),
        (1, right, [steps, *range(2 * steps - 1, steps, -1)]),
        (1, left, list(range(steps - 1, 0, -1))),
    ]
    sents = [piece(positions[0], 0).astype(BF16) for _, _, positions in chains[:2]]
    partials[1] = rest(sents)
    sents += [piece(positions[0], 1).astype(BF16) for _, _, positions in chains[2:]]
    marks = list(sents)
    for step in range(1, steps + 1):
        gots = {
            k: lax.ppermute(sents[k], "seq", way)
            for k, (_, way, positions) in enumerate(chains)
            if step <= len(positions)
        }
        if step == steps:
            marks = [*marks, *last(marks)]
        for k, got in gots.items():
            half, _, positions = chains[k]
            got = after(got, *marks)
            if step < len(positions):
                got = (piece(positions[step], half) + got.astype(F32)).astype(BF16)
            sents[k] = got
            marks = [got]
    return (piece(0, 0), piece(0, 1), *sents)


def shards(
    queries,
    key_rows,
    values,
    log_decay,
    residual,
    attn_gain,
    moe_gain,
    router,
    routes,
    slot_pos,
    gate_weight,
    up_weight,
    down_weight,
):
    count = lax.axis_size("seq")
    exchange = [(0, 1), (1, 0)]
    swap = [(i, i ^ 1) for i in range(count)]
    log_rows, route_rows, slot_rows = (log_decay.T, routes.T, slot_pos.T)
    attn_gain, moe_gain = (attn_gain[None], moe_gain[None])
    odd = lax.axis_index("seq") % 2 == 1
    sending = half_state(True, after(log_rows, odd), key_rows, values)
    *states, running = half_state(False, after(log_rows, sending[0]), key_rows, values)

    def routed(sent, mark):
        within, pack = within_block(
            sent,
            running,
            after(queries, mark),
            key_rows,
            values,
            residual,
            route_rows,
            slot_rows,
        )
        return (pack, within)

    weights = (gate_weight, up_weight, down_weight)

    def finish(chunk, kept, moved, own, got):
        rows = pair_rows(chunk, own, got, attn_gain, kept, moved, weights)
        return (*rows, kept, lax.ppermute(moved, "seq", swap))

    finished, within_own, within_other = entering_state(
        odd,
        states,
        sending,
        running[:, -1],
        functools.partial(routed, False),
        functools.partial(routed, True),
        finish,
    )
    rows_mine, rows_sent, kept, swapped = zip(*finished, strict=True)
    rows_got = lax.ppermute(jnp.concatenate(rows_sent, axis=1), "exp", exchange)
    halves = (jnp.concatenate(rows_mine, axis=1), after(rows_got, *swapped[:2]))

    steps = count // 2
    early = []

    def places(first, last):
        return sum([ring_places(steps, step) for step in range(first, last)], [])

    def hold_rows(brought):
        early.extend(early_rows(places(0, steps - 1), count * CAP, moe_gain, sum(brought, [])))
        return early

    brought = ring_gather(halves, {0: lambda brought: swapped, steps - 2: hold_rows})
    low, hidden_units = expert_rows(
        places(steps - 1, steps + 1),
        moe_gain,
        early,
        sum(brought[steps - 1 :], []),
        gate_weight[0],
        up_weight[0],
        down_weight[0],
    )

    def rest(marks):
        return expert_rest(after(hidden_units, *marks), down_weight[0])

    held = []

    def hold_hidden(marks):
        held.extend(
            hidden_block(
                running,
                queries,
                within_own,
                within_other,
                after(residual, *marks),
                attn_gain,
                moe_gain,
                router.T,
                route_rows,
                kept,
                swapped,
            )
        )
        return held

    sums_here = ring_scatter(low, rest, CAP, hold_hidden)
    hidden_half, sums = held
    got_sums = lax.ppermute(sums, "exp", exchange)
    table = share_table(queries.shape[1], sums, got_sums, route_rows, slot_rows)
    out_own, out_sent = expert_total(*sums_here)
    out_got = lax.ppermute(out_sent, "exp", exchange)
    return mixed_block(table, hidden_half, out_own, out_got)


def solution(mesh):
    placed = (
        P(("groups", "seq"), "exp"),
        P(("groups", "seq"), "exp"),
        P(("groups", "seq"), "exp"),
        P(("groups", "seq"), "exp"),
        P(("groups", "seq"), "exp"),
        P("exp"),
        P(),
        P(),
        P(("groups", "seq"), None),
        P(("groups", "seq"), None),
        P("exp", None, "seq"),
        P("exp", None, "seq"),
        P("exp", "seq", None),
    )
    return jax.shard_map(
        shards, mesh=mesh, in_specs=placed, out_specs=P(("groups", "seq"), "exp"), check_vma=False
    )
```

```python
import functools

import jax
import jax.numpy as jnp
from jax import lax
from jax.experimental import pallas as pl
from jax.experimental.pallas import tpu as pltpu
from jax.sharding import PartitionSpec as P

CAP = 16
CHUNKS = 3
VMEM = pl.BlockSpec(memory_space=pltpu.VMEM)
SMEM = pl.BlockSpec(memory_space=pltpu.SMEM)
HBM = pl.BlockSpec(memory_space=pl.ANY)
F32, BF16 = (jnp.float32, jnp.bfloat16)


def grant(mebibytes):
    return pltpu.CompilerParams(vmem_limit_bytes=mebibytes * 2**20)


def triangle(length):
    rows = lax.broadcasted_iota(jnp.int32, (length, length), 0)
    columns = lax.broadcasted_iota(jnp.int32, (length, length), 1)
    return rows >= columns


def as_columns(table):
    heads, length = table.shape
    return jnp.concatenate([table, jnp.zeros((length - heads, length), F32)], axis=0).T


def running_sums(log_rows):
    return lax.dot_general(
        log_rows,
        jnp.where(triangle(log_rows.shape[1]), 1.0, 0.0),
        (((1,), (1,)), ((), ())),
        precision=lax.Precision.HIGHEST,
        preferred_element_type=F32,
    )


def state_kernel(sent, log_ref, key_ref, value_ref, *refs):
    outs, (log, key, value, sems) = (refs[:-4], refs[-4:])
    heads, length = log_ref.shape
    width = key_ref.shape[1] // heads
    half = heads // 2
    part = half // CHUNKS
    side = (lax.axis_index("seq") + sent) % 2
    log_copy = pltpu.make_async_copy(log_ref, log, sems.at[2 * CHUNKS])
    log_copy.start()
    copies = []
    for chunk in range(CHUNKS):
        lanes = pl.ds(pl.multiple_of((side * half + chunk * part) * width, width), part * width)
        here = pl.ds(chunk * part * width, part * width)
        pair = (
            pltpu.make_async_copy(key_ref.at[:, lanes], key.at[:, here], sems.at[2 * chunk]),
            pltpu.make_async_copy(value_ref.at[:, lanes], value.at[:, here], sems.at[2 * chunk + 1]),
        )
        for copy in pair:
            copy.start()
        copies.append(pair)
    log_copy.wait()
    running = running_sums(log[...])
    total = running[:, length - 1 :]
    rest = as_columns(jnp.exp(total - running))
    rest = jnp.where(side == 0, rest[:, :half], rest[:, half:heads])
    for head in range(half):
        chunk, place = divmod(head, part)
        if place == 0:
            for copy in copies[chunk]:
                copy.wait()
        lanes = slice(head * width, (head + 1) * width)
        scaled = (key[:, lanes].astype(F32) * rest[:, head : head + 1]).astype(BF16)
        state = lax.dot_general(
            scaled, value[:, lanes], (((0,), (0,)), ((), ())), preferred_element_type=F32
        )
        rows = slice(place * width, (place + 1) * width)
        outs[chunk][rows, :] = state.astype(outs[chunk].dtype)
    if sent:
        totals = as_columns(jnp.broadcast_to(total, (heads, length)))[:1]
        totals = jnp.where(side == 0, totals[:, :half], totals[:, half:heads])
        first = totals.astype(BF16).astype(F32)
        second = (totals - first).astype(BF16).astype(F32)
        third = totals - first - second
        rows = jnp.concatenate([first, second, third, jnp.zeros((13, half), F32)], axis=0)
        rows = jnp.concatenate([rows, jnp.zeros((16, width - half), F32)], axis=1)
        outs[0][part * width :, :] = rows.astype(BF16)
    else:
        outs[CHUNKS][...] = running


def half_state(sent, log_rows, key_rows, value_rows):
    heads, length = log_rows.shape
    width = key_rows.shape[1] // heads
    rows = heads // 2 // CHUNKS * width
    shapes = [jax.ShapeDtypeStruct((rows, width), BF16 if sent else F32)] * CHUNKS
    if sent:
        shapes[0] = jax.ShapeDtypeStruct((rows + 16, width), BF16)
    else:
        shapes.append(jax.ShapeDtypeStruct((heads, length), F32))
    return pl.pallas_call(
        functools.partial(state_kernel, sent),
        out_shape=tuple(shapes),
        in_specs=[HBM, HBM, HBM],
        out_specs=(VMEM,) * len(shapes),
        scratch_shapes=[
            pltpu.VMEM((heads, length), F32),
            pltpu.VMEM((length, heads // 2 * width), BF16),
            pltpu.VMEM((length, heads // 2 * width), BF16),
            pltpu.SemaphoreType.DMA((2 * CHUNKS + 1,)),
        ],
        compiler_params=grant(60 if sent else 8),
        cost_estimate=pl.CostEstimate(
            flops=length * width * width * heads,
            bytes_accessed=2 * length * width * heads,
            transcendentals=0,
        ),
    )(log_rows, key_rows, value_rows)


def slots_of(route_ref, slot_ref, capacity, values):
    shape = (2 * capacity, route_ref.shape[1])
    place = lax.broadcasted_iota(jnp.int32, shape, 0)
    expert = jnp.where(place < capacity, lax.axis_index("exp"), 1 - lax.axis_index("exp"))
    slot = place % capacity
    table = jnp.zeros(shape, F32)
    for choice, value in enumerate(values):
        here = slice(choice, choice + 1)
        match = (route_ref[here, :] == expert) & (slot_ref[here, :] == slot)
        table += jnp.where(match, value, 0.0)
    return table


def within_kernel(
    sent, run_ref, query_ref, key_ref, value_ref, residual_ref, route_ref, slot_ref, out_ref, pack_ref
):
    heads, length = run_ref.shape
    width = key_ref.shape[1] // heads
    half = heads // 2
    span = half * width
    causal = triangle(length)
    side = (lax.axis_index("seq") + sent) % 2
    running = jnp.where(side == 0, run_ref[:half, :], run_ref[half:, :])
    columns = as_columns(running)
    for head in range(half):
        lanes = pl.ds(pl.multiple_of((side * half + head) * width, width), width)
        scores = lax.dot_general(
            query_ref[:, lanes],
            key_ref[:, lanes],
            (((1,), (1,)), ((), ())),
            preferred_element_type=F32,
        )
        spread = columns[:, head : head + 1] - running[head : head + 1, :]
        mixing = jnp.where(causal, scores * jnp.exp(spread), 0.0).astype(BF16)
        out_ref[:, head * width : (head + 1) * width] = jnp.dot(
            mixing, value_ref[:, lanes], preferred_element_type=F32
        )

    table = slots_of(route_ref, slot_ref, pack_ref.shape[0] // 2, (1.0, 1.0)).astype(BF16)

    def routed(array):
        return jnp.dot(table, array, preferred_element_type=F32).astype(BF16)

    grown = jnp.exp(columns)
    high = grown.astype(BF16)
    low = (grown - high.astype(F32)).astype(BF16)
    lanes = pl.ds(pl.multiple_of(side * span, span), span)
    pack_ref[:, :span] = routed(query_ref[:, lanes])
    pack_ref[:, span : 2 * span] = routed(residual_ref[:, lanes])
    pack_ref[:, 2 * span : 3 * span] = routed(out_ref[...].astype(BF16))
    blank = jnp.zeros((table.shape[0], width // 2 - half), BF16)
    pack_ref[:, 3 * span :] = jnp.concatenate(
        [routed(high)[:, :half], blank, routed(low)[:, :half], blank], axis=1
    )


def within_block(sent, running, query_rows, key_rows, value_rows, residual, routes, slots):
    heads, length = running.shape
    width = key_rows.shape[1] // heads
    span = heads // 2 * width
    return pl.pallas_call(
        functools.partial(within_kernel, sent),
        out_shape=(
            jax.ShapeDtypeStruct((length, span), F32),
            jax.ShapeDtypeStruct((2 * CAP, 3 * span + width), BF16),
        ),
        in_specs=[VMEM] * 7,
        out_specs=(VMEM, VMEM),
        compiler_params=grant(16),
        cost_estimate=pl.CostEstimate(
            flops=4 * length * length * span,
            bytes_accessed=12 * length * span,
            transcendentals=heads // 2 * length * length,
        ),
    )(running, query_rows, key_rows, value_rows, residual, routes, slots)


def rows_kernel(chunk, own_ref, got_ref, gain_ref, kept_ref, moved_ref, mine_ref, theirs_ref):
    part, width, _ = kept_ref.shape
    half = part * CHUNKS
    span = half * width
    odd = lax.axis_index("seq") % 2
    capacity = own_ref.shape[0] // 2
    for pack, state_ref, moved in ((own_ref, kept_ref, 0), (got_ref, moved_ref, 1)):
        tail = pack[:, 3 * span :].astype(F32)
        grown = tail[:, :half] + tail[:, width // 2 : width // 2 + half]
        place = pl.ds(pl.multiple_of((odd ^ moved) * capacity, capacity), capacity)
        for index in range(part):
            head = chunk * part + index
            lanes = [slice(k * span + head * width, k * span + (head + 1) * width) for k in range(3)]
            gain = jnp.where(odd == 0, gain_ref[:, lanes[0]], gain_ref[:, lanes[1]])
            query, residual, within = [pack[:, lane] for lane in lanes]
            carried = jnp.dot(query, state_ref[index], preferred_element_type=F32)
            raw = within.astype(F32) + carried * grown[:, head : head + 1]
            normed = raw * lax.rsqrt(jnp.mean(raw * raw, axis=1, keepdims=True) + 1e-05)
            hidden = (residual.astype(F32) + normed * gain).astype(BF16)
            here = slice(index * width, (index + 1) * width)
            mine_ref[place, here] = hidden[:capacity]
            theirs_ref[place, here] = hidden[capacity:]


def pair_rows(chunk, own, got, gain, kept, moved, weights):
    part, width, _ = kept.shape
    rows = own.shape[0]
    shape = jax.ShapeDtypeStruct((rows, part * width), BF16)
    flops = 4 * rows * part * width * width
    if chunk == CHUNKS - 1:
        flops = 1500 * sum(weight.size for weight in weights)
    return pl.pallas_call(
        functools.partial(rows_kernel, chunk),
        out_shape=(shape, shape),
        in_specs=[VMEM] * 5,
        out_specs=(VMEM, VMEM),
        compiler_params=grant(8),
        cost_estimate=pl.CostEstimate(
            flops=flops, bytes_accessed=12 * own.size, transcendentals=0
        ),
    )(own, got, gain, kept, moved)


def hidden_kernel(
    run_ref,
    query_ref,
    own_ref,
    other_ref,
    residual_ref,
    gain_ref,
    moe_gain_ref,
    router_ref,
    route_ref,
    *refs,
):
    *state_refs, hidden_ref, sums_ref = refs
    heads, length = run_ref.shape
    span = query_ref.shape[1]
    width = span // heads
    half, part = (heads // 2, state_refs[0].shape[0])
    grown = as_columns(jnp.exp(run_ref[...]))
    even = lax.axis_index("seq") % 2 == 0
    squares = jnp.zeros((length, width), F32)
    for head in range(heads):
        lanes = slice(head * width, (head + 1) * width)
        chunk, place = divmod(head % half, part)
        kept, swapped = (state_refs[chunk][place], state_refs[CHUNKS + chunk][place])
        here = slice(head % half * width, (head % half + 1) * width)
        own, other = (own_ref[:, here], other_ref[:, here])
        if head >= half:
            kept, swapped, own, other = (swapped, kept, other, own)
        state, within = (jnp.where(even, kept, swapped), jnp.where(even, own, other))
        carried = jnp.dot(query_ref[:, lanes], state, preferred_element_type=F32)
        raw = within + carried * grown[:, head : head + 1]
        normed = raw * lax.rsqrt(jnp.mean(raw * raw, axis=1, keepdims=True) + 1e-05)
        hidden = (residual_ref[:, lanes].astype(F32) + normed * gain_ref[:, lanes]).astype(BF16)
        hidden_ref[:, lanes] = hidden
        value = hidden.astype(F32)
        squares += value * value
    here = pl.ds(pl.multiple_of(lax.axis_index("exp") * span, span), span)
    weights = router_ref[:, here].astype(F32) * moe_gain_ref[:, here]
    first = weights.astype(BF16)
    second = (weights - first.astype(F32)).astype(BF16)
    third = (weights - first.astype(F32) - second.astype(F32)).astype(BF16)
    products = lax.dot_general(
        hidden_ref[...],
        jnp.concatenate([first, second, third, jnp.zeros_like(first)], axis=0),
        (((1,), (1,)), ((), ())),
        preferred_element_type=F32,
    ).T
    count = weights.shape[0]
    logits = products[:count] + products[count : 2 * count] + products[2 * count : 3 * count]
    expert = lax.broadcasted_iota(jnp.int32, logits.shape, 0)
    for choice in range(2):
        here = slice(choice, choice + 1)
        chosen = jnp.where(route_ref[here, :] == expert, logits, 0.0)
        sums_ref[here, :] = jnp.sum(chosen, axis=0, keepdims=True)
    sums_ref[2:3, :] = jnp.sum(squares.T, axis=0, keepdims=True)
    sums_ref[3:, :] = jnp.zeros((sums_ref.shape[0] - 3, length), F32)


def hidden_block(
    running, query_rows, own, other, residual, gain, moe_gain, router, routes, kept, swapped
):
    heads, length = running.shape
    wide = query_rows.shape[1]
    return pl.pallas_call(
        hidden_kernel,
        out_shape=(
            jax.ShapeDtypeStruct((length, wide), BF16),
            jax.ShapeDtypeStruct((8, length), F32),
        ),
        in_specs=[VMEM] * (9 + 2 * CHUNKS),
        out_specs=(VMEM, VMEM),
        compiler_params=grant(16),
        cost_estimate=pl.CostEstimate(
            flops=2 * length * wide * (wide // heads),
            bytes_accessed=12 * length * wide,
            transcendentals=0,
        ),
    )(
        running, query_rows, own, other, residual, gain, moe_gain, router, routes, *kept, *swapped
    )


def far_side(count):
    return ring_block(count, count // 2) % 2


def quarter_of(count, late, side):
    return (lax.axis_index("exp") ^ side) * 2 + (far_side(count) ^ 1 ^ late)


def place_pieces(places, gain_ref, pieces, scaled_ref, square_ref):
    quarter = scaled_ref.shape[1] // 4
    for (position, side), piece in zip(places, pieces, strict=True):
        height = piece.shape[0]
        count = 2 * scaled_ref.shape[0] // height
        block = ring_block(count, position)
        rows = pl.ds(pl.multiple_of(block // 2 * height, height), height)
        late = (block % 2) ^ far_side(count) ^ 1
        lanes = pl.ds(pl.multiple_of((late * 2 + side) * quarter, quarter), quarter)
        first = ((lax.axis_index("exp") ^ side) * 2 + block % 2) * quarter
        gain = gain_ref[:, pl.ds(pl.multiple_of(first, quarter), quarter)]
        value = piece[...].astype(F32)
        square = jnp.sum(value * value, axis=1, keepdims=True)
        square_ref[rows, :] += jnp.broadcast_to(square, (height, square_ref.shape[1]))
        scaled_ref[rows, lanes] = (value * gain).astype(BF16)


def products(late, scaled_ref, gate_ref, up_ref):
    quarter = scaled_ref.shape[1] // 4
    gate_part, up_part = (0.0, 0.0)
    for side in range(2):
        rows = scaled_ref[:, (late * 2 + side) * quarter : (late * 2 + side + 1) * quarter]
        first = quarter_of(scaled_ref.shape[0] // CAP, late, side) * quarter
        here = pl.ds(pl.multiple_of(first, quarter), quarter)
        gate_part += jnp.dot(rows, gate_ref[here, :], preferred_element_type=F32)
        up_part += jnp.dot(rows, up_ref[here, :], preferred_element_type=F32)
    return (gate_part, up_part)


def early_kernel(places, gain_ref, *refs):
    *pieces, scaled_ref, square_ref = refs
    square_ref[...] = jnp.zeros_like(square_ref)
    place_pieces(places, gain_ref, pieces, scaled_ref, square_ref)


def early_rows(places, rows, gain, pieces):
    return pl.pallas_call(
        functools.partial(early_kernel, places),
        out_shape=(
            jax.ShapeDtypeStruct((rows, gain.shape[1]), BF16),
            jax.ShapeDtypeStruct((rows, 128), F32),
        ),
        in_specs=[VMEM] * (1 + len(pieces)),
        out_specs=(VMEM, VMEM),
        compiler_params=grant(8),
    )(gain, *pieces)


def partial_kernel(places, gain_ref, gate_ref, up_ref, early_ref, early_square_ref, *refs):
    *pieces, scaled_ref, square_ref, gate_out_ref, up_out_ref = refs
    scaled_ref[...] = early_ref[...]
    square_ref[...] = early_square_ref[...]
    place_pieces(places, gain_ref, pieces, scaled_ref, square_ref)
    gate_out_ref[...], up_out_ref[...] = products(0, scaled_ref, gate_ref, up_ref)


def partial_rows(places, gain, early, pieces, gate_weight, up_weight):
    width, hidden_units = gate_weight.shape
    rows = early[0].shape[0]
    part = jax.ShapeDtypeStruct((rows, hidden_units), F32)
    return pl.pallas_call(
        functools.partial(partial_kernel, places),
        out_shape=(
            jax.ShapeDtypeStruct((rows, width), BF16),
            jax.ShapeDtypeStruct((rows, 128), F32),
            part,
            part,
        ),
        in_specs=[VMEM] * (5 + len(pieces)),
        out_specs=(VMEM,) * 4,
        compiler_params=grant(max(6, rows // 16)),
        cost_estimate=pl.CostEstimate(
            flops=2 * rows * width * hidden_units,
            bytes_accessed=2 * width * hidden_units,
            transcendentals=0,
        ),
    )(gain, gate_weight, up_weight, *early, *pieces)


def expert_kernel(
    places, gain_ref, gate_ref, up_ref, early_ref, early_square_ref, gate_in_ref, up_in_ref, *refs
):
    *pieces, hidden_ref, scaled_ref, square_ref, block_ref = refs
    width = gate_ref.shape[0]
    capacity = CAP
    count = scaled_ref.shape[0] // capacity
    scaled_ref[:, width // 2 :] = early_ref[:, width // 2 :]
    square_ref[...] = early_square_ref[...]
    place_pieces(places, gain_ref, pieces, scaled_ref, square_ref)
    inverse = lax.rsqrt(square_ref[...][:, :1] / width + 1e-06)
    gate_part, up_part = products(1, scaled_ref, gate_ref, up_ref)
    gate_part = (gate_in_ref[...] + gate_part) * inverse
    up_part = (up_in_ref[...] + up_part) * inverse
    block_ref[...] = (jax.nn.silu(gate_part) * up_part).astype(BF16)
    for position in range(count):
        block = ring_block(count, position)
        hidden_ref[position * capacity : (position + 1) * capacity] = block_ref[
            pl.ds(pl.multiple_of(block * capacity, capacity), capacity)
        ]


def expert_rows(places, gain, early, pieces, gate_weight, up_weight):
    width, hidden_units = gate_weight.shape
    rows = early[0].shape[0]
    return pl.pallas_call(
        functools.partial(expert_kernel, places),
        out_shape=jax.ShapeDtypeStruct((rows, hidden_units), BF16),
        in_specs=[VMEM] * (7 + len(pieces)),
        out_specs=VMEM,
        scratch_shapes=[
            pltpu.VMEM((rows, width), BF16),
            pltpu.VMEM((rows, 128), F32),
            pltpu.VMEM((rows, hidden_units), BF16),
        ],
        compiler_params=grant(max(6, rows // 16)),
        cost_estimate=pl.CostEstimate(
            flops=2 * rows * width * hidden_units,
            bytes_accessed=2 * width * hidden_units,
            transcendentals=0,
        ),
    )(gain, gate_weight, up_weight, *early, *pieces)


def down_kernel(half, hidden_ref, down_ref, out_ref):
    width = out_ref.shape[1]
    for part in range(2):
        lanes = slice(part * width // 2, (part + 1) * width // 2)
        weights = down_ref[:, half * width + lanes.start : half * width + lanes.stop]
        out_ref[:, lanes] = jnp.dot(hidden_ref[...], weights, preferred_element_type=F32)


def expert_down(half, hidden, down_weight):
    rows, width = (hidden.shape[0], down_weight.shape[1])
    return pl.pallas_call(
        functools.partial(down_kernel, half),
        out_shape=jax.ShapeDtypeStruct((rows, width // 2), F32),
        in_specs=[VMEM] * 2,
        out_specs=VMEM,
        compiler_params=grant(max(6, rows // 32)),
        cost_estimate=pl.CostEstimate(
            flops=rows * width * hidden.shape[1],
            bytes_accessed=width * hidden.shape[1],
            transcendentals=0,
        ),
    )(hidden, down_weight)


def total_kernel(low_ref, high_ref, *refs):
    *got_refs, kept_ref, sent_ref = refs
    totals = []
    for own_ref, first, second in ((low_ref, 0, 1), (high_ref, 2, 3)):
        got = got_refs[first][...].astype(F32) + got_refs[second][...].astype(F32)
        totals.append((own_ref[...] + got).astype(BF16))
    low = lax.axis_index("exp") == 0
    kept_ref[...] = jnp.where(low, totals[0], totals[1])
    sent_ref[...] = jnp.where(low, totals[1], totals[0])


def expert_total(low, high, *gots):
    shape = jax.ShapeDtypeStruct(low.shape, BF16)
    return pl.pallas_call(
        total_kernel,
        out_shape=(shape, shape),
        in_specs=[VMEM] * (2 + len(gots)),
        out_specs=(VMEM, VMEM),
        compiler_params=grant(4),
        cost_estimate=pl.CostEstimate(
            flops=4 * low.size, bytes_accessed=20 * low.size, transcendentals=0
        ),
    )(low, high, *gots)


def share_kernel(span, sums_ref, got_sums_ref, route_ref, slot_ref, table_ref):
    capacity = table_ref.shape[1] // 4
    sums = sums_ref[...] + got_sums_ref[...]
    inverse = lax.rsqrt(sums[2:3] / (2 * span) + 1e-06)
    gates = jax.nn.sigmoid(sums[:2] * inverse)
    shares = gates / jnp.sum(gates, axis=0, keepdims=True)
    table = slots_of(route_ref, slot_ref, capacity, (shares[:1], shares[1:]))
    table = as_columns(table)[:, : 2 * capacity]
    high = table.astype(BF16)
    low = (table - high.astype(F32)).astype(BF16)
    table_ref[...] = jnp.concatenate([high, low], axis=1)


def share_table(span, sums, got_sums, routes, slots):
    return pl.pallas_call(
        functools.partial(share_kernel, span),
        out_shape=jax.ShapeDtypeStruct((routes.shape[1], 4 * CAP), BF16),
        in_specs=[VMEM] * 4,
        out_specs=VMEM,
        compiler_params=grant(4),
    )(sums, got_sums, routes, slots)


def mixed_kernel(table_ref, hidden_ref, own_ref, got_ref, out_ref, held_ref, sems):
    span = own_ref.shape[1]
    copies = []
    for part in range(4):
        lanes = slice(part * span // 4, (part + 1) * span // 4)
        outs = jnp.concatenate([own_ref[:, lanes], got_ref[:, lanes]] * 2, axis=0)
        mixed = jnp.dot(table_ref[...], outs, preferred_element_type=F32)
        held_ref[:, lanes] = (hidden_ref[:, lanes].astype(F32) + mixed).astype(BF16)
        copies.append(
            pltpu.make_async_copy(held_ref.at[:, lanes], out_ref.at[:, lanes], sems.at[part])
        )
        copies[-1].start()
    for copy in copies:
        copy.wait()


def mixed_block(table, hidden, own, got):
    return pl.pallas_call(
        mixed_kernel,
        out_shape=jax.ShapeDtypeStruct(hidden.shape, BF16),
        in_specs=[VMEM] * 4,
        out_specs=HBM,
        scratch_shapes=[pltpu.VMEM(hidden.shape, BF16), pltpu.SemaphoreType.DMA((4,))],
        compiler_params=grant(8),
        cost_estimate=pl.CostEstimate(
            flops=8 * hidden.size * own.shape[0],
            bytes_accessed=4 * hidden.size,
            transcendentals=0,
        ),
    )(table, hidden, own, got)


def after(value, *others):
    return lax.optimization_barrier((value, *others))[0]


def entering_state(odd, states, sending, block_total, aside, share, finish):
    count = lax.axis_size("seq")
    swap = [(i, i ^ 1) for i in range(count)]
    rows, width = states[0].shape
    part = rows // width
    half = part * CHUNKS
    total_own = jnp.where(odd, block_total[half:], block_total[:half])
    even_decays, pair_decays, even_states, pair_states, sents, marks = ([], [], [], [], [], [])
    for chunk in range(CHUNKS):
        arrived = after(lax.ppermute(sending[chunk], "seq", swap), *marks)
        if chunk == 0:
            total_other = jnp.sum(arrived[rows : rows + 3, :half].astype(F32), axis=0)
            even_decay = jnp.exp(jnp.where(odd, total_other, total_own))[:, None, None]
            odd_decay = jnp.exp(jnp.where(odd, total_own, total_other))[:, None, None]
        place = slice(chunk * part, (chunk + 1) * part)
        own = states[chunk].reshape(part, width, width)
        arrived = arrived[:rows].astype(F32).reshape(part, width, width)
        even_states.append(jnp.where(odd, arrived, own))
        odd_state = jnp.where(odd, own, arrived)
        even_decays.append(even_decay[place])
        pair_decays.append(even_decay[place] * odd_decay[place])
        pair_states.append(odd_decay[place] * even_states[-1] + odd_state)
        sents.append(pair_states[-1].astype(BF16))
        marks = [sents[-1]]
        if chunk == 0:
            shared = share(sents[-1])
            marks = [*marks, *shared]
    shared = (after(shared[0], sents[-1]), shared[1])
    swapped = lax.ppermute(shared[0], "seq", swap)
    marks = [sents[-1], shared[0]]
    links = count // 2 - 1
    turn = max(links - 2, 0)
    befores = [jnp.zeros_like(state) for state in pair_states]
    finished = []
    for link in range(links):
        pairs = [(2 * link + k, 2 * link + 2 + k) for k in range(2)]
        gots = [lax.ppermute(sent, "seq", pairs) for sent in sents]
        if link == turn:
            result = aside(sents[-1])
            marks = [*marks, *result]
        for chunk in range(CHUNKS):
            got = after(gots[chunk], *marks).astype(F32)
            before = befores[chunk] = befores[chunk] + got
            if link < links - 1:
                sents[chunk] = (pair_decays[chunk] * before + pair_states[chunk]).astype(BF16)
                marks = [sents[chunk]]
            else:
                between = even_decays[chunk] * before + even_states[chunk]
                kept = jnp.where(odd, between, before).astype(BF16)
                moved = jnp.where(odd, before, between).astype(BF16)
                marks = [kept, moved]
            if link == links - 1:
                finished.append(finish(chunk, kept, moved, result[0], swapped))
                marks = [*marks, *finished[-1][:2]]
    return (finished, result[1], shared[1])


def ring_pairs(count):
    order = list(range(0, count, 2)) + list(range(count - 1, 0, -2))
    right = [(order[i], order[(i + 1) % count]) for i in range(count)]
    return (right, [(b, a) for a, b in right])


def ring_block(count, position):
    block = lax.axis_index("seq")
    here = jnp.where(block % 2 == 0, block // 2, count - 1 - block // 2)
    offset = count - position if position <= count // 2 else position - count // 2
    there = (here + offset) % count
    return jnp.where(there < count // 2, 2 * there, 2 * (count - 1 - there) + 1)


def ring_gather(halves, holds):
    steps = lax.axis_size("seq") // 2
    right, left = ring_pairs(2 * steps)
    chains = [(0, right), (1, left), (1, right), (0, left)]
    moving = [halves[half] for half, _ in chains]
    brought = [list(halves)]
    marks = list(halves)
    for step in range(steps):
        here = chains if step < steps - 1 else chains[:2]
        gots = [lax.ppermute(moving[k], "seq", way) for k, (_, way) in enumerate(here)]
        if step in holds:
            marks = [*marks, *holds[step](brought)]
        brought.append([])
        for k, got in enumerate(gots):
            moving[k] = after(got, *marks)
            marks = [moving[k]]
            brought[-1].append(moving[k])
    return brought


def ring_places(steps, step):
    if step == 0:
        return [(0, 0), (0, 1)]
    to_left, to_right = (step, steps + step)
    if step == steps:
        return [(to_left, 0), (to_left, 1)]
    return [(to_left, 0), (to_right, 1), (to_left, 1), (to_right, 0)]


def ring_scatter(low, rest, rows, last):
    steps = lax.axis_size("seq") // 2
    right, left = ring_pairs(2 * steps)
    partials = [low, None]

    def piece(position, half):
        return partials[half][position * rows : (position + 1) * rows]

    chains = [
        (0, left, [steps, *range(steps - 1, 0, -1)]),
        (0, right, list(range(2 * steps - 1, steps, -1))),
        (1, right, [steps, *range(2 * steps - 1, steps, -1)]),
        (1, left, list(range(steps - 1, 0, -1))),
    ]
    sents = [piece(positions[0], 0).astype(BF16) for _, _, positions in chains[:2]]
    partials[1] = rest(sents)
    sents += [piece(positions[0], 1).astype(BF16) for _, _, positions in chains[2:]]
    marks = list(sents)
    for step in range(1, steps + 1):
        order = (0, 2, 3, 1)
        gots = {
            k: lax.ppermute(sents[k], "seq", chains[k][1])
            for k in order
            if step <= len(chains[k][2])
        }
        if step == steps:
            marks = [*marks, *last(marks)]
        for k, got in gots.items():
            half, _, positions = chains[k]
            got = after(got, *marks)
            if step < len(positions):
                got = (piece(positions[step], half) + got.astype(F32)).astype(BF16)
            sents[k] = got
            marks = [got]
    return (piece(0, 0), piece(0, 1), *sents)


def shards(
    queries,
    key_rows,
    values,
    log_decay,
    residual,
    attn_gain,
    moe_gain,
    router,
    routes,
    slot_pos,
    gate_weight,
    up_weight,
    down_weight,
):
    count = lax.axis_size("seq")
    exchange = [(0, 1), (1, 0)]
    swap = [(i, i ^ 1) for i in range(count)]
    log_rows, route_rows, slot_rows = (log_decay.T, routes.T, slot_pos.T)
    attn_gain, moe_gain = (attn_gain[None], moe_gain[None])
    odd = lax.axis_index("seq") % 2 == 1
    sending = half_state(True, after(log_rows, odd), key_rows, values)
    *states, running = half_state(False, after(log_rows, sending[0]), key_rows, values)

    def routed(sent, mark):
        within, pack = within_block(
            sent,
            running,
            after(queries, mark),
            key_rows,
            values,
            residual,
            route_rows,
            slot_rows,
        )
        return (pack, within)

    weights = (gate_weight, up_weight, down_weight)

    def finish(chunk, kept, moved, own, got):
        rows = pair_rows(chunk, own, got, attn_gain, kept, moved, weights)
        return (*rows, kept, lax.ppermute(moved, "seq", swap))

    finished, within_own, within_other = entering_state(
        odd,
        states,
        sending,
        running[:, -1],
        functools.partial(routed, False),
        functools.partial(routed, True),
        finish,
    )
    rows_mine, rows_sent, kept, swapped = zip(*finished, strict=True)
    rows_got = lax.ppermute(jnp.concatenate(rows_sent, axis=1), "exp", exchange)
    halves = (jnp.concatenate(rows_mine, axis=1), after(rows_got, *swapped[:2]))

    steps = count // 2
    early = []

    def hold_rows(brought):
        places = sum([ring_places(steps, step) for step in range(steps - 1)], [])
        early.append(early_rows(places, count * CAP, moe_gain, sum(brought, [])))
        return early[-1]

    def hold_partial(brought):
        early.append(
            partial_rows(
                ring_places(steps, steps - 1),
                moe_gain,
                early[-1],
                brought[-1],
                gate_weight[0],
                up_weight[0],
            )
        )
        return early[-1]

    holds = {0: lambda brought: swapped, steps - 2: hold_rows, steps - 1: hold_partial}
    brought = ring_gather(halves, holds)
    hidden_units = expert_rows(
        ring_places(steps, steps),
        moe_gain,
        early[-1],
        brought[-1],
        gate_weight[0],
        up_weight[0],
    )
    low = expert_down(0, hidden_units, down_weight[0])

    def rest(marks):
        return expert_down(1, after(hidden_units, *marks), down_weight[0])

    held = []

    def hold_hidden(marks):
        held.extend(
            hidden_block(
                running,
                queries,
                within_own,
                within_other,
                after(residual, *marks),
                attn_gain,
                moe_gain,
                router.T,
                route_rows,
                kept,
                swapped,
            )
        )
        return held

    sums_here = ring_scatter(low, rest, CAP, hold_hidden)
    hidden_half, sums = held
    got_sums = lax.ppermute(sums, "exp", exchange)
    table = share_table(queries.shape[1], sums, got_sums, route_rows, slot_rows)
    out_own, out_sent = expert_total(*sums_here)
    out_got = lax.ppermute(out_sent, "exp", exchange)
    return mixed_block(table, hidden_half, out_own, out_got)


def solution(mesh):
    placed = (
        P(("groups", "seq"), "exp"),
        P(("groups", "seq"), "exp"),
        P(("groups", "seq"), "exp"),
        P(("groups", "seq"), "exp"),
        P(("groups", "seq"), "exp"),
        P("exp"),
        P(),
        P(),
        P(("groups", "seq"), None),
        P(("groups", "seq"), None),
        P("exp", None, "seq"),
        P("exp", None, "seq"),
        P("exp", "seq", None),
    )
    return jax.shard_map(
        shards, mesh=mesh, in_specs=placed, out_specs=P(("groups", "seq"), "exp"), check_vma=False
    )
```

```python
import functools

import jax
import jax.numpy as jnp
from jax import lax
from jax.experimental import pallas as pl
from jax.experimental.pallas import tpu as pltpu
from jax.sharding import PartitionSpec as P

CAP = 16
CHUNKS = 3
VMEM = pl.BlockSpec(memory_space=pltpu.VMEM)
SMEM = pl.BlockSpec(memory_space=pltpu.SMEM)
HBM = pl.BlockSpec(memory_space=pl.ANY)
F32, BF16 = (jnp.float32, jnp.bfloat16)


def grant(mebibytes):
    return pltpu.CompilerParams(vmem_limit_bytes=mebibytes * 2**20)


def triangle(length):
    rows = lax.broadcasted_iota(jnp.int32, (length, length), 0)
    columns = lax.broadcasted_iota(jnp.int32, (length, length), 1)
    return rows >= columns


def as_columns(table):
    heads, length = table.shape
    return jnp.concatenate([table, jnp.zeros((length - heads, length), F32)], axis=0).T


def running_sums(log_rows):
    return lax.dot_general(
        log_rows,
        jnp.where(triangle(log_rows.shape[1]), 1.0, 0.0),
        (((1,), (1,)), ((), ())),
        precision=lax.Precision.HIGHEST,
        preferred_element_type=F32,
    )


def state_kernel(sent, log_ref, key_ref, value_ref, *refs):
    outs, (log, key, value, sems) = (refs[:-4], refs[-4:])
    heads, length = log_ref.shape
    width = key_ref.shape[1] // heads
    half = heads // 2
    part = half // CHUNKS
    side = (lax.axis_index("seq") + sent) % 2
    log_copy = pltpu.make_async_copy(log_ref, log, sems.at[2 * CHUNKS])
    log_copy.start()
    copies = []
    for chunk in range(CHUNKS):
        lanes = pl.ds(pl.multiple_of((side * half + chunk * part) * width, width), part * width)
        here = pl.ds(chunk * part * width, part * width)
        pair = (
            pltpu.make_async_copy(key_ref.at[:, lanes], key.at[:, here], sems.at[2 * chunk]),
            pltpu.make_async_copy(value_ref.at[:, lanes], value.at[:, here], sems.at[2 * chunk + 1]),
        )
        for copy in pair:
            copy.start()
        copies.append(pair)
    log_copy.wait()
    running = running_sums(log[...])
    columns = as_columns(running)
    columns = jnp.where(side == 0, columns[:, :half], columns[:, half:heads])
    totals = columns[length - 1 :, :]
    rest = jnp.exp(totals - columns)
    for head in range(half):
        chunk, place = divmod(head, part)
        if place == 0:
            for copy in copies[chunk]:
                copy.wait()
        lanes = slice(head * width, (head + 1) * width)
        scaled = (key[:, lanes].astype(F32) * rest[:, head : head + 1]).astype(BF16)
        state = lax.dot_general(
            scaled, value[:, lanes], (((0,), (0,)), ((), ())), preferred_element_type=F32
        )
        rows = slice(place * width, (place + 1) * width)
        outs[chunk][rows, :] = state.astype(outs[chunk].dtype)
    if sent:
        first = totals.astype(BF16).astype(F32)
        second = (totals - first).astype(BF16).astype(F32)
        third = totals - first - second
        rows = jnp.concatenate([first, second, third, jnp.zeros((13, half), F32)], axis=0)
        rows = jnp.concatenate([rows, jnp.zeros((16, width - half), F32)], axis=1)
        outs[0][part * width :, :] = rows.astype(BF16)
    else:
        outs[CHUNKS][...] = running


def half_state(sent, log_rows, key_rows, value_rows):
    heads, length = log_rows.shape
    width = key_rows.shape[1] // heads
    rows = heads // 2 // CHUNKS * width
    shapes = [jax.ShapeDtypeStruct((rows, width), BF16 if sent else F32)] * CHUNKS
    if sent:
        shapes[0] = jax.ShapeDtypeStruct((rows + 16, width), BF16)
    else:
        shapes.append(jax.ShapeDtypeStruct((heads, length), F32))
    return pl.pallas_call(
        functools.partial(state_kernel, sent),
        out_shape=tuple(shapes),
        in_specs=[HBM, HBM, HBM],
        out_specs=(VMEM,) * len(shapes),
        scratch_shapes=[
            pltpu.VMEM((heads, length), F32),
            pltpu.VMEM((length, heads // 2 * width), BF16),
            pltpu.VMEM((length, heads // 2 * width), BF16),
            pltpu.SemaphoreType.DMA((2 * CHUNKS + 1,)),
        ],
        compiler_params=grant(60 if sent else 8),
        cost_estimate=pl.CostEstimate(
            flops=length * width * width * heads,
            bytes_accessed=2 * length * width * heads,
            transcendentals=0,
        ),
    )(log_rows, key_rows, value_rows)


def slots_of(route_ref, slot_ref, capacity, values):
    shape = (2 * capacity, route_ref.shape[1])
    place = lax.broadcasted_iota(jnp.int32, shape, 0)
    expert = jnp.where(place < capacity, lax.axis_index("exp"), 1 - lax.axis_index("exp"))
    slot = place % capacity
    table = jnp.zeros(shape, F32)
    for choice, value in enumerate(values):
        here = slice(choice, choice + 1)
        match = (route_ref[here, :] == expert) & (slot_ref[here, :] == slot)
        table += jnp.where(match, value, 0.0)
    return table


def within_kernel(
    sent, run_ref, query_ref, key_ref, value_ref, residual_ref, route_ref, slot_ref, out_ref, pack_ref
):
    heads, length = run_ref.shape
    width = key_ref.shape[1] // heads
    half = heads // 2
    span = half * width
    causal = triangle(length)
    side = (lax.axis_index("seq") + sent) % 2
    running = jnp.where(side == 0, run_ref[:half, :], run_ref[half:, :])
    columns = as_columns(running)
    for head in range(half):
        lanes = pl.ds(pl.multiple_of((side * half + head) * width, width), width)
        scores = lax.dot_general(
            query_ref[:, lanes],
            key_ref[:, lanes],
            (((1,), (1,)), ((), ())),
            preferred_element_type=F32,
        )
        spread = columns[:, head : head + 1] - running[head : head + 1, :]
        mixing = jnp.where(causal, scores * jnp.exp(spread), 0.0).astype(BF16)
        out_ref[:, head * width : (head + 1) * width] = jnp.dot(
            mixing, value_ref[:, lanes], preferred_element_type=F32
        )

    table = slots_of(route_ref, slot_ref, pack_ref.shape[0] // 2, (1.0, 1.0)).astype(BF16)

    def routed(array):
        return jnp.dot(table, array, preferred_element_type=F32).astype(BF16)

    grown = jnp.exp(columns)
    high = grown.astype(BF16)
    low = (grown - high.astype(F32)).astype(BF16)
    lanes = pl.ds(pl.multiple_of(side * span, span), span)
    pack_ref[:, :span] = routed(query_ref[:, lanes])
    pack_ref[:, span : 2 * span] = routed(residual_ref[:, lanes])
    pack_ref[:, 2 * span : 3 * span] = routed(out_ref[...].astype(BF16))
    blank = jnp.zeros((table.shape[0], width // 2 - half), BF16)
    pack_ref[:, 3 * span :] = jnp.concatenate(
        [routed(high)[:, :half], blank, routed(low)[:, :half], blank], axis=1
    )


def within_block(sent, running, query_rows, key_rows, value_rows, residual, routes, slots):
    heads, length = running.shape
    width = key_rows.shape[1] // heads
    span = heads // 2 * width
    return pl.pallas_call(
        functools.partial(within_kernel, sent),
        out_shape=(
            jax.ShapeDtypeStruct((length, span), F32),
            jax.ShapeDtypeStruct((2 * CAP, 3 * span + width), BF16),
        ),
        in_specs=[VMEM] * 7,
        out_specs=(VMEM, VMEM),
        compiler_params=grant(16),
        cost_estimate=pl.CostEstimate(
            flops=4 * length * length * span,
            bytes_accessed=12 * length * span,
            transcendentals=heads // 2 * length * length,
        ),
    )(running, query_rows, key_rows, value_rows, residual, routes, slots)


def rows_kernel(chunk, own_ref, got_ref, gain_ref, kept_ref, moved_ref, mine_ref, theirs_ref):
    part, width, _ = kept_ref.shape
    half = part * CHUNKS
    span = half * width
    odd = lax.axis_index("seq") % 2
    capacity = own_ref.shape[0] // 2
    for pack, state_ref, moved in ((own_ref, kept_ref, 0), (got_ref, moved_ref, 1)):
        tail = pack[:, 3 * span :].astype(F32)
        grown = tail[:, :half] + tail[:, width // 2 : width // 2 + half]
        place = pl.ds(pl.multiple_of((odd ^ moved) * capacity, capacity), capacity)
        for index in range(part):
            head = chunk * part + index
            lanes = [slice(k * span + head * width, k * span + (head + 1) * width) for k in range(3)]
            gain = jnp.where(odd == 0, gain_ref[:, lanes[0]], gain_ref[:, lanes[1]])
            query, residual, within = [pack[:, lane] for lane in lanes]
            carried = jnp.dot(query, state_ref[index], preferred_element_type=F32)
            raw = within.astype(F32) + carried * grown[:, head : head + 1]
            normed = raw * lax.rsqrt(jnp.mean(raw * raw, axis=1, keepdims=True) + 1e-05)
            hidden = (residual.astype(F32) + normed * gain).astype(BF16)
            here = slice(index * width, (index + 1) * width)
            mine_ref[place, here] = hidden[:capacity]
            theirs_ref[place, here] = hidden[capacity:]


def pair_rows(chunk, own, got, gain, kept, moved, weights):
    part, width, _ = kept.shape
    rows = own.shape[0]
    shape = jax.ShapeDtypeStruct((rows, part * width), BF16)
    flops = 4 * rows * part * width * width
    if chunk == CHUNKS - 1:
        flops = 1500 * sum(weight.size for weight in weights)
    return pl.pallas_call(
        functools.partial(rows_kernel, chunk),
        out_shape=(shape, shape),
        in_specs=[VMEM] * 5,
        out_specs=(VMEM, VMEM),
        compiler_params=grant(8),
        cost_estimate=pl.CostEstimate(
            flops=flops, bytes_accessed=12 * own.size, transcendentals=0
        ),
    )(own, got, gain, kept, moved)


def hidden_kernel(
    sent,
    run_ref,
    query_ref,
    within_ref,
    residual_ref,
    gain_ref,
    moe_gain_ref,
    router_ref,
    route_ref,
    before_ref,
    *refs,
):
    *state_refs, hidden_ref, sums_ref = refs
    heads, length = run_ref.shape
    span = hidden_ref.shape[1]
    half, part = (heads // 2, state_refs[0].shape[0])
    width = span // half
    side = (lax.axis_index("seq") + sent) % 2
    grown = as_columns(jnp.exp(jnp.where(side == 0, run_ref[:half, :], run_ref[half:, :])))
    squares = jnp.zeros((length, width), F32)
    for head in range(half):
        here = slice(head * width, (head + 1) * width)
        lanes = pl.ds(pl.multiple_of((side * half + head) * width, width), width)
        state = state_refs[head // part][head % part]
        carried = jnp.dot(query_ref[:, lanes], state, preferred_element_type=F32)
        raw = within_ref[:, here] + carried * grown[:, head : head + 1]
        normed = raw * lax.rsqrt(jnp.mean(raw * raw, axis=1, keepdims=True) + 1e-05)
        hidden = (residual_ref[:, lanes].astype(F32) + normed * gain_ref[:, lanes]).astype(BF16)
        hidden_ref[:, here] = hidden
        value = hidden.astype(F32)
        squares += value * value
    here = pl.ds(pl.multiple_of((lax.axis_index("exp") * 2 + side) * span, span), span)
    weights = router_ref[:, here].astype(F32) * moe_gain_ref[:, here]
    first = weights.astype(BF16)
    second = (weights - first.astype(F32)).astype(BF16)
    third = (weights - first.astype(F32) - second.astype(F32)).astype(BF16)
    products = lax.dot_general(
        hidden_ref[...],
        jnp.concatenate([first, second, third, jnp.zeros_like(first)], axis=0),
        (((1,), (1,)), ((), ())),
        preferred_element_type=F32,
    ).T
    count = weights.shape[0]
    logits = products[:count] + products[count : 2 * count] + products[2 * count : 3 * count]
    expert = lax.broadcasted_iota(jnp.int32, logits.shape, 0)
    for choice in range(2):
        here = slice(choice, choice + 1)
        chosen = jnp.where(route_ref[here, :] == expert, logits, 0.0)
        sums_ref[here, :] = before_ref[here, :] + jnp.sum(chosen, axis=0, keepdims=True)
    sums_ref[2:3, :] = before_ref[2:3, :] + jnp.sum(squares.T, axis=0, keepdims=True)
    sums_ref[3:, :] = jnp.zeros((sums_ref.shape[0] - 3, length), F32)


def hidden_block(
    sent, running, query_rows, within, residual, gain, moe_gain, router, routes, before, states
):
    heads, length = running.shape
    return pl.pallas_call(
        functools.partial(hidden_kernel, sent),
        out_shape=(
            jax.ShapeDtypeStruct(within.shape, BF16),
            jax.ShapeDtypeStruct(before.shape, F32),
        ),
        in_specs=[VMEM] * (9 + CHUNKS),
        out_specs=(VMEM, VMEM),
        compiler_params=grant(8),
        cost_estimate=pl.CostEstimate(
            flops=4 * within.size * within.shape[1] // heads,
            bytes_accessed=12 * within.size,
            transcendentals=0,
        ),
    )(running, query_rows, within, residual, gain, moe_gain, router, routes, before, *states)


def far_side(count):
    return ring_block(count, count // 2) % 2


def quarter_of(count, late, side):
    return (lax.axis_index("exp") ^ side) * 2 + (far_side(count) ^ 1 ^ late)


def place_pieces(places, gain_ref, pieces, scaled_ref, square_ref):
    quarter = scaled_ref.shape[1] // 4
    for (position, side), piece in zip(places, pieces, strict=True):
        height = piece.shape[0]
        count = 2 * scaled_ref.shape[0] // height
        block = ring_block(count, position)
        rows = pl.ds(pl.multiple_of(block // 2 * height, height), height)
        late = (block % 2) ^ far_side(count) ^ 1
        lanes = pl.ds(pl.multiple_of((late * 2 + side) * quarter, quarter), quarter)
        first = ((lax.axis_index("exp") ^ side) * 2 + block % 2) * quarter
        gain = gain_ref[:, pl.ds(pl.multiple_of(first, quarter), quarter)]
        value = piece[...].astype(F32)
        square = jnp.sum(value * value, axis=1, keepdims=True)
        square_ref[rows, :] += jnp.broadcast_to(square, (height, square_ref.shape[1]))
        scaled_ref[rows, lanes] = (value * gain).astype(BF16)


def products(late, scaled_ref, gate_ref, up_ref):
    quarter = scaled_ref.shape[1] // 4
    gate_part, up_part = (0.0, 0.0)
    for side in range(2):
        rows = scaled_ref[:, (late * 2 + side) * quarter : (late * 2 + side + 1) * quarter]
        first = quarter_of(scaled_ref.shape[0] // CAP, late, side) * quarter
        here = pl.ds(pl.multiple_of(first, quarter), quarter)
        gate_part += jnp.dot(rows, gate_ref[here, :], preferred_element_type=F32)
        up_part += jnp.dot(rows, up_ref[here, :], preferred_element_type=F32)
    return (gate_part, up_part)


def early_kernel(places, gain_ref, *refs):
    *pieces, scaled_ref, square_ref = refs
    square_ref[...] = jnp.zeros_like(square_ref)
    place_pieces(places, gain_ref, pieces, scaled_ref, square_ref)


def early_rows(places, rows, gain, pieces):
    return pl.pallas_call(
        functools.partial(early_kernel, places),
        out_shape=(
            jax.ShapeDtypeStruct((rows, gain.shape[1]), BF16),
            jax.ShapeDtypeStruct((rows, 128), F32),
        ),
        in_specs=[VMEM] * (1 + len(pieces)),
        out_specs=(VMEM, VMEM),
        compiler_params=grant(8),
    )(gain, *pieces)


def partial_kernel(places, gain_ref, gate_ref, up_ref, early_ref, early_square_ref, *refs):
    *pieces, scaled_ref, square_ref, gate_out_ref, up_out_ref = refs
    scaled_ref[...] = early_ref[...]
    square_ref[...] = early_square_ref[...]
    place_pieces(places, gain_ref, pieces, scaled_ref, square_ref)
    gate_out_ref[...], up_out_ref[...] = products(0, scaled_ref, gate_ref, up_ref)


def partial_rows(places, gain, early, pieces, gate_weight, up_weight):
    width, hidden_units = gate_weight.shape
    rows = early[0].shape[0]
    part = jax.ShapeDtypeStruct((rows, hidden_units), F32)
    return pl.pallas_call(
        functools.partial(partial_kernel, places),
        out_shape=(
            jax.ShapeDtypeStruct((rows, width), BF16),
            jax.ShapeDtypeStruct((rows, 128), F32),
            part,
            part,
        ),
        in_specs=[VMEM] * (5 + len(pieces)),
        out_specs=(VMEM,) * 4,
        compiler_params=grant(max(6, rows // 16)),
        cost_estimate=pl.CostEstimate(
            flops=2 * rows * width * hidden_units,
            bytes_accessed=2 * width * hidden_units,
            transcendentals=0,
        ),
    )(gain, gate_weight, up_weight, *early, *pieces)


def expert_kernel(
    places, gain_ref, gate_ref, up_ref, early_ref, early_square_ref, gate_in_ref, up_in_ref, *refs
):
    *pieces, hidden_ref, scaled_ref, square_ref, block_ref = refs
    width = gate_ref.shape[0]
    capacity = CAP
    count = scaled_ref.shape[0] // capacity
    scaled_ref[:, width // 2 :] = early_ref[:, width // 2 :]
    square_ref[...] = early_square_ref[...]
    place_pieces(places, gain_ref, pieces, scaled_ref, square_ref)
    inverse = lax.rsqrt(square_ref[...][:, :1] / width + 1e-06)
    gate_part, up_part = products(1, scaled_ref, gate_ref, up_ref)
    gate_part = (gate_in_ref[...] + gate_part) * inverse
    up_part = (up_in_ref[...] + up_part) * inverse
    block_ref[...] = (jax.nn.silu(gate_part) * up_part).astype(BF16)
    for position in range(count):
        block = ring_block(count, position)
        hidden_ref[position * capacity : (position + 1) * capacity] = block_ref[
            pl.ds(pl.multiple_of(block * capacity, capacity), capacity)
        ]


def expert_rows(places, gain, early, pieces, gate_weight, up_weight):
    width, hidden_units = gate_weight.shape
    rows = early[0].shape[0]
    return pl.pallas_call(
        functools.partial(expert_kernel, places),
        out_shape=jax.ShapeDtypeStruct((rows, hidden_units), BF16),
        in_specs=[VMEM] * (7 + len(pieces)),
        out_specs=VMEM,
        scratch_shapes=[
            pltpu.VMEM((rows, width), BF16),
            pltpu.VMEM((rows, 128), F32),
            pltpu.VMEM((rows, hidden_units), BF16),
        ],
        compiler_params=grant(max(6, rows // 16)),
        cost_estimate=pl.CostEstimate(
            flops=2 * rows * width * hidden_units,
            bytes_accessed=2 * width * hidden_units,
            transcendentals=0,
        ),
    )(gain, gate_weight, up_weight, *early, *pieces)


def down_kernel(half, hidden_ref, down_ref, out_ref):
    quarter = out_ref.shape[1] // 2
    for part in range(2):
        first = ((lax.axis_index("exp") ^ half) * 2 + part) * quarter
        weights = down_ref[:, pl.ds(pl.multiple_of(first, quarter), quarter)]
        out_ref[:, part * quarter : (part + 1) * quarter] = jnp.dot(
            hidden_ref[...], weights, preferred_element_type=F32
        )


def expert_down(half, hidden, down_weight):
    rows, width = (hidden.shape[0], down_weight.shape[1])
    return pl.pallas_call(
        functools.partial(down_kernel, half),
        out_shape=jax.ShapeDtypeStruct((rows, width // 2), F32),
        in_specs=[VMEM] * 2,
        out_specs=VMEM,
        compiler_params=grant(max(6, rows // 32)),
        cost_estimate=pl.CostEstimate(
            flops=rows * width * hidden.shape[1],
            bytes_accessed=width * hidden.shape[1],
            transcendentals=0,
        ),
    )(hidden, down_weight)


def share_kernel(span, sums_ref, got_sums_ref, route_ref, slot_ref, table_ref):
    capacity = table_ref.shape[1] // 4
    sums = sums_ref[...] + got_sums_ref[...]
    inverse = lax.rsqrt(sums[2:3] / (2 * span) + 1e-06)
    gates = jax.nn.sigmoid(sums[:2] * inverse)
    shares = gates / jnp.sum(gates, axis=0, keepdims=True)
    table = slots_of(route_ref, slot_ref, capacity, (shares[:1], shares[1:]))
    table = as_columns(table)[:, : 2 * capacity]
    high = table.astype(BF16)
    low = (table - high.astype(F32)).astype(BF16)
    table_ref[...] = jnp.concatenate([high, low], axis=1)


def share_table(span, sums, got_sums, routes, slots):
    return pl.pallas_call(
        functools.partial(share_kernel, span),
        out_shape=jax.ShapeDtypeStruct((routes.shape[1], 4 * CAP), BF16),
        in_specs=[VMEM] * 4,
        out_specs=VMEM,
        compiler_params=grant(4),
    )(sums, got_sums, routes, slots)


def mixed_kernel(table_ref, kept_ref, swapped_ref, *refs):
    *part_refs, out_ref, held_ref, sems = refs
    span = out_ref.shape[1]
    even = lax.axis_index("seq") % 2 == 0
    copies = []
    for part in range(4):
        lanes = slice(part * span // 4, (part + 1) * span // 4)
        parts = [ref[:, lanes].astype(F32) for ref in part_refs]
        own, other = [
            (first + second + third).astype(BF16)
            for first, second, third in (parts[:3], parts[3:])
        ]
        outs = jnp.concatenate([own, other] * 2, axis=0)
        mixed = jnp.dot(table_ref[...], outs, preferred_element_type=F32)
        here = slice(part % 2 * span // 4, (part % 2 + 1) * span // 4)
        halves = (kept_ref[:, here], swapped_ref[:, here])
        hidden = jnp.where(even, halves[part // 2], halves[1 - part // 2])
        held_ref[:, lanes] = (hidden.astype(F32) + mixed).astype(BF16)
        copies.append(
            pltpu.make_async_copy(held_ref.at[:, lanes], out_ref.at[:, lanes], sems.at[part])
        )
        copies[-1].start()
    for copy in copies:
        copy.wait()


def mixed_block(table, kept, swapped, parts):
    shape = (kept.shape[0], 2 * kept.shape[1])
    return pl.pallas_call(
        mixed_kernel,
        out_shape=jax.ShapeDtypeStruct(shape, BF16),
        in_specs=[VMEM] * (3 + len(parts)),
        out_specs=HBM,
        scratch_shapes=[pltpu.VMEM(shape, BF16), pltpu.SemaphoreType.DMA((4,))],
        compiler_params=grant(8),
        cost_estimate=pl.CostEstimate(
            flops=16 * kept.size * CAP,
            bytes_accessed=8 * kept.size,
            transcendentals=0,
        ),
    )(table, kept, swapped, *parts)


def after(value, *others):
    return lax.optimization_barrier((value, *others))[0]


def entering_state(odd, states, sending, block_total, aside, share, finish):
    count = lax.axis_size("seq")
    swap = [(i, i ^ 1) for i in range(count)]
    rows, width = states[0].shape
    part = rows // width
    half = part * CHUNKS
    total_own = jnp.where(odd, block_total[half:], block_total[:half])
    even_decays, pair_decays, even_states, pair_states, sents, marks = ([], [], [], [], [], [])
    for chunk in range(CHUNKS):
        arrived = after(lax.ppermute(sending[chunk], "seq", swap), *marks)
        if chunk == 0:
            total_other = jnp.sum(arrived[rows : rows + 3, :half].astype(F32), axis=0)
            even_decay = jnp.exp(jnp.where(odd, total_other, total_own))[:, None, None]
            odd_decay = jnp.exp(jnp.where(odd, total_own, total_other))[:, None, None]
        place = slice(chunk * part, (chunk + 1) * part)
        own = states[chunk].reshape(part, width, width)
        arrived = arrived[:rows].astype(F32).reshape(part, width, width)
        even_states.append(jnp.where(odd, arrived, own))
        odd_state = jnp.where(odd, own, arrived)
        even_decays.append(even_decay[place])
        pair_decays.append(even_decay[place] * odd_decay[place])
        pair_states.append(odd_decay[place] * even_states[-1] + odd_state)
        sents.append(pair_states[-1].astype(BF16))
        marks = [sents[-1]]
        if chunk == 0:
            shared = share(sents[-1])
            marks = [*marks, *shared]
    shared = (after(shared[0], sents[-1]), shared[1])
    swapped = lax.ppermute(shared[0], "seq", swap)
    marks = [sents[-1], shared[0]]
    links = count // 2 - 1
    turn = max(links - 2, 0)
    befores = [jnp.zeros_like(state) for state in pair_states]
    finished = []
    for link in range(links):
        pairs = [(2 * link + k, 2 * link + 2 + k) for k in range(2)]
        gots = [lax.ppermute(sent, "seq", pairs) for sent in sents]
        if link == turn:
            result = aside(sents[-1])
            marks = [*marks, *result]
        for chunk in range(CHUNKS):
            got = after(gots[chunk], *marks).astype(F32)
            before = befores[chunk] = befores[chunk] + got
            if link < links - 1:
                sents[chunk] = (pair_decays[chunk] * before + pair_states[chunk]).astype(BF16)
                marks = [sents[chunk]]
            else:
                between = even_decays[chunk] * before + even_states[chunk]
                kept = jnp.where(odd, between, before).astype(BF16)
                moved = jnp.where(odd, before, between).astype(BF16)
                marks = [kept, moved]
            if link == links - 1:
                finished.append(finish(chunk, kept, moved, result[0], swapped))
                marks = [*marks, *finished[-1][:2]]
    return (finished, result[1], shared[1])


def ring_pairs(count):
    order = list(range(0, count, 2)) + list(range(count - 1, 0, -2))
    right = [(order[i], order[(i + 1) % count]) for i in range(count)]
    return (right, [(b, a) for a, b in right])


def ring_block(count, position):
    block = lax.axis_index("seq")
    here = jnp.where(block % 2 == 0, block // 2, count - 1 - block // 2)
    offset = count - position if position <= count // 2 else position - count // 2
    there = (here + offset) % count
    return jnp.where(there < count // 2, 2 * there, 2 * (count - 1 - there) + 1)


def ring_gather(halves, holds):
    steps = lax.axis_size("seq") // 2
    right, left = ring_pairs(2 * steps)
    chains = [(0, right), (1, left), (1, right), (0, left)]
    moving = [halves[half] for half, _ in chains]
    brought = [list(halves)]
    marks = list(halves)
    for step in range(steps):
        here = chains if step < steps - 1 else chains[:2]
        gots = [lax.ppermute(moving[k], "seq", way) for k, (_, way) in enumerate(here)]
        if step in holds:
            marks = [*marks, *holds[step](brought)]
        brought.append([])
        for k, got in enumerate(gots):
            moving[k] = after(got, *marks)
            marks = [moving[k]]
            brought[-1].append(moving[k])
    return brought


def ring_places(steps, step):
    if step == 0:
        return [(0, 0), (0, 1)]
    to_left, to_right = (step, steps + step)
    if step == steps:
        return [(to_left, 0), (to_left, 1)]
    return [(to_left, 0), (to_right, 1), (to_left, 1), (to_right, 0)]


def ring_scatter(own, rest, rows, holds):
    steps = lax.axis_size("seq") // 2
    right, left = ring_pairs(2 * steps)
    partials = [own, None]

    def piece(position, half):
        return partials[half][position * rows : (position + 1) * rows]

    def move(sent, half, way, last):
        if half == 0 or not last:
            return lax.ppermute(sent, "seq", way)
        across = [(2 * a + core, 2 * b + 1 - core) for a, b in way for core in range(2)]
        return lax.ppermute(sent, ("seq", "exp"), across)

    chains = [
        (0, left, [steps, *range(steps - 1, 0, -1)]),
        (0, right, list(range(2 * steps - 1, steps, -1))),
        (1, right, [steps, *range(2 * steps - 1, steps, -1)]),
        (1, left, list(range(steps - 1, 0, -1))),
    ]
    sents = [piece(positions[0], 0).astype(BF16) for _, _, positions in chains[:2]]
    partials[1] = rest(sents)
    sents += [piece(positions[0], 1).astype(BF16) for _, _, positions in chains[2:]]
    here = piece(0, 1).astype(BF16)
    marks = list(sents)
    for step in range(1, steps + 1):
        gots = {}
        for k in (0, 2, 3, 1):
            half, way, positions = chains[k]
            if step <= len(positions):
                gots[k] = move(sents[k], half, way, step == len(positions))
        if step == 2:
            here = lax.ppermute(here, "exp", [(0, 1), (1, 0)])
            marks = [*marks, here]
        if step in holds:
            marks = [*marks, *holds[step]([sents[k] for k in gots])]
        for k, got in gots.items():
            half, _, positions = chains[k]
            got = after(got, *marks)
            if step < len(positions):
                got = (piece(positions[step], half) + got.astype(F32)).astype(BF16)
            sents[k] = got
            marks = [got]
    return (piece(0, 0), sents[0], sents[1], here, sents[2], sents[3])


def shards(
    queries,
    key_rows,
    values,
    log_decay,
    residual,
    attn_gain,
    moe_gain,
    router,
    routes,
    slot_pos,
    gate_weight,
    up_weight,
    down_weight,
):
    count = lax.axis_size("seq")
    exchange = [(0, 1), (1, 0)]
    swap = [(i, i ^ 1) for i in range(count)]
    log_rows, route_rows, slot_rows = (log_decay.T, routes.T, slot_pos.T)
    attn_gain, moe_gain = (attn_gain[None], moe_gain[None])
    odd = lax.axis_index("seq") % 2 == 1
    sending = half_state(True, after(log_rows, odd), key_rows, values)
    *states, running = half_state(False, after(log_rows, sending[0]), key_rows, values)

    def routed(sent, mark):
        within, pack = within_block(
            sent,
            running,
            after(queries, mark),
            key_rows,
            values,
            residual,
            route_rows,
            slot_rows,
        )
        return (pack, within)

    weights = (gate_weight, up_weight, down_weight)

    def finish(chunk, kept, moved, own, got):
        rows = pair_rows(chunk, own, got, attn_gain, kept, moved, weights)
        return (*rows, kept, lax.ppermute(moved, "seq", swap))

    finished, within_own, within_other = entering_state(
        odd,
        states,
        sending,
        running[:, -1],
        functools.partial(routed, False),
        functools.partial(routed, True),
        finish,
    )
    rows_mine, rows_sent, kept, swapped = zip(*finished, strict=True)
    rows_got = lax.ppermute(jnp.concatenate(rows_sent, axis=1), "exp", exchange)

    def all_rows(sent, mark, within, before, entering):
        return hidden_block(
            sent,
            running,
            queries,
            within,
            after(residual, *mark),
            attn_gain,
            moe_gain,
            router.T,
            route_rows,
            before,
            entering,
        )

    zeros = jnp.zeros((8, running.shape[1]), F32)
    hidden_own, sums = all_rows(False, rows_sent, within_own, zeros, kept)
    halves = (
        jnp.concatenate(rows_mine, axis=1),
        after(rows_got, *swapped[:2], hidden_own, sums),
    )

    steps = count // 2
    early = []

    def hold_rows(brought):
        places = sum([ring_places(steps, step) for step in range(steps - 1)], [])
        early.append(early_rows(places, count * CAP, moe_gain, sum(brought, [])))
        return early[-1]

    def hold_partial(brought):
        early.append(
            partial_rows(
                ring_places(steps, steps - 1),
                moe_gain,
                early[-1],
                brought[-1],
                gate_weight[0],
                up_weight[0],
            )
        )
        return early[-1]

    holds = {0: lambda brought: swapped, steps - 2: hold_rows, steps - 1: hold_partial}
    brought = ring_gather(halves, holds)
    hidden_units = expert_rows(
        ring_places(steps, steps),
        moe_gain,
        early[-1],
        brought[-1],
        gate_weight[0],
        up_weight[0],
    )
    own = expert_down(0, hidden_units, down_weight[0])

    def rest(marks):
        return expert_down(1, after(hidden_units, *marks), down_weight[0])

    held = []

    def hold_hidden(marks):
        held.extend(all_rows(True, marks, within_other, sums, swapped))
        got_sums = lax.ppermute(held[1], "exp", exchange)
        held.append(
            share_table(queries.shape[1], held[1], got_sums, route_rows, slot_rows)
        )
        return held

    parts = ring_scatter(own, rest, CAP, {steps: hold_hidden})
    hidden_other, _, table = held
    return mixed_block(table, hidden_own, hidden_other, parts)


def solution(mesh):
    placed = (
        P(("groups", "seq"), "exp"),
        P(("groups", "seq"), "exp"),
        P(("groups", "seq"), "exp"),
        P(("groups", "seq"), "exp"),
        P(("groups", "seq"), "exp"),
        P("exp"),
        P(),
        P(),
        P(("groups", "seq"), None),
        P(("groups", "seq"), None),
        P("exp", None, "seq"),
        P("exp", None, "seq"),
        P("exp", "seq", None),
    )
    return jax.shard_map(
        shards, mesh=mesh, in_specs=placed, out_specs=P(("groups", "seq"), "exp"), check_vma=False
    )
```

```python
import functools

import jax
import jax.numpy as jnp
from jax import lax
from jax.experimental import pallas as pl
from jax.experimental.pallas import tpu as pltpu
from jax.sharding import PartitionSpec as P

CAP = 16
CHUNKS = 3
VMEM = pl.BlockSpec(memory_space=pltpu.VMEM)
SMEM = pl.BlockSpec(memory_space=pltpu.SMEM)
HBM = pl.BlockSpec(memory_space=pl.ANY)
F32, BF16 = (jnp.float32, jnp.bfloat16)


def grant(mebibytes):
    return pltpu.CompilerParams(vmem_limit_bytes=mebibytes * 2**20)


def triangle(length):
    rows = lax.broadcasted_iota(jnp.int32, (length, length), 0)
    columns = lax.broadcasted_iota(jnp.int32, (length, length), 1)
    return rows >= columns


def as_columns(table):
    heads, length = table.shape
    return jnp.concatenate([table, jnp.zeros((length - heads, length), F32)], axis=0).T


def running_sums(log_rows):
    return lax.dot_general(
        log_rows,
        jnp.where(triangle(log_rows.shape[1]), 1.0, 0.0),
        (((1,), (1,)), ((), ())),
        precision=lax.Precision.HIGHEST,
        preferred_element_type=F32,
    )


def state_kernel(sent, log_ref, key_ref, value_ref, *refs):
    outs, (log, key, value, sems) = (refs[:-4], refs[-4:])
    heads, length = log_ref.shape
    width = key_ref.shape[1] // heads
    half = heads // 2
    part = half // CHUNKS
    side = (lax.axis_index("seq") + sent) % 2
    log_copy = pltpu.make_async_copy(log_ref, log, sems.at[2 * CHUNKS])
    log_copy.start()
    copies = []
    for chunk in range(CHUNKS):
        lanes = pl.ds(pl.multiple_of((side * half + chunk * part) * width, width), part * width)
        here = pl.ds(chunk * part * width, part * width)
        pair = (
            pltpu.make_async_copy(key_ref.at[:, lanes], key.at[:, here], sems.at[2 * chunk]),
            pltpu.make_async_copy(value_ref.at[:, lanes], value.at[:, here], sems.at[2 * chunk + 1]),
        )
        for copy in pair:
            copy.start()
        copies.append(pair)
    log_copy.wait()
    running = running_sums(log[...])
    columns = as_columns(running)
    columns = jnp.where(side == 0, columns[:, :half], columns[:, half:heads])
    totals = columns[length - 1 :, :]
    rest = jnp.exp(totals - columns)
    for head in range(half):
        chunk, place = divmod(head, part)
        if place == 0:
            for copy in copies[chunk]:
                copy.wait()
        lanes = slice(head * width, (head + 1) * width)
        scaled = (key[:, lanes].astype(F32) * rest[:, head : head + 1]).astype(BF16)
        state = lax.dot_general(
            scaled, value[:, lanes], (((0,), (0,)), ((), ())), preferred_element_type=F32
        )
        rows = slice(place * width, (place + 1) * width)
        outs[chunk][rows, :] = state.astype(outs[chunk].dtype)
    if sent:
        first = totals.astype(BF16).astype(F32)
        second = (totals - first).astype(BF16).astype(F32)
        third = totals - first - second
        rows = jnp.concatenate([first, second, third, jnp.zeros((13, half), F32)], axis=0)
        rows = jnp.concatenate([rows, jnp.zeros((16, width - half), F32)], axis=1)
        outs[0][part * width :, :] = rows.astype(BF16)
    else:
        outs[CHUNKS][...] = running


def half_state(sent, log_rows, key_rows, value_rows):
    heads, length = log_rows.shape
    width = key_rows.shape[1] // heads
    rows = heads // 2 // CHUNKS * width
    shapes = [jax.ShapeDtypeStruct((rows, width), BF16 if sent else F32)] * CHUNKS
    if sent:
        shapes[0] = jax.ShapeDtypeStruct((rows + 16, width), BF16)
    else:
        shapes.append(jax.ShapeDtypeStruct((heads, length), F32))
    return pl.pallas_call(
        functools.partial(state_kernel, sent),
        out_shape=tuple(shapes),
        in_specs=[HBM, HBM, HBM],
        out_specs=(VMEM,) * len(shapes),
        scratch_shapes=[
            pltpu.VMEM((heads, length), F32),
            pltpu.VMEM((length, heads // 2 * width), BF16),
            pltpu.VMEM((length, heads // 2 * width), BF16),
            pltpu.SemaphoreType.DMA((2 * CHUNKS + 1,)),
        ],
        compiler_params=grant(60 if sent else 8),
        cost_estimate=pl.CostEstimate(
            flops=length * width * width * heads,
            bytes_accessed=2 * length * width * heads,
            transcendentals=0,
        ),
    )(log_rows, key_rows, value_rows)


def slots_of(route_ref, slot_ref, capacity, values):
    shape = (2 * capacity, route_ref.shape[1])
    place = lax.broadcasted_iota(jnp.int32, shape, 0)
    expert = jnp.where(place < capacity, lax.axis_index("exp"), 1 - lax.axis_index("exp"))
    slot = place % capacity
    table = jnp.zeros(shape, F32)
    for choice, value in enumerate(values):
        here = slice(choice, choice + 1)
        match = (route_ref[here, :] == expert) & (slot_ref[here, :] == slot)
        table += jnp.where(match, value, 0.0)
    return table


def within_kernel(
    sent, run_ref, query_ref, key_ref, value_ref, residual_ref, route_ref, slot_ref, out_ref, pack_ref
):
    heads, length = run_ref.shape
    width = key_ref.shape[1] // heads
    half = heads // 2
    span = half * width
    causal = triangle(length)
    side = (lax.axis_index("seq") + sent) % 2
    running = jnp.where(side == 0, run_ref[:half, :], run_ref[half:, :])
    columns = as_columns(running)
    for head in range(half):
        lanes = pl.ds(pl.multiple_of((side * half + head) * width, width), width)
        scores = lax.dot_general(
            query_ref[:, lanes],
            key_ref[:, lanes],
            (((1,), (1,)), ((), ())),
            preferred_element_type=F32,
        )
        spread = columns[:, head : head + 1] - running[head : head + 1, :]
        mixing = jnp.where(causal, scores * jnp.exp(spread), 0.0).astype(BF16)
        out_ref[:, head * width : (head + 1) * width] = jnp.dot(
            mixing, value_ref[:, lanes], preferred_element_type=F32
        )

    table = slots_of(route_ref, slot_ref, pack_ref.shape[0] // 2, (1.0, 1.0)).astype(BF16)

    def routed(array):
        return jnp.dot(table, array, preferred_element_type=F32).astype(BF16)

    grown = jnp.exp(columns)
    high = grown.astype(BF16)
    low = (grown - high.astype(F32)).astype(BF16)
    lanes = pl.ds(pl.multiple_of(side * span, span), span)
    pack_ref[:, :span] = routed(query_ref[:, lanes])
    pack_ref[:, span : 2 * span] = routed(residual_ref[:, lanes])
    pack_ref[:, 2 * span : 3 * span] = routed(out_ref[...].astype(BF16))
    blank = jnp.zeros((table.shape[0], width // 2 - half), BF16)
    pack_ref[:, 3 * span :] = jnp.concatenate(
        [routed(high)[:, :half], blank, routed(low)[:, :half], blank], axis=1
    )


def within_block(sent, running, query_rows, key_rows, value_rows, residual, routes, slots):
    heads, length = running.shape
    width = key_rows.shape[1] // heads
    span = heads // 2 * width
    return pl.pallas_call(
        functools.partial(within_kernel, sent),
        out_shape=(
            jax.ShapeDtypeStruct((length, span), F32),
            jax.ShapeDtypeStruct((2 * CAP, 3 * span + width), BF16),
        ),
        in_specs=[VMEM] * 7,
        out_specs=(VMEM, VMEM),
        compiler_params=grant(16),
        cost_estimate=pl.CostEstimate(
            flops=4 * length * length * span,
            bytes_accessed=12 * length * span,
            transcendentals=heads // 2 * length * length,
        ),
    )(running, query_rows, key_rows, value_rows, residual, routes, slots)


def rows_kernel(chunk, own_ref, got_ref, gain_ref, kept_ref, moved_ref, mine_ref, theirs_ref):
    part, width, _ = kept_ref.shape
    half = part * CHUNKS
    span = half * width
    odd = lax.axis_index("seq") % 2
    capacity = own_ref.shape[0] // 2
    for pack, state_ref, moved in ((own_ref, kept_ref, 0), (got_ref, moved_ref, 1)):
        tail = pack[:, 3 * span :].astype(F32)
        grown = tail[:, :half] + tail[:, width // 2 : width // 2 + half]
        place = pl.ds(pl.multiple_of((odd ^ moved) * capacity, capacity), capacity)
        for index in range(part):
            head = chunk * part + index
            lanes = [slice(k * span + head * width, k * span + (head + 1) * width) for k in range(3)]
            gain = jnp.where(odd == 0, gain_ref[:, lanes[0]], gain_ref[:, lanes[1]])
            query, residual, within = [pack[:, lane] for lane in lanes]
            carried = jnp.dot(query, state_ref[index], preferred_element_type=F32)
            raw = within.astype(F32) + carried * grown[:, head : head + 1]
            normed = raw * lax.rsqrt(jnp.mean(raw * raw, axis=1, keepdims=True) + 1e-05)
            hidden = (residual.astype(F32) + normed * gain).astype(BF16)
            here = slice(index * width, (index + 1) * width)
            mine_ref[place, here] = hidden[:capacity]
            theirs_ref[place, here] = hidden[capacity:]


def pair_rows(chunk, own, got, gain, kept, moved, weights):
    part, width, _ = kept.shape
    rows = own.shape[0]
    shape = jax.ShapeDtypeStruct((rows, part * width), BF16)
    flops = 4 * rows * part * width * width
    if chunk == CHUNKS - 1:
        flops = 1500 * sum(weight.size for weight in weights)
    return pl.pallas_call(
        functools.partial(rows_kernel, chunk),
        out_shape=(shape, shape),
        in_specs=[VMEM] * 5,
        out_specs=(VMEM, VMEM),
        compiler_params=grant(8),
        cost_estimate=pl.CostEstimate(
            flops=flops, bytes_accessed=12 * own.size, transcendentals=0
        ),
    )(own, got, gain, kept, moved)


def hidden_kernel(
    sent,
    run_ref,
    query_ref,
    within_ref,
    residual_ref,
    gain_ref,
    moe_gain_ref,
    router_ref,
    route_ref,
    before_ref,
    *refs,
):
    *state_refs, hidden_ref, sums_ref = refs
    heads, length = run_ref.shape
    span = hidden_ref.shape[1]
    half, part = (heads // 2, state_refs[0].shape[0])
    width = span // half
    side = (lax.axis_index("seq") + sent) % 2
    grown = as_columns(jnp.exp(jnp.where(side == 0, run_ref[:half, :], run_ref[half:, :])))
    squares = jnp.zeros((length, width), F32)
    for head in range(half):
        here = slice(head * width, (head + 1) * width)
        lanes = pl.ds(pl.multiple_of((side * half + head) * width, width), width)
        state = state_refs[head // part][head % part]
        carried = jnp.dot(query_ref[:, lanes], state, preferred_element_type=F32)
        raw = within_ref[:, here] + carried * grown[:, head : head + 1]
        normed = raw * lax.rsqrt(jnp.mean(raw * raw, axis=1, keepdims=True) + 1e-05)
        hidden = (residual_ref[:, lanes].astype(F32) + normed * gain_ref[:, lanes]).astype(BF16)
        hidden_ref[:, here] = hidden
        value = hidden.astype(F32)
        squares += value * value
    here = pl.ds(pl.multiple_of((lax.axis_index("exp") * 2 + side) * span, span), span)
    weights = router_ref[:, here].astype(F32) * moe_gain_ref[:, here]
    first = weights.astype(BF16)
    second = (weights - first.astype(F32)).astype(BF16)
    third = (weights - first.astype(F32) - second.astype(F32)).astype(BF16)
    products = lax.dot_general(
        hidden_ref[...],
        jnp.concatenate([first, second, third, jnp.zeros_like(first)], axis=0),
        (((1,), (1,)), ((), ())),
        preferred_element_type=F32,
    ).T
    count = weights.shape[0]
    logits = products[:count] + products[count : 2 * count] + products[2 * count : 3 * count]
    expert = lax.broadcasted_iota(jnp.int32, logits.shape, 0)
    for choice in range(2):
        here = slice(choice, choice + 1)
        chosen = jnp.where(route_ref[here, :] == expert, logits, 0.0)
        sums_ref[here, :] = before_ref[here, :] + jnp.sum(chosen, axis=0, keepdims=True)
    sums_ref[2:3, :] = before_ref[2:3, :] + jnp.sum(squares.T, axis=0, keepdims=True)
    sums_ref[3:, :] = jnp.zeros((sums_ref.shape[0] - 3, length), F32)


def hidden_block(
    sent, running, query_rows, within, residual, gain, moe_gain, router, routes, before, states
):
    heads, length = running.shape
    return pl.pallas_call(
        functools.partial(hidden_kernel, sent),
        out_shape=(
            jax.ShapeDtypeStruct(within.shape, BF16),
            jax.ShapeDtypeStruct(before.shape, F32),
        ),
        in_specs=[VMEM] * (9 + CHUNKS),
        out_specs=(VMEM, VMEM),
        compiler_params=grant(8),
        cost_estimate=pl.CostEstimate(
            flops=4 * within.size * within.shape[1] // heads,
            bytes_accessed=12 * within.size,
            transcendentals=0,
        ),
    )(running, query_rows, within, residual, gain, moe_gain, router, routes, before, *states)


def far_side(count):
    return ring_block(count, count // 2) % 2


def quarter_of(count, late, side):
    return (lax.axis_index("exp") ^ side) * 2 + (far_side(count) ^ 1 ^ late)


def place_pieces(places, gain_ref, pieces, scaled_ref, square_ref):
    quarter = scaled_ref.shape[1] // 4
    for (position, side), piece in zip(places, pieces, strict=True):
        height = piece.shape[0]
        count = 2 * scaled_ref.shape[0] // height
        block = ring_block(count, position)
        rows = pl.ds(pl.multiple_of(block // 2 * height, height), height)
        late = (block % 2) ^ far_side(count) ^ 1
        lanes = pl.ds(pl.multiple_of((late * 2 + side) * quarter, quarter), quarter)
        first = ((lax.axis_index("exp") ^ side) * 2 + block % 2) * quarter
        gain = gain_ref[:, pl.ds(pl.multiple_of(first, quarter), quarter)]
        value = piece[...].astype(F32)
        square = jnp.sum(value * value, axis=1, keepdims=True)
        square_ref[rows, :] += jnp.broadcast_to(square, (height, square_ref.shape[1]))
        scaled_ref[rows, lanes] = (value * gain).astype(BF16)


def products(late, scaled_ref, gate_ref, up_ref):
    quarter = scaled_ref.shape[1] // 4
    gate_part, up_part = (0.0, 0.0)
    for side in range(2):
        rows = scaled_ref[:, (late * 2 + side) * quarter : (late * 2 + side + 1) * quarter]
        first = quarter_of(scaled_ref.shape[0] // CAP, late, side) * quarter
        here = pl.ds(pl.multiple_of(first, quarter), quarter)
        gate_part += jnp.dot(rows, gate_ref[here, :], preferred_element_type=F32)
        up_part += jnp.dot(rows, up_ref[here, :], preferred_element_type=F32)
    return (gate_part, up_part)


def early_kernel(places, gain_ref, *refs):
    *pieces, scaled_ref, square_ref = refs
    square_ref[...] = jnp.zeros_like(square_ref)
    place_pieces(places, gain_ref, pieces, scaled_ref, square_ref)


def early_rows(places, rows, gain, pieces):
    return pl.pallas_call(
        functools.partial(early_kernel, places),
        out_shape=(
            jax.ShapeDtypeStruct((rows, gain.shape[1]), BF16),
            jax.ShapeDtypeStruct((rows, 128), F32),
        ),
        in_specs=[VMEM] * (1 + len(pieces)),
        out_specs=(VMEM, VMEM),
        compiler_params=grant(8),
    )(gain, *pieces)


def partial_kernel(places, gain_ref, gate_ref, up_ref, early_ref, early_square_ref, *refs):
    *pieces, scaled_ref, square_ref, gate_out_ref, up_out_ref = refs
    scaled_ref[...] = early_ref[...]
    square_ref[...] = early_square_ref[...]
    place_pieces(places, gain_ref, pieces, scaled_ref, square_ref)
    gate_out_ref[...], up_out_ref[...] = products(0, scaled_ref, gate_ref, up_ref)


def partial_rows(places, gain, early, pieces, gate_weight, up_weight):
    width, hidden_units = gate_weight.shape
    rows = early[0].shape[0]
    part = jax.ShapeDtypeStruct((rows, hidden_units), F32)
    return pl.pallas_call(
        functools.partial(partial_kernel, places),
        out_shape=(
            jax.ShapeDtypeStruct((rows, width), BF16),
            jax.ShapeDtypeStruct((rows, 128), F32),
            part,
            part,
        ),
        in_specs=[VMEM] * (5 + len(pieces)),
        out_specs=(VMEM,) * 4,
        compiler_params=grant(max(6, rows // 16)),
        cost_estimate=pl.CostEstimate(
            flops=2 * rows * width * hidden_units,
            bytes_accessed=2 * width * hidden_units,
            transcendentals=0,
        ),
    )(gain, gate_weight, up_weight, *early, *pieces)


def expert_kernel(
    places, gain_ref, gate_ref, up_ref, early_ref, early_square_ref, gate_in_ref, up_in_ref, *refs
):
    *pieces, hidden_ref, scaled_ref, square_ref, block_ref = refs
    width = gate_ref.shape[0]
    capacity = CAP
    count = scaled_ref.shape[0] // capacity
    scaled_ref[:, width // 2 :] = early_ref[:, width // 2 :]
    square_ref[...] = early_square_ref[...]
    place_pieces(places, gain_ref, pieces, scaled_ref, square_ref)
    inverse = lax.rsqrt(square_ref[...][:, :1] / width + 1e-06)
    gate_part, up_part = products(1, scaled_ref, gate_ref, up_ref)
    gate_part = (gate_in_ref[...] + gate_part) * inverse
    up_part = (up_in_ref[...] + up_part) * inverse
    block_ref[...] = (jax.nn.silu(gate_part) * up_part).astype(BF16)
    for position in range(count):
        block = ring_block(count, position)
        hidden_ref[position * capacity : (position + 1) * capacity] = block_ref[
            pl.ds(pl.multiple_of(block * capacity, capacity), capacity)
        ]


def expert_rows(places, gain, early, pieces, gate_weight, up_weight):
    width, hidden_units = gate_weight.shape
    rows = early[0].shape[0]
    return pl.pallas_call(
        functools.partial(expert_kernel, places),
        out_shape=jax.ShapeDtypeStruct((rows, hidden_units), BF16),
        in_specs=[VMEM] * (7 + len(pieces)),
        out_specs=VMEM,
        scratch_shapes=[
            pltpu.VMEM((rows, width), BF16),
            pltpu.VMEM((rows, 128), F32),
            pltpu.VMEM((rows, hidden_units), BF16),
        ],
        compiler_params=grant(max(6, rows // 16)),
        cost_estimate=pl.CostEstimate(
            flops=2 * rows * width * hidden_units,
            bytes_accessed=2 * width * hidden_units,
            transcendentals=0,
        ),
    )(gain, gate_weight, up_weight, *early, *pieces)


def down_kernel(half, hidden_ref, down_ref, out_ref):
    quarter = out_ref.shape[1] // 2
    for part in range(2):
        first = ((lax.axis_index("exp") ^ half) * 2 + part) * quarter
        weights = down_ref[:, pl.ds(pl.multiple_of(first, quarter), quarter)]
        out_ref[:, part * quarter : (part + 1) * quarter] = jnp.dot(
            hidden_ref[...], weights, preferred_element_type=F32
        )


def expert_down(half, hidden, down_weight):
    rows, width = (hidden.shape[0], down_weight.shape[1])
    return pl.pallas_call(
        functools.partial(down_kernel, half),
        out_shape=jax.ShapeDtypeStruct((rows, width // 2), F32),
        in_specs=[VMEM] * 2,
        out_specs=VMEM,
        compiler_params=grant(max(6, rows // 32)),
        cost_estimate=pl.CostEstimate(
            flops=rows * width * hidden.shape[1],
            bytes_accessed=width * hidden.shape[1],
            transcendentals=0,
        ),
    )(hidden, down_weight)


def share_kernel(span, sums_ref, got_sums_ref, route_ref, slot_ref, table_ref):
    capacity = table_ref.shape[1] // 4
    sums = sums_ref[...] + got_sums_ref[...]
    inverse = lax.rsqrt(sums[2:3] / (2 * span) + 1e-06)
    gates = jax.nn.sigmoid(sums[:2] * inverse)
    shares = gates / jnp.sum(gates, axis=0, keepdims=True)
    table = slots_of(route_ref, slot_ref, capacity, (shares[:1], shares[1:]))
    table = as_columns(table)[:, : 2 * capacity]
    high = table.astype(BF16)
    low = (table - high.astype(F32)).astype(BF16)
    table_ref[...] = jnp.concatenate([high, low], axis=1)


def share_table(span, sums, got_sums, routes, slots):
    return pl.pallas_call(
        functools.partial(share_kernel, span),
        out_shape=jax.ShapeDtypeStruct((routes.shape[1], 4 * CAP), BF16),
        in_specs=[VMEM] * 4,
        out_specs=VMEM,
        compiler_params=grant(4),
    )(sums, got_sums, routes, slots)


def mixed_kernel(table_ref, kept_ref, swapped_ref, *refs):
    *part_refs, out_ref, held_ref, sems = refs
    span = out_ref.shape[1]
    even = lax.axis_index("seq") % 2 == 0
    copies = []
    for part in range(4):
        lanes = slice(part * span // 4, (part + 1) * span // 4)
        parts = [ref[:, lanes].astype(F32) for ref in part_refs]
        own, other = [
            (first + second + third).astype(BF16)
            for first, second, third in (parts[:3], parts[3:])
        ]
        outs = jnp.concatenate([own, other] * 2, axis=0)
        mixed = jnp.dot(table_ref[...], outs, preferred_element_type=F32)
        here = slice(part % 2 * span // 4, (part % 2 + 1) * span // 4)
        halves = (kept_ref[:, here], swapped_ref[:, here])
        hidden = jnp.where(even, halves[part // 2], halves[1 - part // 2])
        held_ref[:, lanes] = (hidden.astype(F32) + mixed).astype(BF16)
        copies.append(
            pltpu.make_async_copy(held_ref.at[:, lanes], out_ref.at[:, lanes], sems.at[part])
        )
        copies[-1].start()
    for copy in copies:
        copy.wait()


def mixed_block(table, kept, swapped, parts):
    shape = (kept.shape[0], 2 * kept.shape[1])
    return pl.pallas_call(
        mixed_kernel,
        out_shape=jax.ShapeDtypeStruct(shape, BF16),
        in_specs=[VMEM] * (3 + len(parts)),
        out_specs=HBM,
        scratch_shapes=[pltpu.VMEM(shape, BF16), pltpu.SemaphoreType.DMA((4,))],
        compiler_params=grant(8),
        cost_estimate=pl.CostEstimate(
            flops=16 * kept.size * CAP,
            bytes_accessed=8 * kept.size,
            transcendentals=0,
        ),
    )(table, kept, swapped, *parts)


def after(value, *others):
    return lax.optimization_barrier((value, *others))[0]


def entering_state(odd, states, sending, block_total, aside, share, finish):
    count = lax.axis_size("seq")
    swap = [(i, i ^ 1) for i in range(count)]
    rows, width = states[0].shape
    part = rows // width
    half = part * CHUNKS
    total_own = jnp.where(odd, block_total[half:], block_total[:half])
    even_decays, pair_decays, even_states, pair_states, sents, marks = ([], [], [], [], [], [])
    for chunk in range(CHUNKS):
        arrived = after(lax.ppermute(sending[chunk], "seq", swap), *marks)
        if chunk == 0:
            total_other = jnp.sum(arrived[rows : rows + 3, :half].astype(F32), axis=0)
            even_decay = jnp.exp(jnp.where(odd, total_other, total_own))[:, None, None]
            odd_decay = jnp.exp(jnp.where(odd, total_own, total_other))[:, None, None]
        place = slice(chunk * part, (chunk + 1) * part)
        own = states[chunk].reshape(part, width, width)
        arrived = arrived[:rows].astype(F32).reshape(part, width, width)
        even_states.append(jnp.where(odd, arrived, own))
        odd_state = jnp.where(odd, own, arrived)
        even_decays.append(even_decay[place])
        pair_decays.append(even_decay[place] * odd_decay[place])
        pair_states.append(odd_decay[place] * even_states[-1] + odd_state)
        sents.append(pair_states[-1].astype(BF16))
        marks = [sents[-1]]
        if chunk == 0:
            shared = share(sents[-1])
            marks = [*marks, *shared]
    shared = (after(shared[0], sents[-1]), shared[1])
    swapped = lax.ppermute(shared[0], "seq", swap)
    marks = [sents[-1], shared[0]]
    links = count // 2 - 1
    turn = max(links - 2, 0)
    befores = [jnp.zeros_like(state) for state in pair_states]
    finished = []
    for link in range(links):
        pairs = [(2 * link + k, 2 * link + 2 + k) for k in range(2)]
        gots = [lax.ppermute(sent, "seq", pairs) for sent in sents]
        if link == turn:
            result = aside(sents[-1])
            marks = [*marks, *result]
        for chunk in range(CHUNKS):
            got = after(gots[chunk], *marks).astype(F32)
            before = befores[chunk] = befores[chunk] + got
            if link < links - 1:
                sents[chunk] = (pair_decays[chunk] * before + pair_states[chunk]).astype(BF16)
                marks = [sents[chunk]]
            else:
                between = even_decays[chunk] * before + even_states[chunk]
                kept = jnp.where(odd, between, before).astype(BF16)
                moved = jnp.where(odd, before, between).astype(BF16)
                marks = [kept, moved]
            if link == links - 1:
                finished.append(finish(chunk, kept, moved, result[0], swapped))
                marks = [*marks, *finished[-1][:2]]
    return (finished, result[1], shared[1])


def ring_pairs(count):
    order = list(range(0, count, 2)) + list(range(count - 1, 0, -2))
    right = [(order[i], order[(i + 1) % count]) for i in range(count)]
    return (right, [(b, a) for a, b in right])


def ring_block(count, position):
    block = lax.axis_index("seq")
    here = jnp.where(block % 2 == 0, block // 2, count - 1 - block // 2)
    offset = count - position if position <= count // 2 else position - count // 2
    there = (here + offset) % count
    return jnp.where(there < count // 2, 2 * there, 2 * (count - 1 - there) + 1)


def move(sent, way, across):
    if not across:
        return lax.ppermute(sent, "seq", way)
    pairs = [(2 * a + core, 2 * b + 1 - core) for a, b in way for core in range(2)]
    return lax.ppermute(sent, ("seq", "exp"), pairs)


def ring_gather(halves, second, holds):
    steps = lax.axis_size("seq") // 2
    right, left = ring_pairs(2 * steps)
    chains = [(0, right), (1, left), (1, right), (0, left)]
    moving = [halves[half] for half, _ in chains]
    brought = [[halves[0], second]]
    marks = list(halves)
    for step in range(steps):
        here = chains if step < steps - 1 else chains[:2]
        gots = [
            move(moving[k], way, half == 1 and step == 0) for k, (half, way) in enumerate(here)
        ]
        if step in holds:
            marks = [*marks, *holds[step](brought)]
        brought.append([])
        for k, got in enumerate(gots):
            moving[k] = after(got, *marks)
            marks = [moving[k]]
            brought[-1].append(moving[k])
    return brought


def ring_places(steps, step):
    if step == 0:
        return [(0, 0), (0, 1)]
    to_left, to_right = (step, steps + step)
    if step == steps:
        return [(to_left, 0), (to_left, 1)]
    return [(to_left, 0), (to_right, 1), (to_left, 1), (to_right, 0)]


def ring_scatter(own, rest, rows, holds):
    steps = lax.axis_size("seq") // 2
    right, left = ring_pairs(2 * steps)
    partials = [own, None]

    def piece(position, half):
        return partials[half][position * rows : (position + 1) * rows]

    chains = [
        (0, left, [steps, *range(steps - 1, 0, -1)]),
        (0, right, list(range(2 * steps - 1, steps, -1))),
        (1, right, [steps, *range(2 * steps - 1, steps, -1)]),
        (1, left, list(range(steps - 1, 0, -1))),
    ]
    sents = [piece(positions[0], 0).astype(BF16) for _, _, positions in chains[:2]]
    partials[1] = rest(sents)
    sents += [piece(positions[0], 1).astype(BF16) for _, _, positions in chains[2:]]
    here = piece(0, 1).astype(BF16)
    marks = list(sents)
    for step in range(1, steps + 1):
        gots = {}
        for k in (0, 2, 3, 1):
            half, way, positions = chains[k]
            if step <= len(positions):
                gots[k] = move(sents[k], way, half == 1 and step == len(positions))
        if step == 2:
            here = lax.ppermute(here, "exp", [(0, 1), (1, 0)])
            marks = [*marks, here]
        if step in holds:
            marks = [*marks, *holds[step]([sents[k] for k in gots])]
        for k, got in gots.items():
            half, _, positions = chains[k]
            got = after(got, *marks)
            if step < len(positions):
                got = (piece(positions[step], half) + got.astype(F32)).astype(BF16)
            sents[k] = got
            marks = [got]
    return (piece(0, 0), sents[0], sents[1], here, sents[2], sents[3])


def shards(
    queries,
    key_rows,
    values,
    log_decay,
    residual,
    attn_gain,
    moe_gain,
    router,
    routes,
    slot_pos,
    gate_weight,
    up_weight,
    down_weight,
):
    count = lax.axis_size("seq")
    exchange = [(0, 1), (1, 0)]
    swap = [(i, i ^ 1) for i in range(count)]
    log_rows, route_rows, slot_rows = (log_decay.T, routes.T, slot_pos.T)
    attn_gain, moe_gain = (attn_gain[None], moe_gain[None])
    odd = lax.axis_index("seq") % 2 == 1
    sending = half_state(True, after(log_rows, odd), key_rows, values)
    *states, running = half_state(False, after(log_rows, sending[0]), key_rows, values)

    def routed(sent, mark):
        within, pack = within_block(
            sent,
            running,
            after(queries, mark),
            key_rows,
            values,
            residual,
            route_rows,
            slot_rows,
        )
        return (pack, within)

    weights = (gate_weight, up_weight, down_weight)

    def finish(chunk, kept, moved, own, got):
        rows = pair_rows(chunk, own, got, attn_gain, kept, moved, weights)
        return (*rows, kept, lax.ppermute(moved, "seq", swap))

    finished, within_own, within_other = entering_state(
        odd,
        states,
        sending,
        running[:, -1],
        functools.partial(routed, False),
        functools.partial(routed, True),
        finish,
    )
    rows_mine, rows_sent, kept, swapped = zip(*finished, strict=True)
    rows_sent = jnp.concatenate(rows_sent, axis=1)
    rows_got = lax.ppermute(rows_sent, "exp", exchange)

    def all_rows(sent, mark, within, before, entering):
        return hidden_block(
            sent,
            running,
            queries,
            within,
            after(residual, *mark),
            attn_gain,
            moe_gain,
            router.T,
            route_rows,
            before,
            entering,
        )

    zeros = jnp.zeros((8, running.shape[1]), F32)
    hidden_own, sums = all_rows(False, [rows_sent], within_own, zeros, kept)
    halves = (jnp.concatenate(rows_mine, axis=1), rows_sent)
    second = after(rows_got, *swapped[:2], hidden_own, sums)

    steps = count // 2
    early = []

    def hold_rows(brought):
        places = sum([ring_places(steps, step) for step in range(steps - 1)], [])
        early.append(early_rows(places, count * CAP, moe_gain, sum(brought, [])))
        return early[-1]

    def hold_partial(brought):
        early.append(
            partial_rows(
                ring_places(steps, steps - 1),
                moe_gain,
                early[-1],
                brought[-1],
                gate_weight[0],
                up_weight[0],
            )
        )
        return early[-1]

    holds = {0: lambda brought: (second, *swapped), steps - 2: hold_rows, steps - 1: hold_partial}
    brought = ring_gather(halves, second, holds)
    hidden_units = expert_rows(
        ring_places(steps, steps),
        moe_gain,
        early[-1],
        brought[-1],
        gate_weight[0],
        up_weight[0],
    )
    own = expert_down(0, hidden_units, down_weight[0])

    def rest(marks):
        return expert_down(1, after(hidden_units, *marks), down_weight[0])

    held = []

    def hold_hidden(marks):
        held.extend(all_rows(True, marks, within_other, sums, swapped))
        got_sums = lax.ppermute(held[1], "exp", exchange)
        held.append(
            share_table(queries.shape[1], held[1], got_sums, route_rows, slot_rows)
        )
        return held

    parts = ring_scatter(own, rest, CAP, {steps: hold_hidden})
    hidden_other, _, table = held
    return mixed_block(table, hidden_own, hidden_other, parts)


def solution(mesh):
    placed = (
        P(("groups", "seq"), "exp"),
        P(("groups", "seq"), "exp"),
        P(("groups", "seq"), "exp"),
        P(("groups", "seq"), "exp"),
        P(("groups", "seq"), "exp"),
        P("exp"),
        P(),
        P(),
        P(("groups", "seq"), None),
        P(("groups", "seq"), None),
        P("exp", None, "seq"),
        P("exp", None, "seq"),
        P("exp", "seq", None),
    )
    return jax.shard_map(
        shards, mesh=mesh, in_specs=placed, out_specs=P(("groups", "seq"), "exp"), check_vma=False
    )
```
